128 devices in a mesh: ctx: 8 (over x_hi, y), exp: 16 (over z, x_lo, core).
Axes of the slice: x: 4 (x_hi: 2, x_lo: 2; x = x_hi * 2 + x_lo), y: 4, z: 4, core: 2. Of those that a mesh axis runs over, the one named last changes fastest.
Arguments:
- hidden_in: bfloat16 [16384, 2048], P(('ctx', 'exp')), may hold values from -6 to 6
- attn_gain: float32 [2048], replicated, may hold values from 0.1 to 1.9
- w_query: bfloat16 [2048, 2048], P(None, 'exp'), may hold values from -0.125 to 0.125
- w_key: bfloat16 [2048, 256], replicated, may hold values from -0.125 to 0.125
- w_value: bfloat16 [2048, 256], replicated, may hold values from -0.125 to 0.125
- q_gain: float32 [128], replicated, may hold values from 1.4 to 10
- k_gain: float32 [128], replicated, may hold values from 1.4 to 10
- w_out: bfloat16 [2048, 2048], P('exp'), may hold values from -0.125 to 0.125
- ffn_gain: float32 [2048], replicated, may hold values from 0.1 to 1.9
- w_gate: bfloat16 [128, 2048, 768], P(('ctx', 'exp')), may hold values from -0.125 to 0.125
- w_up: bfloat16 [128, 2048, 768], P(('ctx', 'exp')), may hold values from -0.125 to 0.125
- w_down: bfloat16 [128, 768, 2048], P(('ctx', 'exp')), may hold values from -0.21875 to 0.21875
- expert_ids: int32 [16384, 8], P(('ctx', 'exp')), may hold values from 0 to 127, all different within a row; in each aligned block of 128 rows (0 to 127, 128 to 255, ...) at most 10 rows name the same one
- gate_weights: float32 [16384, 8], P(('ctx', 'exp')), may hold values from 0.05 to 1
Outputs:
- layer_out: bfloat16 [16384, 2048], P(('ctx', 'exp'))
The draws below stay inside these ranges and needn't reach their ends.
Inputs may be any that keep to these rules, and one draw needn't show every extreme that they name: `expert_ids`: each row names 8 different experts. Among the rows of one device no expert is named more than 10 times, and in every draw some expert is named exactly 10 times by the rows of some device.
All inputs are finite; a program needn't handle non-finite values.
Results may differ from the reference program's by a relative error of at most 0.023.
The reference program's roundings to bfloat16 on the way count: a program that leaves them out, or rounds other values in their place, can miss the bound.
Values may be sent and summed in bfloat16 or wider, within the bound.
A program may use at most 128 MiB of HBM per device.

```python
import math
import jax
import jax.numpy as jnp
import numpy as np
from jax import lax

D = 2048
HD = 128
FF = 768
TOPK = 8
HEADS = 16
KVH = 2
TOK_DEV = 128
EXPERTS = 128
SEQ = 16384
CAP = 10
N_CTX = 8
N_EXP = 16


def draw_q_gain(key, part):
    key = jax.random.fold_in(key, 11)
    return jax.random.uniform(key, (HD,), jnp.float32, 1.4, 2.6)


def draw_k_gain(key, part):
    key = jax.random.fold_in(key, 23)
    return jax.random.uniform(key, (HD,), jnp.float32, 1.4, 2.6)


def steps_of(stream_key, extent, cuts, least, largest):
    loudness = 1.0
    for position, blocks in cuts:
        steps = jax.random.uniform(jax.random.fold_in(jax.random.fold_in(stream_key, 6), position), (blocks,), jnp.float32, least / len(cuts), largest / len(cuts))
        loudness = loudness * jnp.repeat(jnp.exp(steps), extent[position] // blocks).reshape((-1,) + (1,) * (len(extent) - 1 - position))
    return loudness


def assign_block(stream_key, own, number, rows, count, top, most, lean):
    sequence = jax.random.permutation(stream_key, count)
    packed, common = portions_of(count, rows * top, most, lean, True), portions_of(count, rows * top, most, lean, False)
    places = jnp.arange(count)

    def named(sizes, turn):
        used = int((sizes > 0).sum())
        fixed = max(1, used // 4)
        moved = fixed + (places - fixed + turn * (used - fixed)) % max(1, count - fixed)
        return jnp.zeros((count,), jnp.int32).at[sequence[jnp.where(places < fixed, places, moved)]].set(jnp.asarray(sizes, jnp.int32))

    sizes = jnp.where(number % 4 == 0, named(packed, number // 4), named(common, number - number // 4 - 1))
    mixed = jax.random.permutation(jax.random.fold_in(own, 3), count)
    giver, taker = mixed[0:count // 2 * 2:2], mixed[1:count // 2 * 2:2]
    margin = jnp.minimum(sizes[giver] - 1, most - sizes[taker]) // 2
    margin = jnp.where((giver == sequence[0]) | (taker == sequence[0]) | (sizes[taker] == 0), 0, jnp.maximum(margin, 0))
    moved = jax.random.randint(jax.random.fold_in(own, 4), (count // 2,), 0, 1 << 20) % (margin + 1)
    sizes = sizes.at[giver].add(-moved).at[taker].add(moved)
    items = jnp.searchsorted(jnp.cumsum(sizes), jnp.arange(rows * top), side="right").astype(jnp.int32)
    table = items.reshape(top, rows).T
    table = table[jax.random.permutation(jax.random.fold_in(own, 1), rows)]
    turn = jax.random.randint(jax.random.fold_in(own, 2), (rows, 1), 0, top)
    return jnp.take_along_axis(table, (jnp.arange(top)[None, :] + turn) % top, axis=1)


def portions_of(amount, total, most, lean, full):
    loads = [(1 << 20) // math.isqrt(rank ** lean) + 1 for rank in range(1, amount + 1)]
    largest = most if full else min(most, max(-(-total // amount), total * loads[0] // sum(loads)))
    least = 1 if total - largest >= amount - 1 else 0
    counts, spare = [largest] + [least] * (amount - 1), total - largest - least * (amount - 1)
    while spare > 0:
        free = [i for i in range(1, amount) if counts[i] < largest] or [i for i in range(1, amount) if counts[i] < most]
        whole, budget = sum([loads[i] for i in free]), spare
        for i in free:
            more = min(most - counts[i], max(1, budget * loads[i] // whole), spare)
            counts[i] = counts[i] + more
            spare = spare - more
    return np.array(counts)


def centred(key, extent, deviation, bound, cuts=(), held_as=jnp.bfloat16):
    gain = steps_of(key, extent, cuts, -0.22, 0.18) if cuts else 1.0
    array = jax.random.normal(key, extent, jnp.float32) * deviation * gain
    return jnp.minimum(jnp.maximum(array, -bound), bound).astype(held_as)


def setup_inputs(seed: int = 0) -> dict:
    splits = jax.random.split(jax.random.key(seed), 15)
    hidden_in = centred(splits[0], (SEQ, D), 1.0, 6.0, ((0, 128),))
    attn_gain = jnp.clip(1.0 + 0.18 * jax.random.normal(splits[1], (D,), jnp.float32), 0.1, 1.9)
    w_query = centred(splits[2], (D, HEADS * HD), D ** -0.5, 0.125, ((1, 16),))
    w_key = centred(splits[3], (D, KVH * HD), D ** -0.5, 0.125)
    w_value = centred(splits[4], (D, KVH * HD), D ** -0.5, 0.125)
    q_gain = draw_q_gain(jax.random.fold_in(splits[14], 71), 0)
    k_gain = draw_k_gain(jax.random.fold_in(splits[14], 71), 0)
    w_out = centred(splits[7], (HEADS * HD, D), (HEADS * HD) ** -0.5, 0.125, ((0, 16),))
    ffn_gain = jnp.clip(1.0 + 0.18 * jax.random.normal(splits[8], (D,), jnp.float32), 0.1, 1.9)
    w_gate = centred(splits[9], (EXPERTS, D, FF), D ** -0.5, 0.125, ((0, 128),))
    w_up = centred(splits[10], (EXPERTS, D, FF), D ** -0.5, 0.125, ((0, 128),))
    w_down = centred(splits[11], (EXPERTS, FF, D), FF ** -0.5, 0.21875, ((0, 128),))
    expert_ids_keys = jax.random.split(jax.random.fold_in(splits[12], 1), SEQ // TOK_DEV)
    expert_ids_turns = jax.random.permutation(jax.random.fold_in(splits[12], 3), SEQ // TOK_DEV)
    expert_ids = jax.vmap(lambda own, number: assign_block(jax.random.fold_in(splits[12], 2), own, number, TOK_DEV, EXPERTS, TOPK, CAP, 2))(expert_ids_keys, expert_ids_turns).reshape((SEQ, TOPK))
    gate_weights = jnp.clip(jnp.exp(math.log(1.0) - 2.9957323 * jax.random.uniform(splits[13], (SEQ, TOPK), jnp.float32) ** steps_of(splits[13], (SEQ, TOPK), ((0, 128),), -0.2, 0.2)), 0.05, 1.0)
    return dict(hidden_in=hidden_in, attn_gain=attn_gain, w_query=w_query, w_key=w_key, w_value=w_value, q_gain=q_gain, k_gain=k_gain, w_out=w_out, ffn_gain=ffn_gain, w_gate=w_gate, w_up=w_up, w_down=w_down, expert_ids=expert_ids, gate_weights=gate_weights)


epsilon = 1e-06
rope_base = 1000000.0

def rms_scale(values, gains):
    return values * lax.rsqrt(lax.optimization_barrier(jnp.mean(values * values, axis=-1, keepdims=True)) + epsilon) * gains

def rotate(values, places):
    half_dim = values.shape[-1] // 2
    frequency = jnp.exp(jnp.arange(half_dim, dtype=jnp.float32) * (-2.0 * math.log(rope_base) / values.shape[-1]))
    angles = places.astype(jnp.float32)[:, None] * frequency[None, :]
    cosine = jnp.cos(angles)[:, None, :]
    sine_part = jnp.sin(angles)[:, None, :]
    first_part = values[..., :half_dim]
    second_part = values[..., half_dim:]
    return jnp.concatenate([first_part * cosine - second_part * sine_part, second_part * cosine + first_part * sine_part], axis=-1)

def reference(hidden_in, attn_gain, w_query, w_key, w_value, q_gain, k_gain, w_out, ffn_gain, w_gate, w_up, w_down, expert_ids, gate_weights):
    seq_len = hidden_in.shape[0]
    model_width = hidden_in.shape[1]
    group_size = HEADS // KVH
    places = jnp.arange(seq_len, dtype=jnp.int32)
    normed = rms_scale(hidden_in.astype(jnp.float32), attn_gain).astype(jnp.bfloat16)
    query_raw = jnp.dot(normed, w_query, preferred_element_type=jnp.float32)
    key_raw = jnp.dot(normed, w_key, preferred_element_type=jnp.float32)
    value_raw = jnp.dot(normed, w_value, preferred_element_type=jnp.float32)
    queries = rotate(rms_scale(query_raw.reshape(seq_len, HEADS, HD), q_gain), places).astype(jnp.bfloat16)
    key_rows = rotate(rms_scale(key_raw.reshape(seq_len, KVH, HD), k_gain), places).astype(jnp.bfloat16)
    value_rows = value_raw.reshape(seq_len, KVH, HD).astype(jnp.bfloat16)
    block_size = math.gcd(seq_len, 1024)
    score_scale = 1.0 / math.sqrt(HD)
    results = []
    for first_row in range(0, seq_len, block_size):
        reach = first_row + block_size
        query_block = queries[first_row:reach]
        key_seen = key_rows[:reach]
        value_seen = value_rows[:reach]
        visible = places[None, :reach] <= places[first_row:reach, None]

        def one_head(head_idx, query_block=query_block, key_seen=key_seen, value_seen=value_seen, visible=visible):
            query_one = lax.dynamic_index_in_dim(query_block, head_idx, 1, False)
            key_one = lax.dynamic_index_in_dim(key_seen, head_idx // group_size, 1, False)
            value_one = lax.dynamic_index_in_dim(value_seen, head_idx // group_size, 1, False)
            scores = jnp.dot(query_one, key_one.T, preferred_element_type=jnp.float32) * score_scale
            row_top = lax.optimization_barrier(jnp.max(jnp.where(visible, scores, -jnp.inf), axis=1, keepdims=True))
            exp_weights = jnp.where(visible, jnp.exp(scores - row_top), 0.0)
            totals = lax.optimization_barrier(jnp.sum(exp_weights, axis=1, keepdims=True))
            summed = jnp.dot(exp_weights.astype(jnp.bfloat16), value_one, preferred_element_type=jnp.float32)
            return (summed / totals).astype(jnp.bfloat16)
        results.append(lax.map(one_head, jnp.arange(HEADS, dtype=jnp.int32)))
    attended = jnp.concatenate(results, axis=1)
    attended = jnp.transpose(attended, (1, 0, 2)).reshape(seq_len, HEADS * HD)
    projected = jnp.dot(attended, w_out, preferred_element_type=jnp.float32)
    resid = (hidden_in.astype(jnp.float32) + projected).astype(jnp.bfloat16)
    normed_ffn = rms_scale(resid.astype(jnp.float32), ffn_gain).astype(jnp.bfloat16)
    shares = gate_weights / lax.optimization_barrier(jnp.sum(gate_weights, axis=1, keepdims=True))
    flat_ids = expert_ids.reshape(-1)
    count_rows = flat_ids.shape[0]
    token_pad = jnp.concatenate([jnp.arange(count_rows, dtype=jnp.int32) // TOPK, jnp.full((1,), seq_len, jnp.int32)])
    share_pad = jnp.concatenate([shares.reshape(-1), jnp.zeros((1,), jnp.float32)])
    normed_pad = jnp.concatenate([normed_ffn, jnp.zeros((1, model_width), jnp.bfloat16)], axis=0)
    most_rows = N_CTX * N_EXP * CAP

    def one_expert(running, expert):
        picked = jnp.nonzero(flat_ids == expert, size=most_rows, fill_value=count_rows)[0].astype(jnp.int32)
        tokens_of = token_pad[picked]
        rows_in = normed_pad[tokens_of]
        gate_out = jnp.dot(rows_in, w_gate[expert], preferred_element_type=jnp.float32)
        up_out = jnp.dot(rows_in, w_up[expert], preferred_element_type=jnp.float32)
        inner_act = (jax.nn.silu(gate_out) * up_out).astype(jnp.bfloat16)
        answer = jnp.dot(inner_act, w_down[expert], preferred_element_type=jnp.float32).astype(jnp.bfloat16)
        weighted = share_pad[picked][:, None] * answer.astype(jnp.float32)
        return (running.at[tokens_of].add(weighted, mode='drop'), None)
    mixture, unused = lax.scan(one_expert, jnp.zeros((seq_len, model_width), jnp.float32), jnp.arange(EXPERTS, dtype=jnp.int32))
    return (resid.astype(jnp.float32) + mixture).astype(jnp.bfloat16)
```

```python
import functools
import math

import jax
import jax.numpy as jnp
from jax import lax
from jax.experimental import pallas as pl
from jax.experimental.pallas import tpu as pltpu
from jax.sharding import PartitionSpec as P

MESH = pl.DeviceIdType.MESH
TOPK = 8
HEADS = 16
KVH = 2
CAP = 10
GROUPS = 4
PEERS = 32


def my_coords():
    ctx = lax.axis_index("ctx")
    exp = lax.axis_index("exp")
    x = (ctx // 4) * 2 + (exp // 2) % 2
    return x, ctx % 4, exp // 4, exp % 2


def device_at(x, y, z, core):
    return ((x // 2) * 4 + y, z * 4 + (x % 2) * 2 + core)


def offset_parts(o):
    g, j = o // PEERS, o % PEERS
    dc, dx, dy = j % 2, (j // 2) % 4, (j // 8) % 4
    dz = (g + 8 - dx - dy) % 4
    return dx, dy, dz, dc


def peer_to(o):
    x, y, z, c = my_coords()
    dx, dy, dz, dc = offset_parts(o)
    return device_at((x + dx) % 4, (y + dy) % 4, (z + dz) % 4, (c + dc) % 2)


def peer_from(o):
    x, y, z, c = my_coords()
    dx, dy, dz, dc = offset_parts(o)
    return device_at((x + 4 - dx) % 4, (y + 4 - dy) % 4, (z + 4 - dz) % 4, (c + 2 - dc) % 2)


def offset_of_expert(e):
    x, y, z, c = my_coords()
    ce, ee = e // 16, e % 16
    dx = ((ce // 4) * 2 + (ee // 2) % 2 + 4 - x) % 4
    dy = (ce % 4 + 4 - y) % 4
    dz = (ee // 4 + 4 - z) % 4
    dc = (ee % 2 + 2 - c) % 2
    return ((dx + dy + dz) % 4) * PEERS + dc + 2 * dx + 8 * dy


def moe_kernel(
    cap,
    slot_tok, slot_at, shares,
    x_tiles, resid, w_gate, w_up, w_down,
    out_ref,
    send_buf, in_buf, ans_buf, ret_buf, vg, vu, vd, stage, xrows,
    wsem, dsend, drecv, asend, arecv,
):
    copies = [
        pltpu.make_async_copy(w_gate, vg, wsem.at[0]),
        pltpu.make_async_copy(w_up, vu, wsem.at[1]),
        pltpu.make_async_copy(w_down, vd, wsem.at[2]),
    ]
    for copy in copies:
        copy.start()
    barrier = pltpu.get_barrier_semaphore()

    def greet(o, carry):
        pl.semaphore_signal(barrier, inc=1, device_id=peer_to(o), device_id_type=MESH)
        return carry

    lax.fori_loop(1, GROUPS * PEERS, greet, 0)
    for r in range(cap):
        in_buf[0, r] = x_tiles[slot_tok[r]]

    def fill(o, carry):
        for r in range(cap):
            send_buf[o, r] = x_tiles[slot_tok[o * cap + r]]
        return carry

    lax.fori_loop(1, PEERS, fill, 0)
    pl.semaphore_wait(barrier, GROUPS * PEERS - 1)

    def dispatch(o, sem):
        return pltpu.make_async_remote_copy(
            src_ref=send_buf.at[o], dst_ref=in_buf.at[o],
            send_sem=dsend.at[sem], recv_sem=drecv.at[sem],
            device_id=peer_to(o), device_id_type=MESH,
        )

    def give_back(o, sem):
        return pltpu.make_async_remote_copy(
            src_ref=ans_buf.at[o], dst_ref=ret_buf.at[o],
            send_sem=asend.at[sem], recv_sem=arecv.at[sem],
            device_id=peer_from(o), device_id_type=MESH,
        )

    def send_first(o, carry):
        dispatch(o, 0).start()
        return carry

    lax.fori_loop(1, PEERS, send_first, 0)

    def send_rest(o, carry):
        fill(o, 0)
        dispatch(o, o // PEERS).start()
        return carry

    lax.fori_loop(PEERS, GROUPS * PEERS, send_rest, 0)
    for copy in copies:
        copy.wait()
    rows = PEERS * cap

    def compute(g):
        block = in_buf[pl.ds(g * PEERS, PEERS)]
        stage[...] = block.astype(jnp.float32).reshape(rows * 16, 128)
        for s in range(16):
            xrows[:, s * 128 : (s + 1) * 128] = stage[pl.ds(s, rows, stride=16), :].astype(jnp.bfloat16)
        rows_in = xrows[...]
        gate = jnp.dot(rows_in, vg[...], preferred_element_type=jnp.float32)
        up = jnp.dot(rows_in, vu[...], preferred_element_type=jnp.float32)
        inner = (gate / (1.0 + jnp.exp(-gate)) * up).astype(jnp.bfloat16)
        for q in range(4):
            part = jnp.dot(inner, vd[:, q * 512 : (q + 1) * 512], preferred_element_type=jnp.float32)
            for s in range(4):
                stage[pl.ds(q * 4 + s, rows, stride=16), :] = part[:, s * 128 : (s + 1) * 128]
        return stage[...].astype(jnp.bfloat16).reshape(PEERS, cap, 16, 128)

    def wait_bytes(buf, start, count, sem):
        pltpu.make_async_copy(buf.at[pl.ds(start, count)], buf.at[pl.ds(start, count)], sem).wait()

    def start_back(o, sem):
        give_back(o, sem).start()
        return sem

    for g in range(GROUPS):
        first = 1 if g == 0 else 0
        wait_bytes(in_buf, g * PEERS + first, PEERS - first, drecv.at[g])
        answers = compute(g)
        if g == 0:
            ret_buf[0] = answers[0]
        ans_buf[pl.ds(g * PEERS, PEERS)] = answers
        lax.fori_loop(g * PEERS + first, (g + 1) * PEERS, lambda o, c, g=g: start_back(o, g), g)
    for g in range(GROUPS):
        first = 1 if g == 0 else 0
        wait_bytes(ret_buf, g * PEERS + first, PEERS - first, arecv.at[g])

    def combine(t, carry):
        total = jnp.zeros((16, 128), jnp.float32)
        for k in range(TOPK):
            at = slot_at[t * TOPK + k]
            total += shares[t * TOPK + k] * ret_buf[at // cap, at % cap].astype(jnp.float32)
        out_ref[t] = (resid[t].astype(jnp.float32) + total).astype(jnp.bfloat16)
        return carry

    lax.fori_loop(0, out_ref.shape[0], combine, 0)
    for g in range(GROUPS):
        first = 1 if g == 0 else 0
        wait_bytes(send_buf, g * PEERS + first, PEERS - first, dsend.at[g])
        wait_bytes(ans_buf, g * PEERS + first, PEERS - first, asend.at[g])


def slots_of(expert_ids, tok_rows, cap):
    flat = expert_ids.reshape(-1)
    count = flat.shape[0]
    ids = jnp.arange(128, dtype=jnp.int32)
    matches = flat[:, None] == ids[None, :]
    row = jnp.arange(count, dtype=jnp.int32)
    earlier = (row[:, None] > row[None, :]).astype(jnp.bfloat16)
    before = jnp.dot(earlier, matches.astype(jnp.bfloat16), preferred_element_type=jnp.float32)
    rank = jnp.sum(jnp.where(matches, before, 0.0), axis=1).astype(jnp.int32)
    slot_at = offset_of_expert(flat) * cap + rank
    slot_tok = jnp.full((128 * cap,), tok_rows, jnp.int32).at[slot_at].set(row // TOPK)
    return slot_tok, slot_at


def moe(normed_ffn, resid, slot_tok, slot_at, shares, w_gate, w_up, w_down, cap=10):
    tok, width = normed_ffn.shape
    ff = w_gate.shape[1]
    x_tiles = jnp.concatenate([normed_ffn, jnp.zeros((8, width), jnp.bfloat16)], axis=0).reshape(tok + 8, 16, 128)
    n = GROUPS * PEERS
    out = pl.pallas_call(
        functools.partial(moe_kernel, cap),
        out_shape=jax.ShapeDtypeStruct((tok, 16, 128), jnp.bfloat16),
        in_specs=[pl.BlockSpec(memory_space=pltpu.SMEM)] * 3
        + [pl.BlockSpec(memory_space=pltpu.VMEM)] * 2
        + [pl.BlockSpec(memory_space=pl.ANY)] * 3,
        out_specs=pl.BlockSpec(memory_space=pltpu.VMEM),
        scratch_shapes=[pltpu.VMEM((n, cap, 16, 128), jnp.bfloat16)] * 4
        + [
            pltpu.VMEM((width, ff), jnp.bfloat16),
            pltpu.VMEM((width, ff), jnp.bfloat16),
            pltpu.VMEM((ff, width), jnp.bfloat16),
            pltpu.VMEM((PEERS * cap * 16, 128), jnp.float32),
            pltpu.VMEM((PEERS * cap, width), jnp.bfloat16),
            pltpu.SemaphoreType.DMA((3,)),
        ]
        + [pltpu.SemaphoreType.DMA((GROUPS,))] * 4,
        compiler_params=pltpu.CompilerParams(
            collective_id=3, has_side_effects=True, vmem_limit_bytes=60 * 1024 * 1024
        ),
        name="moe",
    )(slot_tok, slot_at, shares.reshape(-1), x_tiles, resid.reshape(tok, 16, 128), w_gate, w_up, w_down)
    return out.reshape(tok, width)


epsilon = 1e-06
rope_base = 1000000.0


def rms_scale(values, gains):
    return values * lax.rsqrt(jnp.mean(values * values, axis=-1, keepdims=True) + epsilon) * gains


def rotate(values, places):
    half_dim = values.shape[-1] // 2
    frequency = jnp.exp(
        jnp.arange(half_dim, dtype=jnp.float32) * (-2.0 * math.log(rope_base) / values.shape[-1])
    )
    angles = places.astype(jnp.float32)[:, None] * frequency[None, :]
    cosine = jnp.cos(angles)[:, None, :]
    sine_part = jnp.sin(angles)[:, None, :]
    first_part = values[..., :half_dim]
    second_part = values[..., half_dim:]
    return jnp.concatenate(
        [
            first_part * cosine - second_part * sine_part,
            second_part * cosine + first_part * sine_part,
        ],
        axis=-1,
    )


def token_place(row_ids, ctx_of, half_rows):
    half_idx = row_ids // half_rows
    offset = row_ids % half_rows
    segment = 2 * ctx_of + half_idx
    return segment * half_rows + offset


def on_device(
    hidden_in,
    attn_gain,
    w_query,
    w_key,
    w_value,
    q_gain,
    k_gain,
    w_out,
    ffn_gain,
    w_gate,
    w_up,
    w_down,
    expert_ids,
    gate_weights,
):
    head_dim = q_gain.shape[0]
    tok_rows = hidden_in.shape[0]
    model_width = hidden_in.shape[1]
    ctx_count = lax.axis_size("ctx")
    exp_count = lax.axis_size("exp")
    ctx_index = lax.axis_index("ctx")
    exp_index = lax.axis_index("exp")
    block_rows = tok_rows * exp_count
    half_rows = block_rows // 2
    heads_here = w_query.shape[1] // head_dim
    normed = rms_scale(hidden_in.astype(jnp.float32), attn_gain).astype(jnp.bfloat16)
    kv_column = exp_index * heads_here // (HEADS // KVH) * head_dim
    key_cols = lax.dynamic_slice_in_dim(w_key, kv_column, head_dim, 1)
    value_cols = lax.dynamic_slice_in_dim(w_value, kv_column, head_dim, 1)
    w_joined = jnp.concatenate([w_query, key_cols, value_cols], axis=1)
    query_width = heads_here * head_dim
    row_piece = lax.all_gather(normed, "exp", axis=0, tiled=True)
    projected = jnp.dot(row_piece, w_joined, preferred_element_type=jnp.float32)
    row_ids = jnp.arange(row_piece.shape[0], dtype=jnp.int32)
    places = token_place(row_ids, ctx_index, half_rows)
    queries = rotate(
        rms_scale(projected[:, :query_width].reshape(-1, heads_here, head_dim), q_gain), places
    )
    key_part = rotate(
        rms_scale(projected[:, query_width : query_width + head_dim][:, None, :], k_gain), places
    )[:, 0]
    value_part = projected[:, query_width + head_dim :]
    joined = jnp.concatenate(
        [queries.reshape(-1, query_width), key_part, value_part], axis=1
    ).astype(jnp.bfloat16)
    queries = joined[:, :query_width].reshape(block_rows, heads_here, head_dim)
    key_rows = joined[:, query_width : query_width + head_dim]
    value_rows = joined[:, query_width + head_dim :]
    query_places = token_place(jnp.arange(block_rows, dtype=jnp.int32), ctx_index, half_rows)
    query_halves = (queries[:half_rows], queries[half_rows:])
    place_halves = (query_places[:half_rows], query_places[half_rows:])
    score_scale = 1.0 / math.sqrt(head_dim)
    start_state = (
        jnp.full((heads_here, half_rows), -1e30, jnp.float32),
        jnp.zeros((heads_here, half_rows), jnp.float32),
        jnp.zeros((half_rows, heads_here, head_dim), jnp.float32),
    )
    key_block = lax.all_gather(key_rows, "ctx", axis=0, tiled=True)
    value_block = lax.all_gather(value_rows, "ctx", axis=0, tiled=True)
    piece_len = key_block.shape[0]
    tile_len = math.gcd(piece_len, 1024)

    def visit_tile(tile_idx, state):
        key_tile = lax.dynamic_slice_in_dim(key_block, tile_idx * tile_len, tile_len, 0)
        value_tile = lax.dynamic_slice_in_dim(value_block, tile_idx * tile_len, tile_len, 0)
        key_ids = tile_idx * tile_len + jnp.arange(tile_len, dtype=jnp.int32)
        key_places = token_place(key_ids % block_rows, key_ids // block_rows, half_rows)
        renewed = []
        for query_half, place_half, running in zip(query_halves, place_halves, state):

            def update(current, query_half=query_half, place_half=place_half):
                run_max, run_sum, run_out = current
                scores = (
                    jnp.einsum(
                        "qhd,kd->hqk", query_half, key_tile, preferred_element_type=jnp.float32
                    )
                    * score_scale
                )
                visible = key_places[None, None, :] <= place_half[None, :, None]
                row_top = jnp.max(jnp.where(visible, scores, -jnp.inf), axis=2)
                new_max = jnp.maximum(run_max, row_top)
                exp_weights = jnp.where(visible, jnp.exp(scores - new_max[:, :, None]), 0.0)
                rescale = jnp.exp(run_max - new_max)
                new_sum = run_sum * rescale + jnp.sum(exp_weights, axis=2)
                new_out = run_out * rescale.T[:, :, None] + jnp.einsum(
                    "hqk,kd->qhd",
                    exp_weights.astype(jnp.bfloat16),
                    value_tile,
                    preferred_element_type=jnp.float32,
                )
                return (new_max, new_sum, new_out)

            def keep_state(current):
                return current

            renewed.append(
                lax.cond(jnp.min(key_places) <= jnp.max(place_half), update, keep_state, running)
            )
        return tuple(renewed)

    final_state = lax.fori_loop(0, piece_len // tile_len, visit_tile, (start_state, start_state))
    halves_out = []
    for run_max, run_sum, run_out in final_state:
        halves_out.append(
            (run_out / run_sum.T[:, :, None]).astype(jnp.bfloat16).reshape(half_rows, query_width)
        )
    attended = jnp.concatenate(halves_out, axis=0)
    projected_out = lax.psum_scatter(
        jnp.dot(attended, w_out, preferred_element_type=jnp.float32).astype(jnp.bfloat16),
        "exp",
        scatter_dimension=0,
        tiled=True,
    ).astype(jnp.float32)
    resid = (hidden_in.astype(jnp.float32) + projected_out).astype(jnp.bfloat16)
    normed_ffn = rms_scale(resid.astype(jnp.float32), ffn_gain).astype(jnp.bfloat16)
    shares = gate_weights / jnp.sum(gate_weights, axis=1, keepdims=True)
    slot_tok, slot_at = slots_of(expert_ids, tok_rows, CAP)
    return moe(normed_ffn, resid, slot_tok, slot_at, shares, w_gate[0], w_up[0], w_down[0], CAP)


def solution(mesh):
    placed = (
        P(("ctx", "exp"), None),
        P(),
        P(None, "exp"),
        P(),
        P(),
        P(),
        P(),
        P("exp", None),
        P(),
        P(("ctx", "exp"), None, None),
        P(("ctx", "exp"), None, None),
        P(("ctx", "exp"), None, None),
        P(("ctx", "exp"), None),
        P(("ctx", "exp"), None),
    )
    return jax.shard_map(
        on_device, mesh=mesh, in_specs=placed, out_specs=P(("ctx", "exp"), None), check_vma=False
    )
```

```python
import functools
import math

import jax
import jax.numpy as jnp
from jax import lax
from jax.experimental import pallas as pl
from jax.experimental.pallas import tpu as pltpu
from jax.sharding import PartitionSpec as P

MESH = pl.DeviceIdType.MESH
TOPK = 8
CAP = 10
HEADS = 16
GROUPS = 4
PEERS = 32


def my_coords():
    ctx = lax.axis_index("ctx")
    exp = lax.axis_index("exp")
    x = (ctx // 4) * 2 + (exp // 2) % 2
    return x, ctx % 4, exp // 4, exp % 2


def device_at(x, y, z, core):
    return ((x // 2) * 4 + y, z * 4 + (x % 2) * 2 + core)


def offset_parts(o):
    g, j = o // PEERS, o % PEERS
    dc, dx, dy = j % 2, (j // 2) % 4, (j // 8) % 4
    dz = (g + 8 - dx - dy) % 4
    return dx, dy, dz, dc


def peer_to(o):
    x, y, z, c = my_coords()
    dx, dy, dz, dc = offset_parts(o)
    return device_at((x + dx) % 4, (y + dy) % 4, (z + dz) % 4, (c + dc) % 2)


def peer_from(o):
    x, y, z, c = my_coords()
    dx, dy, dz, dc = offset_parts(o)
    return device_at((x + 4 - dx) % 4, (y + 4 - dy) % 4, (z + 4 - dz) % 4, (c + 2 - dc) % 2)


def offset_of_expert(e):
    x, y, z, c = my_coords()
    ce, ee = e // 16, e % 16
    dx = ((ce // 4) * 2 + (ee // 2) % 2 + 4 - x) % 4
    dy = (ce % 4 + 4 - y) % 4
    dz = (ee // 4 + 4 - z) % 4
    dc = (ee % 2 + 2 - c) % 2
    return ((dx + dy + dz) % 4) * PEERS + dc + 2 * dx + 8 * dy


epsilon = 1e-06
rope_base = 1000000.0


def rms_scale(values, gains):
    return values * lax.rsqrt(jnp.mean(values * values, axis=-1, keepdims=True) + epsilon) * gains


def rope(values, cosine, sine):
    return values * cosine + pltpu.roll(values, 64, 1) * sine


def push(src, dst, ssem, rsem, device):
    pltpu.make_async_remote_copy(
        src_ref=src, dst_ref=dst, send_sem=ssem, recv_sem=rsem,
        device_id=device, device_id_type=MESH,
    ).start()


def wait_for(ref, sem):
    pltpu.make_async_copy(ref, ref, sem).wait()


class Ring:
    def __init__(self, blocks, halves, plus, minus, ssem, rsem, source=None):
        self.own, self.left, self.right = blocks
        self.left_half, self.right_half, self.far_first, self.far_second = halves
        self.plus, self.minus, self.ssem, self.rsem = plus, minus, ssem, rsem
        self.source = self.own if source is None else source

    def start(self):
        push(self.source, self.own, self.ssem.at[0], self.rsem.at[0], self.plus)
        push(self.source, self.own, self.ssem.at[1], self.rsem.at[1], self.minus)

    def forward_left(self):
        wait_for(self.left, self.rsem.at[0])
        push(self.left_half, self.left_half, self.ssem.at[2], self.rsem.at[2], self.plus)

    def forward_right(self):
        wait_for(self.right, self.rsem.at[1])
        push(self.right_half, self.right_half, self.ssem.at[3], self.rsem.at[3], self.minus)

    def finish(self):
        wait_for(self.far_first, self.rsem.at[2])
        wait_for(self.far_second, self.rsem.at[3])

    def drain(self):
        wait_for(self.source, self.ssem.at[0])
        wait_for(self.source, self.ssem.at[1])
        wait_for(self.left_half, self.ssem.at[2])
        wait_for(self.right_half, self.ssem.at[3])


def qkv_kernel(
    hidden, attn_gain, wq, wk, wv, q_gain, k_gain, cosine, sine,
    q_out, kv_out,
    wq_all, normed, kv_stage, q_stage,
    own_sem, wq_s, wq_r, n_s, n_r, z_s, z_r, short_s, short_r, long_s, long_r, d_s, d_r, q_s, q_r,
):
    x, y, z, core = my_coords()
    ctx = lax.axis_index("ctx")
    x_lo = x % 2
    sibling = device_at(x, y, z, 1 - core)
    x_other = (x // 2) * 2 + 1 - x_lo
    x_near = device_at(x_other, y, z, core)
    far_ctx = jnp.where(z < 2, ctx, 7 - ctx)

    def head_device(block, zz):
        return (block, zz * 4 + x_lo * 2 + core)

    own_wq = pltpu.make_async_copy(wq, wq_all.at[z], own_sem)
    own_wq.start()
    barrier = pltpu.get_barrier_semaphore()

    def greet(device):
        pl.semaphore_signal(barrier, inc=1, device_id=device, device_id_type=MESH)

    for dz in range(4):
        for dc in range(2):
            if dz + dc > 0:
                greet(device_at(x, y, (z + dz) % 4, (core + dc) % 2))
        greet(head_device(7 - ctx, dz))
    for d in (1, 3):
        greet(device_at((x + d) % 4, y, z, core))
        greet(device_at(x, (y + d) % 4, z, core))
    mine = x_lo * 2 + core
    normed[mine] = rms_scale(hidden[...].astype(jnp.float32), attn_gain[...]).astype(jnp.bfloat16)
    pl.semaphore_wait(barrier, 15)

    def wq_half(zz, half):
        return wq_all.at[zz, pl.ds(half * 1024, 1024)]

    z_left, z_right, z_far = (z + 3) % 4, (z + 1) % 4, (z + 2) % 4
    wq_ring = Ring(
        (wq_all.at[z], wq_all.at[z_left], wq_all.at[z_right]),
        (wq_half(z_left, 0), wq_half(z_right, 1), wq_half(z_far, 0), wq_half(z_far, 1)),
        device_at(x, y, z_right, core), device_at(x, y, z_left, core), wq_s, wq_r, wq,
    )
    other = (1 - x_lo) * 2 + core
    push(normed.at[mine], normed.at[mine], n_s.at[1], n_r.at[1], x_near)
    push(normed.at[mine], normed.at[mine], n_s.at[0], n_r.at[0], sibling)
    wq_ring.start()

    here = pl.ds(mine * 128, 128)
    own_normed = normed[mine]
    key_raw = jnp.dot(own_normed, wk[...], preferred_element_type=jnp.float32)
    value_raw = jnp.dot(own_normed, wv[...], preferred_element_type=jnp.float32)
    for g in range(2):
        cols = slice(g * 128, (g + 1) * 128)
        key = rope(rms_scale(key_raw[:, cols], k_gain[...]), cosine[here, :], sine[here, :])
        kv_stage[0, g] = key.astype(jnp.bfloat16)
        kv_stage[1, g] = value_raw[:, cols].astype(jnp.bfloat16)

    def piece(which, xx, yy, zz, cc):
        return kv_out.at[which, xx // 2, yy, zz, xx % 2, pl.ds(cc * 128, 128)]

    for which in range(2):
        for zz in range(4):
            is_self = (zz == z) & (which == core)
            src = kv_stage.at[which, zz // 2]
            dst = piece(which, x, y, z, core)

            @pl.when(is_self)
            def _(src=src, dst=dst):
                pltpu.make_async_copy(src, dst, z_r.at[z * 2 + core]).start()

            @pl.when(jnp.logical_not(is_self))
            def _(src=src, dst=dst, which=which, zz=zz):
                push(src, dst, z_s.at[which * 4 + zz], z_r.at[z * 2 + core], device_at(x, y, zz, which))

    for zz in range(4):
        for cc in range(2):
            wait_for(piece(core, x, y, zz, cc), z_r.at[zz * 2 + cc])

    step_x, step_y = 1 - core, core

    def column(n, zs=None):
        xx, yy = (x + n * step_x) % 4, (y + n * step_y) % 4
        if zs is None:
            return kv_out.at[core, xx // 2, yy, :, xx % 2]
        return kv_out.at[core, xx // 2, yy, pl.ds(zs * 2, 2), xx % 2]

    short = Ring(
        (column(0), column(3), column(1)),
        (column(3, 0), column(1, 1), column(2, 0), column(2, 1)),
        device_at((x + step_x) % 4, (y + step_y) % 4, z, core),
        device_at((x + 3 * step_x) % 4, (y + 3 * step_y) % 4, z, core), short_s, short_r,
    )
    short.start()
    short.forward_left()
    short.forward_right()
    short.finish()

    def keys_of(n, half=None):
        yy = (y + n) % 4
        return kv_out.at[0, :, yy] if half is None else kv_out.at[0, half, yy]

    def values_of(n, half=None):
        xx = (x + n) % 4
        if half is None:
            return kv_out.at[1, xx // 2, :, :, xx % 2]
        return kv_out.at[1, xx // 2, pl.ds(half * 2, 2), :, xx % 2]

    def long_ring(of, plus, minus):
        return Ring(
            (of(0), of(3), of(1)), (of(3, 0), of(1, 1), of(2, 0), of(2, 1)), plus, minus, long_s, long_r
        )

    def rings():
        return (
            long_ring(keys_of, device_at(x, (y + 1) % 4, z, core), device_at(x, (y + 3) % 4, z, core)),
            long_ring(values_of, device_at((x + 1) % 4, y, z, core), device_at((x + 3) % 4, y, z, core)),
        )

    both = (keys_of, values_of)

    def on_core(body):
        for index in range(2):
            pl.when(core == index)(lambda index=index: body(index))

    def begin(index):
        rings()[index].start()
        push(both[index](0), both[index](0), d_s.at[0], d_r.at[0], sibling)

    on_core(begin)

    wq_ring.forward_left()
    wq_ring.forward_right()
    wait_for(normed.at[other], n_r.at[1])
    push(normed.at[other], normed.at[other], n_s.at[2], n_r.at[2], sibling)
    wait_for(normed.at[x_lo * 2 + 1 - core], n_r.at[0])
    own_wq.wait()
    wq_ring.finish()
    wait_for(normed.at[(1 - x_lo) * 2 + 1 - core], n_r.at[2])

    tokens = normed[...].reshape(512, 2048)
    for pair in range(2):
        weights = jnp.concatenate([wq_all[2 * pair], wq_all[2 * pair + 1]], axis=1)
        raw = jnp.dot(tokens, weights, preferred_element_type=jnp.float32)
        for k in range(2):
            query = rope(rms_scale(raw[:, k * 128 : (k + 1) * 128], q_gain[...]), cosine[...], sine[...])
            q_stage[2 * pair + k] = query.astype(jnp.bfloat16)

    def q_rows(zz):
        return q_out.at[zz // 2, pl.ds((zz % 2) * 512, 512)]

    for zz in range(4):
        is_self = (zz == z) & (z < 2)

        @pl.when(is_self)
        def _(zz=zz):
            pltpu.make_async_copy(q_stage.at[zz], q_rows(z), q_r.at[z]).start()

        @pl.when(jnp.logical_not(is_self))
        def _(zz=zz):
            push(q_stage.at[zz], q_rows(z), q_s.at[zz], q_r.at[z], head_device(far_ctx, zz))

    def later(index):
        ring, of = rings()[index], both[index]
        ring.forward_left()
        push(of(3), of(3), d_s.at[1], d_r.at[1], sibling)
        ring.forward_right()
        push(of(1), of(1), d_s.at[2], d_r.at[2], sibling)
        ring.finish()
        push(of(2), of(2), d_s.at[3], d_r.at[3], sibling)
        theirs = both[1 - index]
        for k, n in enumerate((0, 3, 1, 2)):
            wait_for(theirs(n), d_r.at[k])
        ring.drain()
        for k, n in enumerate((0, 3, 1, 2)):
            wait_for(of(n), d_s.at[k])

    on_core(later)
    for zz in range(4):
        wait_for(q_rows(zz), q_r.at[zz])
    wq_ring.drain()
    short.drain()
    wait_for(normed.at[mine], n_s.at[0])
    wait_for(normed.at[mine], n_s.at[1])
    wait_for(normed.at[other], n_s.at[2])
    for zz in range(4):

        @pl.when(jnp.logical_not((zz == z) & (z < 2)))
        def _(zz=zz):
            wait_for(q_stage.at[zz], q_s.at[zz])

        for which in range(2):

            @pl.when(jnp.logical_not((zz == z) & (which == core)))
            def _(zz=zz, which=which):
                wait_for(kv_stage.at[which, zz // 2], z_s.at[which * 4 + zz])


def project(hidden, attn_gain, wq, wk, wv, q_gain, k_gain, cosine, sine):
    vmem = pl.BlockSpec(memory_space=pltpu.VMEM)
    anywhere = pl.BlockSpec(memory_space=pl.ANY)
    dma = pltpu.SemaphoreType.DMA
    return pl.pallas_call(
        qkv_kernel,
        out_shape=(
            jax.ShapeDtypeStruct((2, 1024, 128), jnp.bfloat16),
            jax.ShapeDtypeStruct((2, 2, 4, 4, 2, 256, 128), jnp.bfloat16),
        ),
        in_specs=[vmem, vmem, anywhere] + [vmem] * 6,
        out_specs=(anywhere, anywhere),
        scratch_shapes=[
            pltpu.VMEM((4, 2048, 128), jnp.bfloat16),
            pltpu.VMEM((4, 128, 2048), jnp.bfloat16),
            pltpu.VMEM((2, 2, 128, 128), jnp.bfloat16),
            pltpu.VMEM((4, 512, 128), jnp.bfloat16),
            dma, dma((4,)), dma((4,)), dma((3,)), dma((3,)), dma((8,)), dma((8,)),
            dma((4,)), dma((4,)), dma((4,)), dma((4,)), dma((4,)), dma((4,)), dma((4,)), dma((4,)),
        ],
        compiler_params=pltpu.CompilerParams(
            collective_id=1, has_side_effects=True, vmem_limit_bytes=40 * 1024 * 1024
        ),
        name="project",
    )(hidden, attn_gain.reshape(1, -1), wq, wk, wv, q_gain.reshape(1, -1), k_gain.reshape(1, -1), cosine, sine)


QB = 256
TK = 1024


def flash_kernel(q_ref, kv_ref, o_ref, m_scr, acc_scr):
    ctx = lax.axis_index("ctx")
    half_rows = q_ref.shape[1]
    scale = math.log2(math.e) / math.sqrt(128)
    blocks = half_rows // QB

    def step(q, k, v, m_prev, acc, first_row):
        s = lax.dot_general(q, k, (((1,), (1,)), ((), ())), preferred_element_type=jnp.float32)
        if first_row is not None:
            row = lax.broadcasted_iota(jnp.int32, s.shape, 0) + first_row
            col = lax.broadcasted_iota(jnp.int32, s.shape, 1)
            s = jnp.where(col <= row, s, -1e30)
        m_new = jnp.maximum(m_prev, jnp.max(s, axis=1, keepdims=True))
        alpha = jnp.exp2((m_prev - m_new) * scale)
        shift = (m_new * scale)[:, :1]
        p = jnp.exp2(s * scale - shift).astype(jnp.bfloat16)
        joined = jnp.concatenate([v, jnp.ones_like(v)], axis=1)
        pv = jnp.dot(p, joined, preferred_element_type=jnp.float32)
        return m_new, acc * jnp.concatenate([alpha, alpha], axis=1) + pv

    for half in range(2):
        h = 2 * ctx if half == 0 else 15 - 2 * ctx
        m_scr[...] = jnp.full_like(m_scr, -1e30)
        acc_scr[...] = jnp.zeros_like(acc_scr)

        def tile(t, carry, half=half):
            k = kv_ref[0, pl.ds(t * TK, TK), :]
            v = kv_ref[1, pl.ds(t * TK, TK), :]
            for b in range(blocks):
                rows = pl.ds(b * QB, QB)
                m, a = step(q_ref[half, rows, :], k, v, m_scr[rows, :], acc_scr[rows, :], None)
                m_scr[rows, :] = m
                acc_scr[rows, :] = a
            return carry

        lax.fori_loop(0, h * (half_rows // TK), tile, 0)
        base = h * half_rows
        for b in range(blocks):
            rows = pl.ds(b * QB, QB)
            seen = (b + 1) * QB
            k = kv_ref[0, pl.ds(base, seen), :]
            v = kv_ref[1, pl.ds(base, seen), :]
            m, a = step(q_ref[half, rows, :], k, v, m_scr[rows, :], acc_scr[rows, :], b * QB)
            o_ref[half, rows, :] = (a[:, :128] / a[:, 128:]).astype(jnp.bfloat16)


def flash(q, kv):
    vmem = pl.BlockSpec(memory_space=pltpu.VMEM)
    return pl.pallas_call(
        flash_kernel,
        out_shape=jax.ShapeDtypeStruct(q.shape, jnp.bfloat16),
        in_specs=[vmem, vmem],
        out_specs=vmem,
        scratch_shapes=[
            pltpu.VMEM((q.shape[1], 128), jnp.float32),
            pltpu.VMEM((q.shape[1], 256), jnp.float32),
        ],
        compiler_params=pltpu.CompilerParams(vmem_limit_bytes=50 * 1024 * 1024),
        cost_estimate=pl.CostEstimate(flops=9 * 10**9, bytes_accessed=9 * 2**20, transcendentals=17 * 2**20),
        name="flash",
    )(q, kv)


def moe_kernel(
    cap,
    slot_tok, slot_at, shares,
    attended, hidden, ffn_gain, w_out, w_gate, w_up, w_down,
    out_ref,
    send_buf, in_buf, ans_buf, ret_buf, vo, vg, vu, vd, stage, xrows, x_tiles, heads, resid,
    wsem, osend, orecv, dsend, drecv, asend, arecv,
):
    ctx = lax.axis_index("ctx")
    exp = lax.axis_index("exp")
    tok = hidden.shape[0]
    copies = [
        pltpu.make_async_copy(w_gate, vg, wsem.at[0]),
        pltpu.make_async_copy(w_up, vu, wsem.at[1]),
        pltpu.make_async_copy(w_down, vd, wsem.at[2]),
        pltpu.make_async_copy(w_out, vo, wsem.at[3]),
    ]
    for copy in copies:
        copy.start()
    barrier = pltpu.get_barrier_semaphore()

    def greet(o, carry):
        pl.semaphore_signal(barrier, inc=1, device_id=peer_to(o), device_id_type=MESH)
        return carry

    lax.fori_loop(1, GROUPS * PEERS, greet, 0)
    x_tiles[tok:] = jnp.zeros((8, 16, 128), jnp.bfloat16)
    pl.semaphore_wait(barrier, GROUPS * PEERS - 1)
    my_columns = pl.ds(pl.multiple_of(exp * 128, 128), 128)

    def head_rows(e):
        return attended.at[e // 8, pl.ds((e % 8) * 128, 128)]

    def swap(e, carry):
        is_self = (e == exp) & (e < 8)

        @pl.when(is_self)
        def _():
            pltpu.make_async_copy(head_rows(e), heads.at[:, my_columns], orecv).start()

        @pl.when(jnp.logical_not(is_self))
        def _():
            push(
                head_rows(e), heads.at[:, my_columns], osend, orecv,
                (jnp.where(e < 8, ctx, 7 - ctx), e),
            )

        return carry

    lax.fori_loop(0, HEADS, swap, 0)
    copies[3].wait()
    wait_for(heads, orecv)
    projected = jnp.dot(heads[...], vo[...], preferred_element_type=jnp.float32)
    summed = (hidden[...].astype(jnp.float32) + projected).astype(jnp.bfloat16)
    resid[...] = summed
    normed = rms_scale(summed.astype(jnp.float32), ffn_gain[...])
    for s in range(16):
        stage[pl.ds(s, tok, stride=16), :] = normed[:, s * 128 : (s + 1) * 128]
    x_tiles[:tok] = stage[: tok * 16].astype(jnp.bfloat16).reshape(tok, 16, 128)

    for r in range(cap):
        in_buf[0, r] = x_tiles[slot_tok[r]]

    def fill(o, carry):
        for r in range(cap):
            send_buf[o, r] = x_tiles[slot_tok[o * cap + r]]
        return carry


    def dispatch(o, sem):
        return pltpu.make_async_remote_copy(
            src_ref=send_buf.at[o], dst_ref=in_buf.at[o],
            send_sem=dsend.at[sem], recv_sem=drecv.at[sem],
            device_id=peer_to(o), device_id_type=MESH,
        )

    def give_back(o, sem):
        return pltpu.make_async_remote_copy(
            src_ref=ans_buf.at[o], dst_ref=ret_buf.at[o],
            send_sem=asend.at[sem], recv_sem=arecv.at[sem],
            device_id=peer_from(o), device_id_type=MESH,
        )

    def send(o, carry):
        fill(o, 0)
        dispatch(o, o // PEERS).start()
        return carry

    lax.fori_loop(1, GROUPS * PEERS, send, 0)
    for copy in copies[:3]:
        copy.wait()
    rows = PEERS * cap

    def compute(g):
        block = in_buf[pl.ds(g * PEERS, PEERS)]
        stage[...] = block.astype(jnp.float32).reshape(rows * 16, 128)
        for s in range(16):
            xrows[:, s * 128 : (s + 1) * 128] = stage[pl.ds(s, rows, stride=16), :].astype(jnp.bfloat16)
        rows_in = xrows[...]
        gate = jnp.dot(rows_in, vg[...], preferred_element_type=jnp.float32)
        up = jnp.dot(rows_in, vu[...], preferred_element_type=jnp.float32)
        inner = (gate / (1.0 + jnp.exp(-gate)) * up).astype(jnp.bfloat16)
        for q in range(4):
            part = jnp.dot(inner, vd[:, q * 512 : (q + 1) * 512], preferred_element_type=jnp.float32)
            for s in range(4):
                stage[pl.ds(q * 4 + s, rows, stride=16), :] = part[:, s * 128 : (s + 1) * 128]
        return stage[...].astype(jnp.bfloat16).reshape(PEERS, cap, 16, 128)

    def wait_bytes(buf, start, count, sem):
        pltpu.make_async_copy(buf.at[pl.ds(start, count)], buf.at[pl.ds(start, count)], sem).wait()

    def start_back(o, sem):
        give_back(o, sem).start()
        return sem

    for g in range(GROUPS):
        first = 1 if g == 0 else 0
        wait_bytes(in_buf, g * PEERS + first, PEERS - first, drecv.at[g])
        answers = compute(g)
        if g == 0:
            ret_buf[0] = answers[0]
        ans_buf[pl.ds(g * PEERS, PEERS)] = answers
        lax.fori_loop(g * PEERS + first, (g + 1) * PEERS, lambda o, c, g=g: start_back(o, g), g)
    for g in range(GROUPS):
        first = 1 if g == 0 else 0
        wait_bytes(ret_buf, g * PEERS + first, PEERS - first, arecv.at[g])

    def combine(t, carry):
        total = jnp.zeros((16, 128), jnp.float32)
        for k in range(TOPK):
            at = slot_at[t * TOPK + k]
            total += shares[t * TOPK + k] * ret_buf[at // cap, at % cap].astype(jnp.float32)
        stage[pl.ds(t * 16, 16), :] = total
        return carry

    lax.fori_loop(0, tok, combine, 0)
    for s in range(16):
        cols = slice(s * 128, (s + 1) * 128)
        mixture = stage[pl.ds(s, tok, stride=16), :]
        out_ref[:, cols] = (resid[:, cols].astype(jnp.float32) + mixture).astype(jnp.bfloat16)
    for g in range(GROUPS):
        first = 1 if g == 0 else 0
        wait_bytes(send_buf, g * PEERS + first, PEERS - first, dsend.at[g])
        wait_bytes(ans_buf, g * PEERS + first, PEERS - first, asend.at[g])

    @pl.when(exp < 8)
    def _():
        wait_for(heads.at[:, pl.ds(0, 15 * 128)], osend)

    @pl.when(exp >= 8)
    def _():
        wait_for(heads, osend)


def slots_of(expert_ids, tok_rows, cap):
    flat = expert_ids.reshape(-1)
    count = flat.shape[0]
    ids = jnp.arange(128, dtype=jnp.int32)
    matches = flat[:, None] == ids[None, :]
    row = jnp.arange(count, dtype=jnp.int32)
    earlier = (row[:, None] > row[None, :]).astype(jnp.bfloat16)
    before = jnp.dot(earlier, matches.astype(jnp.bfloat16), preferred_element_type=jnp.float32)
    rank = jnp.sum(jnp.where(matches, before, 0.0), axis=1).astype(jnp.int32)
    slot_at = offset_of_expert(flat) * cap + rank
    slot_tok = jnp.full((128 * cap,), tok_rows, jnp.int32).at[slot_at].set(row // TOPK)
    return slot_tok, slot_at


def tail(attended, hidden, ffn_gain, w_out, slot_tok, slot_at, shares, w_gate, w_up, w_down):
    tok, width = hidden.shape
    ff = w_gate.shape[1]
    n = GROUPS * PEERS
    vmem = pl.BlockSpec(memory_space=pltpu.VMEM)
    anywhere = pl.BlockSpec(memory_space=pl.ANY)
    dma = pltpu.SemaphoreType.DMA
    return pl.pallas_call(
        functools.partial(moe_kernel, CAP),
        out_shape=jax.ShapeDtypeStruct((tok, width), jnp.bfloat16),
        in_specs=[pl.BlockSpec(memory_space=pltpu.SMEM)] * 3 + [vmem] * 3 + [anywhere] * 4,
        out_specs=vmem,
        scratch_shapes=[pltpu.VMEM((n, CAP, 16, 128), jnp.bfloat16)] * 4
        + [
            pltpu.VMEM((width, width), jnp.bfloat16),
            pltpu.VMEM((width, ff), jnp.bfloat16),
            pltpu.VMEM((width, ff), jnp.bfloat16),
            pltpu.VMEM((ff, width), jnp.bfloat16),
            pltpu.VMEM((PEERS * CAP * 16, 128), jnp.float32),
            pltpu.VMEM((PEERS * CAP, width), jnp.bfloat16),
            pltpu.VMEM((tok + 8, 16, 128), jnp.bfloat16),
            pltpu.VMEM((tok, width), jnp.bfloat16),
            pltpu.VMEM((tok, width), jnp.bfloat16),
            dma((4,)), dma, dma, dma((GROUPS,)), dma((GROUPS,)), dma((GROUPS,)), dma((GROUPS,)),
        ],
        compiler_params=pltpu.CompilerParams(
            collective_id=3, has_side_effects=True, vmem_limit_bytes=62 * 1024 * 1024
        ),
        name="tail",
    )(slot_tok, slot_at, shares.reshape(-1), attended, hidden, ffn_gain.reshape(1, -1), w_out, w_gate, w_up, w_down)


def on_device(
    hidden_in, attn_gain, w_query, w_key, w_value, q_gain, k_gain, w_out, ffn_gain,
    w_gate, w_up, w_down, expert_ids, gate_weights,
):
    ctx, exp = lax.axis_index("ctx"), lax.axis_index("exp")
    w_out_all = lax.all_gather(w_out, "exp", axis=0, tiled=True)
    places = ctx * 2048 + (exp // 4) * 512 + jnp.arange(512, dtype=jnp.int32)
    frequency = jnp.exp(jnp.arange(64, dtype=jnp.float32) * (-2.0 * math.log(rope_base) / 128))
    angles = places.astype(jnp.float32)[:, None] * frequency[None, :]
    cosine, sine = jnp.cos(angles), jnp.sin(angles)
    q, kv = project(
        hidden_in, attn_gain, w_query, w_key, w_value, q_gain, k_gain,
        jnp.concatenate([cosine, cosine], axis=1), jnp.concatenate([-sine, sine], axis=1),
    )
    shares = gate_weights / jnp.sum(gate_weights, axis=1, keepdims=True)
    slot_tok, slot_at = slots_of(expert_ids, hidden_in.shape[0], CAP)
    attended = flash(q, kv.reshape(2, 16384, 128))
    return tail(
        attended, hidden_in, ffn_gain, w_out_all, slot_tok, slot_at, shares, w_gate[0], w_up[0], w_down[0]
    )


def solution(mesh):
    placed = (
        P(("ctx", "exp"), None),
        P(),
        P(None, "exp"),
        P(),
        P(),
        P(),
        P(),
        P("exp", None),
        P(),
        P(("ctx", "exp"), None, None),
        P(("ctx", "exp"), None, None),
        P(("ctx", "exp"), None, None),
        P(("ctx", "exp"), None),
        P(("ctx", "exp"), None),
    )
    return jax.shard_map(
        on_device, mesh=mesh, in_specs=placed, out_specs=P(("ctx", "exp"), None), check_vma=False
    )
```

```python
import functools
import math

import jax
import jax.numpy as jnp
from jax import lax
from jax.experimental import pallas as pl
from jax.experimental.pallas import tpu as pltpu
from jax.sharding import PartitionSpec as P

MESH = pl.DeviceIdType.MESH
TOPK = 8
CAP = 10
HEADS = 16
GROUPS = 4
PEERS = 32


def my_coords():
    ctx = lax.axis_index("ctx")
    exp = lax.axis_index("exp")
    x = (ctx // 4) * 2 + (exp // 2) % 2
    return x, ctx % 4, exp // 4, exp % 2


def device_at(x, y, z, core):
    return ((x // 2) * 4 + y, z * 4 + (x % 2) * 2 + core)


def offset_parts(o):
    dc, k, dy, dx = o // 64, (o // 16) % 4, (o // 4) % 4, o % 4
    return dx, dy, (k + 8 - dx - dy) % 4, dc


def peer_to(o):
    x, y, z, c = my_coords()
    dx, dy, dz, dc = offset_parts(o)
    return device_at((x + dx) % 4, (y + dy) % 4, (z + dz) % 4, (c + dc) % 2)


def peer_from(o):
    x, y, z, c = my_coords()
    dx, dy, dz, dc = offset_parts(o)
    return device_at((x + 4 - dx) % 4, (y + 4 - dy) % 4, (z + 4 - dz) % 4, (c + 2 - dc) % 2)


def offset_of_expert(e):
    x, y, z, c = my_coords()
    dx = (((e >> 6) & 1) * 2 + ((e >> 1) & 1) + 4 - x) & 3
    dy = ((e >> 4) + 4 - y) & 3
    dz = ((e >> 2) + 4 - z) & 3
    dc = (e + 2 - c) & 1
    return dc * 64 + ((dx + dy + dz) & 3) * 16 + dy * 4 + dx
epsilon = 1e-06
rope_base = 1000000.0


def rms_scale(values, gains):
    return values * lax.rsqrt(jnp.mean(values * values, axis=-1, keepdims=True) + epsilon) * gains


def rope(values, cosine, sine):
    return values * cosine + pltpu.roll(values, 64, 1) * sine


def push(src, dst, ssem, rsem, device):
    pltpu.make_async_remote_copy(
        src_ref=src, dst_ref=dst, send_sem=ssem, recv_sem=rsem,
        device_id=device, device_id_type=MESH,
    ).start()


def wait_for(ref, sem):
    pltpu.make_async_copy(ref, ref, sem).wait()


class Ring:
    def __init__(self, blocks, halves, plus, minus, ssem, rsem, source=None):
        self.own, self.left, self.right = blocks
        self.left_half, self.right_half, self.far_first, self.far_second = halves
        self.plus, self.minus, self.ssem, self.rsem = plus, minus, ssem, rsem
        self.source = self.own if source is None else source

    def start(self):
        push(self.source, self.own, self.ssem.at[0], self.rsem.at[0], self.plus)
        push(self.source, self.own, self.ssem.at[1], self.rsem.at[1], self.minus)

    def forward_left(self):
        wait_for(self.left, self.rsem.at[0])
        push(self.left_half, self.left_half, self.ssem.at[2], self.rsem.at[2], self.plus)

    def forward_right(self):
        wait_for(self.right, self.rsem.at[1])
        push(self.right_half, self.right_half, self.ssem.at[3], self.rsem.at[3], self.minus)

    def finish(self):
        wait_for(self.far_first, self.rsem.at[2])
        wait_for(self.far_second, self.rsem.at[3])

    def drain(self):
        wait_for(self.source, self.ssem.at[0])
        wait_for(self.source, self.ssem.at[1])
        wait_for(self.left_half, self.ssem.at[2])
        wait_for(self.right_half, self.ssem.at[3])


def assign_slots(expert_ids, slot_tok, slot_at):
    sub = lax.broadcasted_iota(jnp.int32, (128, 128), 0)
    lane = lax.broadcasted_iota(jnp.int32, (128, 128), 1)
    eye = (sub == lane).astype(jnp.bfloat16)
    before = (sub < lane).astype(jnp.bfloat16)
    ones = jnp.ones((128, 128), jnp.bfloat16)
    ids = expert_ids[...].astype(jnp.float32).astype(jnp.bfloat16)
    turned = lax.dot_general(ids, eye, (((0,), (0,)), ((), ())), preferred_element_type=jnp.float32)
    offsets = offset_of_expert(turned.astype(jnp.int32))
    base = jnp.zeros((128, 128), jnp.float32)
    named, ranks = [], []
    for k in range(TOPK):
        match = (sub == offsets[k : k + 1, :]).astype(jnp.float32)
        match_low = match.astype(jnp.bfloat16)
        place = base + jnp.dot(match_low, before, preferred_element_type=jnp.float32)
        rank = jnp.sum(match * place, axis=0, keepdims=True)
        base = base + jnp.dot(match_low, ones, preferred_element_type=jnp.float32)
        named.append(match)
        ranks.append(rank)
        slot_at[k : k + 1, :] = offsets[k : k + 1, :] * CAP + rank.astype(jnp.int32)
    token = (128 - lane[:8]).astype(jnp.float32).astype(jnp.bfloat16)
    slot_tok[...] = jnp.full(slot_tok.shape, 128, jnp.int32)
    for r in range(CAP):
        chosen = jnp.zeros((128, 128), jnp.float32)
        for k in range(TOPK):
            chosen = chosen + jnp.where(ranks[k] == r, named[k], 0.0)
        found = lax.dot_general(
            token, chosen.astype(jnp.bfloat16), (((1,), (1,)), ((), ())), preferred_element_type=jnp.float32
        )
        slot_tok[r : r + 1, :] = 128 - found[0:1].astype(jnp.int32)


def qkv_kernel(
    hidden, attn_gain, wq, wk, wv, q_gain, k_gain, cosine, sine, expert_ids,
    q_out, kv_out, slot_tok, slot_at,
    wq_all, normed, kv_stage, q_stage,
    own_sem, wq_s, wq_r, n_s, n_r, z_s, z_r, short_s, short_r, long_s, long_r, d_s, d_r, q_s, q_r,
):
    x, y, z, core = my_coords()
    ctx = lax.axis_index("ctx")
    x_lo = x % 2
    sibling = device_at(x, y, z, 1 - core)
    x_other = (x // 2) * 2 + 1 - x_lo
    x_near = device_at(x_other, y, z, core)
    far_ctx = jnp.where(z < 2, ctx, 7 - ctx)

    def head_device(block, zz):
        return (block, zz * 4 + x_lo * 2 + core)

    own_wq = pltpu.make_async_copy(wq, wq_all.at[z], own_sem)
    own_wq.start()
    barrier = pltpu.get_barrier_semaphore()

    def greet(device):
        pl.semaphore_signal(barrier, inc=1, device_id=device, device_id_type=MESH)

    for dz in range(4):
        for dc in range(2):
            if dz + dc > 0:
                greet(device_at(x, y, (z + dz) % 4, (core + dc) % 2))
        greet(head_device(7 - ctx, dz))
    for d in (1, 3):
        greet(device_at((x + d) % 4, y, z, core))
        greet(device_at(x, (y + d) % 4, z, core))
    mine = x_lo * 2 + core
    normed[mine] = rms_scale(hidden[...].astype(jnp.float32), attn_gain[...]).astype(jnp.bfloat16)
    pl.semaphore_wait(barrier, 15)

    def wq_half(zz, half):
        return wq_all.at[zz, pl.ds(half * 1024, 1024)]

    z_left, z_right, z_far = (z + 3) % 4, (z + 1) % 4, (z + 2) % 4
    wq_ring = Ring(
        (wq_all.at[z], wq_all.at[z_left], wq_all.at[z_right]),
        (wq_half(z_left, 0), wq_half(z_right, 1), wq_half(z_far, 0), wq_half(z_far, 1)),
        device_at(x, y, z_right, core), device_at(x, y, z_left, core), wq_s, wq_r, wq,
    )
    other = (1 - x_lo) * 2 + core
    push(normed.at[mine], normed.at[mine], n_s.at[1], n_r.at[1], x_near)
    push(normed.at[mine], normed.at[mine], n_s.at[0], n_r.at[0], sibling)
    wq_ring.start()

    here = pl.ds(mine * 128, 128)
    own_normed = normed[mine]
    key_raw = jnp.dot(own_normed, wk[...], preferred_element_type=jnp.float32)
    value_raw = jnp.dot(own_normed, wv[...], preferred_element_type=jnp.float32)
    for g in range(2):
        cols = slice(g * 128, (g + 1) * 128)
        key = rope(rms_scale(key_raw[:, cols], k_gain[...]), cosine[here, :], sine[here, :])
        kv_stage[0, g] = key.astype(jnp.bfloat16)
        kv_stage[1, g] = value_raw[:, cols].astype(jnp.bfloat16)

    def piece(which, xx, yy, zz, cc):
        return kv_out.at[which, xx // 2, yy, zz, xx % 2, pl.ds(cc * 128, 128)]

    for which in range(2):
        for zz in range(4):
            is_self = (zz == z) & (which == core)
            src = kv_stage.at[which, zz // 2]
            dst = piece(which, x, y, z, core)

            @pl.when(is_self)
            def _(src=src, dst=dst):
                pltpu.make_async_copy(src, dst, z_r.at[z * 2 + core]).start()

            @pl.when(jnp.logical_not(is_self))
            def _(src=src, dst=dst, which=which, zz=zz):
                push(src, dst, z_s.at[which * 4 + zz], z_r.at[z * 2 + core], device_at(x, y, zz, which))

    for zz in range(4):
        for cc in range(2):
            wait_for(piece(core, x, y, zz, cc), z_r.at[zz * 2 + cc])

    step_x, step_y = 1 - core, core

    def column(n, zs=None):
        xx, yy = (x + n * step_x) % 4, (y + n * step_y) % 4
        if zs is None:
            return kv_out.at[core, xx // 2, yy, :, xx % 2]
        return kv_out.at[core, xx // 2, yy, pl.ds(zs * 2, 2), xx % 2]

    short = Ring(
        (column(0), column(3), column(1)),
        (column(3, 0), column(1, 1), column(2, 0), column(2, 1)),
        device_at((x + step_x) % 4, (y + step_y) % 4, z, core),
        device_at((x + 3 * step_x) % 4, (y + 3 * step_y) % 4, z, core), short_s, short_r,
    )
    short.start()
    short.forward_left()
    short.forward_right()
    short.finish()

    def keys_of(n, half=None):
        yy = (y + n) % 4
        return kv_out.at[0, :, yy] if half is None else kv_out.at[0, half, yy]

    def values_of(n, half=None):
        xx = (x + n) % 4
        if half is None:
            return kv_out.at[1, xx // 2, :, :, xx % 2]
        return kv_out.at[1, xx // 2, pl.ds(half * 2, 2), :, xx % 2]

    def long_ring(of, plus, minus):
        return Ring(
            (of(0), of(3), of(1)), (of(3, 0), of(1, 1), of(2, 0), of(2, 1)), plus, minus, long_s, long_r
        )

    def rings():
        return (
            long_ring(keys_of, device_at(x, (y + 1) % 4, z, core), device_at(x, (y + 3) % 4, z, core)),
            long_ring(values_of, device_at((x + 1) % 4, y, z, core), device_at((x + 3) % 4, y, z, core)),
        )

    both = (keys_of, values_of)

    def on_core(body):
        for index in range(2):
            pl.when(core == index)(lambda index=index: body(index))

    def begin(index):
        rings()[index].start()
        push(both[index](0), both[index](0), d_s.at[0], d_r.at[0], sibling)

    on_core(begin)
    assign_slots(expert_ids, slot_tok, slot_at)

    wq_ring.forward_left()
    wq_ring.forward_right()
    wait_for(normed.at[other], n_r.at[1])
    push(normed.at[other], normed.at[other], n_s.at[2], n_r.at[2], sibling)
    wait_for(normed.at[x_lo * 2 + 1 - core], n_r.at[0])
    own_wq.wait()
    wq_ring.finish()
    wait_for(normed.at[(1 - x_lo) * 2 + 1 - core], n_r.at[2])

    tokens = normed[...].reshape(512, 2048)
    for pair in range(2):
        weights = jnp.concatenate([wq_all[2 * pair], wq_all[2 * pair + 1]], axis=1)
        raw = jnp.dot(tokens, weights, preferred_element_type=jnp.float32)
        for k in range(2):
            query = rope(rms_scale(raw[:, k * 128 : (k + 1) * 128], q_gain[...]), cosine[...], sine[...])
            q_stage[2 * pair + k] = query.astype(jnp.bfloat16)

    def q_rows(zz):
        return q_out.at[zz // 2, pl.ds((zz % 2) * 512, 512)]

    for zz in range(4):
        is_self = (zz == z) & (z < 2)

        @pl.when(is_self)
        def _(zz=zz):
            pltpu.make_async_copy(q_stage.at[zz], q_rows(z), q_r.at[z]).start()

        @pl.when(jnp.logical_not(is_self))
        def _(zz=zz):
            push(q_stage.at[zz], q_rows(z), q_s.at[zz], q_r.at[z], head_device(far_ctx, zz))

    def later(index):
        ring, of = rings()[index], both[index]
        ring.forward_left()
        push(of(3), of(3), d_s.at[1], d_r.at[1], sibling)
        ring.forward_right()
        push(of(1), of(1), d_s.at[2], d_r.at[2], sibling)
        ring.finish()
        push(of(2), of(2), d_s.at[3], d_r.at[3], sibling)
        theirs = both[1 - index]
        for k, n in enumerate((0, 3, 1, 2)):
            wait_for(theirs(n), d_r.at[k])
        ring.drain()
        for k, n in enumerate((0, 3, 1, 2)):
            wait_for(of(n), d_s.at[k])

    on_core(later)
    for zz in range(4):
        wait_for(q_rows(zz), q_r.at[zz])
    wq_ring.drain()
    short.drain()
    wait_for(normed.at[mine], n_s.at[0])
    wait_for(normed.at[mine], n_s.at[1])
    wait_for(normed.at[other], n_s.at[2])
    for zz in range(4):

        @pl.when(jnp.logical_not((zz == z) & (z < 2)))
        def _(zz=zz):
            wait_for(q_stage.at[zz], q_s.at[zz])

        for which in range(2):

            @pl.when(jnp.logical_not((zz == z) & (which == core)))
            def _(zz=zz, which=which):
                wait_for(kv_stage.at[which, zz // 2], z_s.at[which * 4 + zz])


def project(hidden, attn_gain, wq, wk, wv, q_gain, k_gain, cosine, sine, expert_ids):
    vmem = pl.BlockSpec(memory_space=pltpu.VMEM)
    anywhere = pl.BlockSpec(memory_space=pl.ANY)
    dma = pltpu.SemaphoreType.DMA
    return pl.pallas_call(
        qkv_kernel,
        out_shape=(
            jax.ShapeDtypeStruct((2, 1024, 128), jnp.bfloat16),
            jax.ShapeDtypeStruct((2, 2, 4, 4, 2, 256, 128), jnp.bfloat16),
            jax.ShapeDtypeStruct((16, 128), jnp.int32),
            jax.ShapeDtypeStruct((TOPK, 128), jnp.int32),
        ),
        in_specs=[vmem, vmem, anywhere] + [vmem] * 7,
        out_specs=(anywhere, anywhere, vmem, vmem),
        scratch_shapes=[
            pltpu.VMEM((4, 2048, 128), jnp.bfloat16),
            pltpu.VMEM((4, 128, 2048), jnp.bfloat16),
            pltpu.VMEM((2, 2, 128, 128), jnp.bfloat16),
            pltpu.VMEM((4, 512, 128), jnp.bfloat16),
            dma, dma((4,)), dma((4,)), dma((3,)), dma((3,)), dma((8,)), dma((8,)),
            dma((4,)), dma((4,)), dma((4,)), dma((4,)), dma((4,)), dma((4,)), dma((4,)), dma((4,)),
        ],
        compiler_params=pltpu.CompilerParams(
            collective_id=1, has_side_effects=True, vmem_limit_bytes=40 * 1024 * 1024
        ),
        name="project",
    )(hidden, attn_gain.reshape(1, -1), wq, wk, wv, q_gain.reshape(1, -1), k_gain.reshape(1, -1), cosine, sine, expert_ids)


QB = 256
TK = 1024


def flash_kernel(q_ref, kv_ref, w_out, o_ref, w_all, kv, m_scr, acc_scr,
                 kv_sem, own_sem, a_s, a_r, b_s, b_r, x_s, x_r, d_s, d_r):
    x, y, z, core = my_coords()
    ctx = lax.axis_index("ctx")
    half_rows = q_ref.shape[1]
    scale = math.log2(math.e) / math.sqrt(128)
    blocks = half_rows // QB
    tiles = kv_ref.shape[1] // TK

    def tile_copy(t):
        rows = pl.ds(t * TK, TK)
        return pltpu.make_async_copy(kv_ref.at[:, rows, :], kv.at[:, rows, :], kv_sem.at[t])

    lax.fori_loop(0, tiles, lambda t, c: (tile_copy(t).start(), c)[1], 0)

    x_lo = x % 2
    sibling = device_at(x, y, z, 1 - core)
    x_near = device_at((x // 2) * 2 + 1 - x_lo, y, z, core)
    plus, minus = device_at(x, y, (z + 1) % 4, core), device_at(x, y, (z + 3) % 4, core)
    barrier = pltpu.get_barrier_semaphore()
    for device in (sibling, x_near, plus, minus):
        pl.semaphore_signal(barrier, inc=1, device_id=device, device_id_type=MESH)

    def shard(dz, xl, cc):
        return w_all.at[(z + dz) % 4, xl, cc]

    def part(dz, xl, half):
        return w_all.at[(z + dz) % 4, xl, core, pl.ds(half * 64, 64)]

    ring = Ring(
        (shard(0, x_lo, core), shard(3, x_lo, core), shard(1, x_lo, core)),
        (part(3, x_lo, 0), part(1, x_lo, 1), part(2, x_lo, 0), part(2, x_lo, 1)),
        plus, minus, a_s, a_r, w_out,
    )
    x_hi_half = 1 - x_lo
    order = [(0, 0), (3, 0), (1, 0), (2, 0), (0, 1), (3, 1), (1, 1), (2, 1)]

    def share(n, src=None):
        dz, flip = order[n]
        xl = x_hi_half if flip else x_lo
        push(shard(dz, xl, core) if src is None else src, shard(dz, xl, core), d_s.at[n], d_r.at[n], sibling)

    own = pltpu.make_async_copy(w_out, shard(0, x_lo, core), own_sem)

    def stage_0():
        own.start()
        ring.start()
        push(w_out, shard(0, x_lo, core), x_s.at[0], x_r.at[0], x_near)
        share(0, w_out)

    def stage_1():
        ring.forward_left()
        ring.forward_right()
        share(1)
        share(2)
        theirs = shard(0, x_hi_half, core)
        wait_for(theirs, x_r.at[0])
        push(theirs, theirs, b_s.at[0], b_r.at[0], plus)
        push(theirs, theirs, b_s.at[1], b_r.at[1], minus)
        share(4)

    def stage_2():
        ring.finish()
        push(shard(2, x_lo, core), shard(2, x_lo, core), x_s.at[1], x_r.at[1], x_near)
        share(3)

    def stage_3():
        wait_for(shard(3, x_hi_half, core), b_r.at[0])
        share(5)
        wait_for(shard(1, x_hi_half, core), b_r.at[1])
        share(6)
        wait_for(shard(2, x_hi_half, core), x_r.at[1])
        share(7)

    def stage_4():
        for n, (dz, flip) in enumerate(order):
            wait_for(shard(dz, x_hi_half if flip else x_lo, 1 - core), d_r.at[n])
            wait_for(shard(dz, x_hi_half if flip else x_lo, core), d_s.at[n])
        own.wait()
        ring.drain()
        wait_for(w_out, x_s.at[0])
        wait_for(w_out, x_s.at[1])
        wait_for(w_out, b_s.at[0])
        wait_for(w_out, b_s.at[1])

    def step(q, k, v, m_prev, acc, first_row):
        s = lax.dot_general(q, k, (((1,), (1,)), ((), ())), preferred_element_type=jnp.float32)
        if first_row is not None:
            row = lax.broadcasted_iota(jnp.int32, s.shape, 0) + first_row
            col = lax.broadcasted_iota(jnp.int32, s.shape, 1)
            s = jnp.where(col <= row, s, -1e30)
        m_new = jnp.maximum(m_prev, jnp.max(s, axis=1, keepdims=True))
        alpha = jnp.exp2((m_prev - m_new) * scale)
        shift = (m_new * scale)[:, :1]
        p = jnp.exp2(s * scale - shift).astype(jnp.bfloat16)
        joined = jnp.concatenate([v, jnp.ones_like(v)], axis=1)
        pv = jnp.dot(p, joined, preferred_element_type=jnp.float32)
        return m_new, acc * jnp.concatenate([alpha, alpha], axis=1) + pv

    m_scr[...] = jnp.full_like(m_scr, -1e30)
    acc_scr[...] = jnp.zeros_like(acc_scr)
    last = (2 * ctx, 15 - 2 * ctx)
    pl.semaphore_wait(barrier, 4)
    stage_0()

    def full(half, t):
        k = kv[0, pl.ds(t * TK, TK), :]
        v = kv[1, pl.ds(t * TK, TK), :]
        for b in range(blocks):
            rows = pl.ds(b * QB, QB)
            m, a = step(q_ref[half, rows, :], k, v, m_scr[half, rows, :], acc_scr[half, rows, :], None)
            m_scr[half, rows, :] = m
            acc_scr[half, rows, :] = a

    def done_by(t):
        return jnp.minimum(t, last[0]) + jnp.minimum(t, last[1])

    def tile(t, carry):
        tile_copy(t).wait()
        done, earlier = done_by(t), done_by(t - 1)
        pl.when((done >= 6) & (earlier < 6))(stage_1)
        pl.when((done >= 11) & (earlier < 11))(stage_2)
        for half in range(2):
            pl.when(t < last[half])(functools.partial(full, half, t))
        return carry

    lax.fori_loop(0, tiles, tile, 0)
    stage_3()
    for half in range(2):
        base = last[half] * half_rows
        for b in range(blocks):
            rows = pl.ds(b * QB, QB)
            seen = (b + 1) * QB
            k = kv[0, pl.ds(base, seen), :]
            v = kv[1, pl.ds(base, seen), :]
            m, a = step(q_ref[half, rows, :], k, v, m_scr[half, rows, :], acc_scr[half, rows, :], b * QB)
            o_ref[half, rows, :] = (a[:, :128] / a[:, 128:]).astype(jnp.bfloat16)
    stage_4()


def flash(q, kv, w_out):
    vmem = pl.BlockSpec(memory_space=pltpu.VMEM)
    anywhere = pl.BlockSpec(memory_space=pl.ANY)
    dma = pltpu.SemaphoreType.DMA
    return pl.pallas_call(
        flash_kernel,
        out_shape=(
            jax.ShapeDtypeStruct(q.shape, jnp.bfloat16),
            jax.ShapeDtypeStruct((4, 2, 2, 128, 2048), jnp.bfloat16),
        ),
        in_specs=[vmem, anywhere, anywhere],
        out_specs=(vmem, anywhere),
        scratch_shapes=[
            pltpu.VMEM(kv.shape, jnp.bfloat16),
            pltpu.VMEM((2, q.shape[1], 128), jnp.float32),
            pltpu.VMEM((2, q.shape[1], 256), jnp.float32),
            dma((kv.shape[1] // TK,)), dma, dma((4,)), dma((4,)), dma((2,)), dma((2,)), dma((2,)), dma((2,)),
            dma((8,)), dma((8,)),
        ],
        compiler_params=pltpu.CompilerParams(
            collective_id=2, has_side_effects=True, vmem_limit_bytes=50 * 1024 * 1024
        ),
        name="flash",
    )(q, kv, w_out)


def moe_kernel(
    cap,
    slot_tok, slot_at, gates,
    attended, hidden, ffn_gain, w_out, w_gate, w_up, w_down,
    out_ref,
    send_buf, in_buf, ans_buf, ret_buf, vo, vg, vu, vd, stage, xrows, x_tiles, heads, resid,
    wsem, osend, orecv, dsend, drecv, asend, arecv,
):
    ctx = lax.axis_index("ctx")
    exp = lax.axis_index("exp")
    tok = hidden.shape[0]
    copies = [
        pltpu.make_async_copy(w_gate, vg, wsem.at[0]),
        pltpu.make_async_copy(w_up, vu, wsem.at[1]),
        pltpu.make_async_copy(w_down, vd, wsem.at[2]),
        pltpu.make_async_copy(w_out, vo, wsem.at[3]),
    ]
    for copy in copies:
        copy.start()
    barrier = pltpu.get_barrier_semaphore()

    def greet(o, carry):
        pl.semaphore_signal(barrier, inc=1, device_id=peer_to(o), device_id_type=MESH)
        return carry

    lax.fori_loop(1, GROUPS * PEERS, greet, 0)
    x_tiles[tok:] = jnp.zeros((8, 16, 128), jnp.bfloat16)
    pl.semaphore_wait(barrier, GROUPS * PEERS - 1)
    my_columns = pl.ds(pl.multiple_of(exp * 128, 128), 128)

    def head_rows(e):
        return attended.at[e // 8, pl.ds((e % 8) * 128, 128)]

    def swap(e, carry):
        is_self = (e == exp) & (e < 8)

        @pl.when(is_self)
        def _():
            pltpu.make_async_copy(head_rows(e), heads.at[:, my_columns], orecv).start()

        @pl.when(jnp.logical_not(is_self))
        def _():
            push(
                head_rows(e), heads.at[:, my_columns], osend, orecv,
                (jnp.where(e < 8, ctx, 7 - ctx), e),
            )

        return carry

    lax.fori_loop(0, HEADS, swap, 0)
    copies[3].wait()
    wait_for(heads, orecv)
    projected = jnp.dot(heads[...], vo[...], preferred_element_type=jnp.float32)
    summed = (hidden[...].astype(jnp.float32) + projected).astype(jnp.bfloat16)
    resid[...] = summed
    normed = rms_scale(summed.astype(jnp.float32), ffn_gain[...])
    for s in range(16):
        stage[pl.ds(s, tok, stride=16), :] = normed[:, s * 128 : (s + 1) * 128]
    x_tiles[:tok] = stage[: tok * 16].astype(jnp.bfloat16).reshape(tok, 16, 128)

    for r in range(cap):
        in_buf[0, r] = x_tiles[slot_tok[r, 0]]

    def fill(o, carry):
        for r in range(cap):
            send_buf[o, r] = x_tiles[slot_tok[r, o]]
        return carry


    def dispatch(o, sem):
        return pltpu.make_async_remote_copy(
            src_ref=send_buf.at[o], dst_ref=in_buf.at[o],
            send_sem=dsend.at[sem], recv_sem=drecv.at[sem],
            device_id=peer_to(o), device_id_type=MESH,
        )

    def give_back(o, sem):
        return pltpu.make_async_remote_copy(
            src_ref=ans_buf.at[o], dst_ref=ret_buf.at[o],
            send_sem=asend.at[sem], recv_sem=arecv.at[sem],
            device_id=peer_from(o), device_id_type=MESH,
        )

    def send(o, carry):
        fill(o, 0)
        dispatch(o, o // PEERS).start()
        return carry

    lax.fori_loop(1, GROUPS * PEERS, send, 0)
    for copy in copies[:3]:
        copy.wait()
    rows = PEERS * cap

    def compute(g):
        block = in_buf[pl.ds(g * PEERS, PEERS)]
        stage[...] = block.astype(jnp.float32).reshape(rows * 16, 128)
        for s in range(16):
            xrows[:, s * 128 : (s + 1) * 128] = stage[pl.ds(s, rows, stride=16), :].astype(jnp.bfloat16)
        rows_in = xrows[...]
        gate = jnp.dot(rows_in, vg[...], preferred_element_type=jnp.float32)
        up = jnp.dot(rows_in, vu[...], preferred_element_type=jnp.float32)
        inner = (gate / (1.0 + jnp.exp(-gate)) * up).astype(jnp.bfloat16)
        for q in range(4):
            part = jnp.dot(inner, vd[:, q * 512 : (q + 1) * 512], preferred_element_type=jnp.float32)
            for s in range(4):
                stage[pl.ds(q * 4 + s, rows, stride=16), :] = part[:, s * 128 : (s + 1) * 128]
        return stage[...].astype(jnp.bfloat16).reshape(PEERS, cap, 16, 128)

    def wait_bytes(buf, start, count, sem):
        pltpu.make_async_copy(buf.at[pl.ds(start, count)], buf.at[pl.ds(start, count)], sem).wait()

    def start_back(o, sem):
        give_back(o, sem).start()
        return sem

    for g in range(GROUPS):
        first = 1 if g == 0 else 0
        wait_bytes(in_buf, g * PEERS + first, PEERS - first, drecv.at[g])
        answers = compute(g)
        if g == 0:
            ret_buf[0] = answers[0]
        ans_buf[pl.ds(g * PEERS, PEERS)] = answers
        lax.fori_loop(g * PEERS + first, (g + 1) * PEERS, lambda o, c, g=g: start_back(o, g), g)
    for g in range(GROUPS):
        first = 1 if g == 0 else 0
        wait_bytes(ret_buf, g * PEERS + first, PEERS - first, arecv.at[g])

    def combine(t, carry):
        total = jnp.zeros((16, 128), jnp.float32)
        weight = jnp.zeros((16, 128), jnp.float32)
        for k in range(TOPK):
            at = slot_at[k, t]
            gate = jnp.full((16, 128), gates[t, k], jnp.float32)
            weight += gate
            total += gate * ret_buf[at // cap, at % cap].astype(jnp.float32)
        total = total / weight
        stage[pl.ds(t * 16, 16), :] = total
        return carry

    lax.fori_loop(0, tok, combine, 0)
    for s in range(16):
        cols = slice(s * 128, (s + 1) * 128)
        mixture = stage[pl.ds(s, tok, stride=16), :]
        out_ref[:, cols] = (resid[:, cols].astype(jnp.float32) + mixture).astype(jnp.bfloat16)
    for g in range(GROUPS):
        first = 1 if g == 0 else 0
        wait_bytes(send_buf, g * PEERS + first, PEERS - first, dsend.at[g])
        wait_bytes(ans_buf, g * PEERS + first, PEERS - first, asend.at[g])

    @pl.when(exp < 8)
    def _():
        wait_for(heads.at[:, pl.ds(0, 15 * 128)], osend)

    @pl.when(exp >= 8)
    def _():
        wait_for(heads, osend)


def tail(attended, hidden, ffn_gain, w_out, slot_tok, slot_at, gates, w_gate, w_up, w_down):
    tok, width = hidden.shape
    ff = w_gate.shape[1]
    n = GROUPS * PEERS
    vmem = pl.BlockSpec(memory_space=pltpu.VMEM)
    anywhere = pl.BlockSpec(memory_space=pl.ANY)
    dma = pltpu.SemaphoreType.DMA
    return pl.pallas_call(
        functools.partial(moe_kernel, CAP),
        out_shape=jax.ShapeDtypeStruct((tok, width), jnp.bfloat16),
        in_specs=[pl.BlockSpec(memory_space=pltpu.SMEM)] * 3 + [vmem] * 3 + [anywhere] * 4,
        out_specs=vmem,
        scratch_shapes=[pltpu.VMEM((n, CAP, 16, 128), jnp.bfloat16)] * 4
        + [
            pltpu.VMEM((width, width), jnp.bfloat16),
            pltpu.VMEM((width, ff), jnp.bfloat16),
            pltpu.VMEM((width, ff), jnp.bfloat16),
            pltpu.VMEM((ff, width), jnp.bfloat16),
            pltpu.VMEM((PEERS * CAP * 16, 128), jnp.float32),
            pltpu.VMEM((PEERS * CAP, width), jnp.bfloat16),
            pltpu.VMEM((tok + 8, 16, 128), jnp.bfloat16),
            pltpu.VMEM((tok, width), jnp.bfloat16),
            pltpu.VMEM((tok, width), jnp.bfloat16),
            dma((4,)), dma, dma, dma((GROUPS,)), dma((GROUPS,)), dma((GROUPS,)), dma((GROUPS,)),
        ],
        compiler_params=pltpu.CompilerParams(
            collective_id=3, has_side_effects=True, vmem_limit_bytes=62 * 1024 * 1024
        ),
        name="tail",
    )(slot_tok, slot_at, gates, attended, hidden, ffn_gain.reshape(1, -1), w_out, w_gate, w_up, w_down)


def on_device(
    hidden_in, attn_gain, w_query, w_key, w_value, q_gain, k_gain, w_out, ffn_gain,
    w_gate, w_up, w_down, expert_ids, gate_weights,
):
    ctx, exp = lax.axis_index("ctx"), lax.axis_index("exp")
    places = ctx * 2048 + (exp // 4) * 512 + jnp.arange(512, dtype=jnp.int32)
    frequency = jnp.exp(jnp.arange(64, dtype=jnp.float32) * (-2.0 * math.log(rope_base) / 128))
    angles = places.astype(jnp.float32)[:, None] * frequency[None, :]
    cosine, sine = jnp.cos(angles), jnp.sin(angles)
    q, kv, slot_tok, slot_at = project(
        hidden_in, attn_gain, w_query, w_key, w_value, q_gain, k_gain,
        jnp.concatenate([cosine, cosine], axis=1), jnp.concatenate([-sine, sine], axis=1), expert_ids,
    )
    attended, w_out_all = flash(q, kv.reshape(2, 16384, 128), w_out)
    return tail(
        attended, hidden_in, ffn_gain, w_out_all.reshape(2048, 2048), slot_tok, slot_at, gate_weights,
        w_gate[0], w_up[0], w_down[0],
    )


def solution(mesh):
    placed = (
        P(("ctx", "exp"), None),
        P(),
        P(None, "exp"),
        P(),
        P(),
        P(),
        P(),
        P("exp", None),
        P(),
        P(("ctx", "exp"), None, None),
        P(("ctx", "exp"), None, None),
        P(("ctx", "exp"), None, None),
        P(("ctx", "exp"), None),
        P(("ctx", "exp"), None),
    )
    return jax.shard_map(
        on_device, mesh=mesh, in_specs=placed, out_specs=P(("ctx", "exp"), None), check_vma=False
    )
```

```python
import functools
import math

import jax
import jax.numpy as jnp
from jax import lax
from jax.experimental import pallas as pl
from jax.experimental.pallas import tpu as pltpu
from jax.sharding import PartitionSpec as P

MESH = pl.DeviceIdType.MESH
TOPK = 8
CAP = 10
GROUPS = 4
PEERS = 32


def my_coords():
    ctx = lax.axis_index("ctx")
    exp = lax.axis_index("exp")
    x = (ctx // 4) * 2 + (exp // 2) % 2
    return x, ctx % 4, exp // 4, exp % 2


def device_at(x, y, z, core):
    return ((x // 2) * 4 + y, z * 4 + (x % 2) * 2 + core)


def offset_parts(o):
    dc, k, dy, dx = o // 64, (o // 16) % 4, (o // 4) % 4, o % 4
    return dx, dy, (k + 8 - dx - dy) % 4, dc


def peer_to(o):
    x, y, z, c = my_coords()
    dx, dy, dz, dc = offset_parts(o)
    return device_at((x + dx) % 4, (y + dy) % 4, (z + dz) % 4, (c + dc) % 2)


def peer_from(o):
    x, y, z, c = my_coords()
    dx, dy, dz, dc = offset_parts(o)
    return device_at((x + 4 - dx) % 4, (y + 4 - dy) % 4, (z + 4 - dz) % 4, (c + 2 - dc) % 2)


def offset_of_expert(e):
    x, y, z, c = my_coords()
    dx = (((e >> 6) & 1) * 2 + ((e >> 1) & 1) + 4 - x) & 3
    dy = ((e >> 4) + 4 - y) & 3
    dz = ((e >> 2) + 4 - z) & 3
    dc = (e + 2 - c) & 1
    return dc * 64 + ((dx + dy + dz) & 3) * 16 + dy * 4 + dx
epsilon = 1e-06
rope_base = 1000000.0


def rms_scale(values, gains):
    return values * lax.rsqrt(jnp.mean(values * values, axis=-1, keepdims=True) + epsilon) * gains


def rope(values, cosine, sine):
    return values * cosine + pltpu.roll(values, 64, 1) * sine


def push(src, dst, ssem, rsem, device):
    pltpu.make_async_remote_copy(
        src_ref=src, dst_ref=dst, send_sem=ssem, recv_sem=rsem,
        device_id=device, device_id_type=MESH,
    ).start()


def wait_for(ref, sem):
    pltpu.make_async_copy(ref, ref, sem).wait()


class Ring:
    def __init__(self, blocks, halves, plus, minus, ssem, rsem, source=None):
        self.own, self.left, self.right = blocks
        self.left_half, self.right_half, self.far_first, self.far_second = halves
        self.plus, self.minus, self.ssem, self.rsem = plus, minus, ssem, rsem
        self.source = self.own if source is None else source

    def start(self):
        push(self.source, self.own, self.ssem.at[0], self.rsem.at[0], self.plus)
        push(self.source, self.own, self.ssem.at[1], self.rsem.at[1], self.minus)

    def forward_left(self):
        wait_for(self.left, self.rsem.at[0])
        push(self.left_half, self.left_half, self.ssem.at[2], self.rsem.at[2], self.plus)

    def forward_right(self):
        wait_for(self.right, self.rsem.at[1])
        push(self.right_half, self.right_half, self.ssem.at[3], self.rsem.at[3], self.minus)

    def finish(self):
        wait_for(self.far_first, self.rsem.at[2])
        wait_for(self.far_second, self.rsem.at[3])

    def drain(self):
        wait_for(self.source, self.ssem.at[0])
        wait_for(self.source, self.ssem.at[1])
        wait_for(self.left_half, self.ssem.at[2])
        wait_for(self.right_half, self.ssem.at[3])


def assign_slots(expert_ids, slot_tok, slot_at):
    sub = lax.broadcasted_iota(jnp.int32, (128, 128), 0)
    lane = lax.broadcasted_iota(jnp.int32, (128, 128), 1)
    before = (sub < lane).astype(jnp.bfloat16)
    ones = jnp.ones((128, 128), jnp.bfloat16)
    offsets = offset_of_expert(expert_ids[...])
    base = jnp.zeros((128, 128), jnp.float32)
    named, ranks = [], []
    for k in range(TOPK):
        match = (sub == offsets[k : k + 1, :]).astype(jnp.float32)
        match_low = match.astype(jnp.bfloat16)
        place = base + jnp.dot(match_low, before, preferred_element_type=jnp.float32)
        rank = jnp.sum(match * place, axis=0, keepdims=True)
        base = base + jnp.dot(match_low, ones, preferred_element_type=jnp.float32)
        named.append(match)
        ranks.append(rank)
    slots = offsets * CAP + jnp.concatenate(ranks, axis=0).astype(jnp.int32)
    slot_at[...] = slots.T
    token = (128 - lane[:8]).astype(jnp.float32).astype(jnp.bfloat16)
    slot_tok[...] = jnp.full(slot_tok.shape, 128, jnp.int32)
    for r in range(CAP):
        chosen = jnp.zeros((128, 128), jnp.float32)
        for k in range(TOPK):
            chosen = chosen + jnp.where(ranks[k] == r, named[k], 0.0)
        found = lax.dot_general(
            token, chosen.astype(jnp.bfloat16), (((1,), (1,)), ((), ())), preferred_element_type=jnp.float32
        )
        slot_tok[r : r + 1, :] = 128 - found[0:1].astype(jnp.int32)


QB = 128
DB = 256
TK = 1024


def attend_kernel(
    hidden_in, attn_gain_in, wq, wk_in, wv_in, q_gain_in, k_gain_in, cosine_in, sine_in, ids_in, w_out,
    heads, w_all, slot_tok, slot_at,
    hidden, attn_gain, wk, wv, q_gain, k_gain, cosine, sine, expert_ids,
    kv, wq_all, normed, kv_stage, q_stage, q_ref, o_ref, m_scr, acc_scr,
    in_sem, own_sem, wq_s, wq_r, n_s, n_r, z_s, z_r, short_s, short_r, long_s, long_r, d_s, d_r, q_s, q_r,
    w_own, a_s, a_r, b_s, b_r, x_s, x_r, w_s, w_r, h_s, h_r,
):
    x, y, z, core = my_coords()
    ctx, exp = lax.axis_index("ctx"), lax.axis_index("exp")
    x_lo = x % 2
    sibling = device_at(x, y, z, 1 - core)
    x_other = (x // 2) * 2 + 1 - x_lo
    x_near = device_at(x_other, y, z, core)
    far_ctx = jnp.where(z < 2, ctx, 7 - ctx)

    loads = [
        pltpu.make_async_copy(src, dst, in_sem.at[i])
        for i, (src, dst) in enumerate(
            [
                (hidden_in, hidden), (attn_gain_in, attn_gain), (wk_in, wk), (wv_in, wv),
                (q_gain_in, q_gain), (k_gain_in, k_gain), (cosine_in, cosine), (sine_in, sine),
                (ids_in, expert_ids),
            ]
        )
    ]
    for load in loads:
        load.start()
    own_wq = pltpu.make_async_copy(wq, wq_all.at[z], own_sem)
    own_wq.start()
    barrier = pltpu.get_barrier_semaphore()

    def greet(device):
        pl.semaphore_signal(barrier, inc=1, device_id=device, device_id_type=MESH)

    def greet_block(e, carry):
        greet((7 - ctx, e))
        pl.when(e != exp)(lambda: greet((ctx, e)))
        return carry

    lax.fori_loop(0, 16, greet_block, 0)
    for d in (1, 3):
        greet(device_at((x + d) % 4, y, z, core))
        greet(device_at(x, (y + d) % 4, z, core))
    mine = x_lo * 2 + core
    loads[0].wait()
    loads[1].wait()
    normed[mine] = rms_scale(hidden[...].astype(jnp.float32), attn_gain[...]).astype(jnp.bfloat16)
    pl.semaphore_wait(barrier, 35)

    def wq_half(zz, half):
        return wq_all.at[zz, pl.ds(half * 1024, 1024)]

    z_left, z_right, z_far = (z + 3) % 4, (z + 1) % 4, (z + 2) % 4
    z_plus, z_minus = device_at(x, y, z_right, core), device_at(x, y, z_left, core)
    wq_ring = Ring(
        (wq_all.at[z], wq_all.at[z_left], wq_all.at[z_right]),
        (wq_half(z_left, 0), wq_half(z_right, 1), wq_half(z_far, 0), wq_half(z_far, 1)),
        z_plus, z_minus, wq_s, wq_r, wq,
    )
    other = (1 - x_lo) * 2 + core
    push(normed.at[mine], normed.at[mine], n_s.at[1], n_r.at[1], x_near)
    push(normed.at[mine], normed.at[mine], n_s.at[0], n_r.at[0], sibling)
    wq_ring.start()

    for load in loads[2:]:
        load.wait()
    here = pl.ds(pl.multiple_of(mine * 128, 128), 128)
    own_normed = normed[mine]
    key_raw = jnp.dot(own_normed, wk[...], preferred_element_type=jnp.float32)
    value_raw = jnp.dot(own_normed, wv[...], preferred_element_type=jnp.float32)
    for g in range(2):
        cols = slice(g * 128, (g + 1) * 128)
        key = rope(rms_scale(key_raw[:, cols], k_gain[...]), cosine[here, :], sine[here, :])
        kv_stage[0, g] = key.astype(jnp.bfloat16)
        kv_stage[1, g] = value_raw[:, cols].astype(jnp.bfloat16)

    def piece(which, zz, cc):
        return kv.at[which, x // 2, y, zz, x_lo, pl.ds(cc * 128, 128)]

    for which in range(2):
        for zz in range(4):
            is_self = (zz == z) & (which == core)
            src = kv_stage.at[which, zz // 2]
            dst = piece(which, z, core)

            @pl.when(is_self)
            def _(src=src, dst=dst):
                pltpu.make_async_copy(src, dst, z_r.at[z * 2 + core]).start()

            @pl.when(jnp.logical_not(is_self))
            def _(src=src, dst=dst, which=which, zz=zz):
                push(src, dst, z_s.at[which * 4 + zz], z_r.at[z * 2 + core], device_at(x, y, zz, which))

    for zz in range(4):
        for cc in range(2):
            wait_for(piece(core, zz, cc), z_r.at[zz * 2 + cc])

    def column(n, zs=None):
        xx = (x + n) % 4
        if zs is None:
            return kv.at[core, xx // 2, y, :, xx % 2]
        return kv.at[core, xx // 2, y, pl.ds(zs * 2, 2), xx % 2]

    short = Ring(
        (column(0), column(3), column(1)),
        (column(3, 0), column(1, 1), column(2, 0), column(2, 1)),
        device_at((x + 1) % 4, y, z, core), device_at((x + 3) % 4, y, z, core), short_s, short_r,
    )
    short.start()
    short.forward_left()
    short.forward_right()
    short.finish()

    def blocks_of(n, which, half=None):
        yy = (y + n) % 4
        return kv.at[which, :, yy] if half is None else kv.at[which, half, yy]

    def mine_of(n, half=None):
        return blocks_of(n, core, half)

    long = Ring(
        (mine_of(0), mine_of(3), mine_of(1)),
        (mine_of(3, 0), mine_of(1, 1), mine_of(2, 0), mine_of(2, 1)),
        device_at(x, (y + 1) % 4, z, core), device_at(x, (y + 3) % 4, z, core), long_s, long_r,
    )

    def share_kv(k, n):
        push(mine_of(n), mine_of(n), d_s.at[k], d_r.at[k], sibling)

    def theirs_kv(k, n):
        wait_for(blocks_of(n, 1 - core), d_r.at[k])

    long.start()
    share_kv(0, 0)
    wq_ring.forward_left()
    wq_ring.forward_right()
    wait_for(normed.at[other], n_r.at[1])
    push(normed.at[other], normed.at[other], n_s.at[2], n_r.at[2], sibling)
    assign_slots(expert_ids, slot_tok, slot_at)
    wait_for(normed.at[x_lo * 2 + 1 - core], n_r.at[0])
    own_wq.wait()
    wq_ring.finish()
    wait_for(normed.at[(1 - x_lo) * 2 + 1 - core], n_r.at[2])

    def q_rows(zz):
        return q_ref.at[zz // 2, pl.ds((zz % 2) * 512, 512)]

    tokens = normed[...].reshape(512, 2048)
    for pair in range(2):
        weights = jnp.concatenate([wq_all[2 * pair], wq_all[2 * pair + 1]], axis=1)
        raw = jnp.dot(tokens, weights, preferred_element_type=jnp.float32)
        for k in range(2):
            zz = 2 * pair + k
            query = rope(rms_scale(raw[:, k * 128 : (k + 1) * 128], q_gain[...]), cosine[...], sine[...])
            q_stage[zz] = query.astype(jnp.bfloat16)
            is_self = (zz == z) & (z < 2)

            @pl.when(is_self)
            def _(zz=zz):
                pltpu.make_async_copy(q_stage.at[zz], q_rows(z), q_r.at[z]).start()

            @pl.when(jnp.logical_not(is_self))
            def _(zz=zz):
                push(q_stage.at[zz], q_rows(z), q_s.at[zz], q_r.at[z], (far_ctx, zz * 4 + x_lo * 2 + core))

    def shard(dz, xl, cc):
        return w_all.at[(z + dz) % 4, xl, cc]

    def part(dz, xl, half):
        return w_all.at[(z + dz) % 4, xl, core, pl.ds(half * 64, 64)]

    ring = Ring(
        (shard(0, x_lo, core), shard(3, x_lo, core), shard(1, x_lo, core)),
        (part(3, x_lo, 0), part(1, x_lo, 1), part(2, x_lo, 0), part(2, x_lo, 1)),
        z_plus, z_minus, a_s, a_r, w_out,
    )
    order = [(0, 0), (3, 0), (1, 0), (2, 0), (0, 1), (3, 1), (1, 1), (2, 1)]

    def share(n, src=None):
        dz, flip = order[n]
        xl = 1 - x_lo if flip else x_lo
        push(shard(dz, xl, core) if src is None else src, shard(dz, xl, core), w_s.at[n], w_r.at[n], sibling)

    own = pltpu.make_async_copy(w_out, shard(0, x_lo, core), w_own)
    own.start()
    ring.start()
    push(w_out, shard(0, x_lo, core), x_s.at[0], x_r.at[0], x_near)
    share(0, w_out)

    def stage_1():
        long.forward_left()
        long.forward_right()
        share_kv(1, 3)
        share_kv(2, 1)
        ring.forward_left()
        ring.forward_right()
        share(1)
        share(2)
        theirs = shard(0, 1 - x_lo, core)
        wait_for(theirs, x_r.at[0])
        push(theirs, theirs, b_s.at[0], b_r.at[0], z_plus)
        push(theirs, theirs, b_s.at[1], b_r.at[1], z_minus)
        share(4)
        theirs_kv(1, 3)

    def stage_2():
        ring.finish()
        push(shard(2, x_lo, core), shard(2, x_lo, core), x_s.at[1], x_r.at[1], x_near)
        share(3)
        theirs_kv(2, 1)

    def stage_3():
        long.finish()
        share_kv(3, 2)
        theirs_kv(3, 2)

    def stage_4():
        wait_for(shard(3, 1 - x_lo, core), b_r.at[0])
        share(5)
        wait_for(shard(1, 1 - x_lo, core), b_r.at[1])
        share(6)
        wait_for(shard(2, 1 - x_lo, core), x_r.at[1])
        share(7)

    scale = math.log2(math.e) / math.sqrt(128)

    def step(q, k, v, m_prev, acc, first_row):
        s = lax.dot_general(q, k, (((1,), (1,)), ((), ())), preferred_element_type=jnp.float32)
        if first_row is not None:
            row = lax.broadcasted_iota(jnp.int32, s.shape, 0) + first_row
            col = lax.broadcasted_iota(jnp.int32, s.shape, 1)
            s = jnp.where(col <= row, s, -1e30)
        m_new = jnp.maximum(m_prev, jnp.max(s, axis=1, keepdims=True))
        alpha = jnp.exp2((m_prev - m_new) * scale)
        shift = (m_new * scale)[:, :1]
        p = jnp.exp2(s * scale - shift).astype(jnp.bfloat16)
        joined = jnp.concatenate([v, jnp.ones_like(v)], axis=1)
        pv = jnp.dot(p, joined, preferred_element_type=jnp.float32)
        return m_new, acc * jnp.concatenate([alpha, alpha], axis=1) + pv

    m_scr[...] = jnp.full_like(m_scr, -1e30)
    acc_scr[...] = jnp.zeros_like(acc_scr)
    last = (2 * ctx, 15 - 2 * ctx)

    def tile_of(t):
        at = (t // 8, (t // 2) % 4, pl.ds((t % 2) * 2, 2))
        return kv[(0, *at)].reshape(TK, 128), kv[(1, *at)].reshape(TK, 128)

    def full(half, t):
        k, v = tile_of(t)
        for b in range(1024 // QB):
            rows = pl.ds(b * QB, QB)
            m, a = step(q_ref[half, rows, :], k, v, m_scr[half, rows, :], acc_scr[half, rows, :], None)
            m_scr[half, rows, :] = m
            acc_scr[half, rows, :] = a

    for zz in range(4):
        wait_for(q_rows(zz), q_r.at[zz])
    theirs_kv(0, 0)

    def visit(s, carry):
        pl.when(s == 1)(stage_1)
        pl.when(s == 2)(stage_2)
        pl.when(s == 3)(stage_3)
        n = jnp.where(s == 1, 3, jnp.where(s == 2, 1, jnp.where(s == 3, 2, 0)))
        yy = (y + n) % 4

        def one(u, carry):
            t = ((u // 4) * 4 + yy) * 2 + (u // 2) % 2
            half = u % 2
            pl.when(t < jnp.where(half == 0, last[0], last[1]))(functools.partial(full, half, t))
            return carry

        return lax.fori_loop(0, 8, one, carry)

    lax.fori_loop(0, 4, visit, 0)
    stage_4()
    my_columns = pl.ds(pl.multiple_of(exp * 128, 128), 128)
    for half in range(2):
        k, v = tile_of(last[half])
        for b in range(1024 // DB):
            rows = pl.ds(b * DB, DB)
            seen = (b + 1) * DB
            m, a = step(
                q_ref[half, rows, :], k[:seen], v[:seen], m_scr[half, rows, :], acc_scr[half, rows, :], b * DB
            )
            o_ref[half, rows, :] = (a[:, :128] / a[:, 128:]).astype(jnp.bfloat16)
            for i in range(2):
                e = half * 8 + b * 2 + i
                src = o_ref.at[half, pl.ds(b * DB + i * 128, 128)]
                dst = heads.at[:, my_columns]
                if half:
                    push(src, dst, h_s, h_r, (7 - ctx, e))
                else:
                    pl.when(e == exp)(lambda src=src: pltpu.make_async_copy(src, dst, h_r).start())
                    pl.when(e != exp)(lambda src=src, e=e: push(src, dst, h_s, h_r, (ctx, e)))

    for n, (dz, flip) in enumerate(order):
        wait_for(shard(dz, 1 - x_lo if flip else x_lo, 1 - core), w_r.at[n])
        wait_for(shard(dz, 1 - x_lo if flip else x_lo, core), w_s.at[n])
    own.wait()
    ring.drain()
    for sem in (x_s.at[0], x_s.at[1], b_s.at[0], b_s.at[1]):
        wait_for(w_out, sem)
    long.drain()
    for k, n in enumerate((0, 3, 1, 2)):
        wait_for(mine_of(n), d_s.at[k])
    wq_ring.drain()
    short.drain()
    wait_for(normed.at[mine], n_s.at[0])
    wait_for(normed.at[mine], n_s.at[1])
    wait_for(normed.at[other], n_s.at[2])
    for zz in range(4):

        @pl.when(jnp.logical_not((zz == z) & (z < 2)))
        def _(zz=zz):
            wait_for(q_stage.at[zz], q_s.at[zz])

        for which in range(2):

            @pl.when(jnp.logical_not((zz == z) & (which == core)))
            def _(zz=zz, which=which):
                wait_for(kv_stage.at[which, zz // 2], z_s.at[which * 4 + zz])

    wait_for(heads, h_r)

    @pl.when(exp < 8)
    def _():
        wait_for(heads.at[:, pl.ds(0, 15 * 128)], h_s)

    @pl.when(exp >= 8)
    def _():
        wait_for(heads, h_s)


def attend(hidden, attn_gain, wq, wk, wv, q_gain, k_gain, cosine, sine, ids, w_out):
    vmem = pl.BlockSpec(memory_space=pltpu.VMEM)
    anywhere = pl.BlockSpec(memory_space=pl.ANY)
    dma = pltpu.SemaphoreType.DMA
    low, f32 = jnp.bfloat16, jnp.float32
    return pl.pallas_call(
        attend_kernel,
        out_shape=(
            jax.ShapeDtypeStruct((128, 2048), low),
            jax.ShapeDtypeStruct((4, 2, 2, 128, 2048), low),
            jax.ShapeDtypeStruct((16, 128), jnp.int32),
            jax.ShapeDtypeStruct((128, TOPK), jnp.int32),
        ),
        in_specs=[anywhere] * 11,
        out_specs=(anywhere, anywhere, vmem, vmem),
        scratch_shapes=[
            pltpu.VMEM((128, 2048), low),
            pltpu.VMEM((1, 2048), f32),
            pltpu.VMEM((2048, 256), low),
            pltpu.VMEM((2048, 256), low),
            pltpu.VMEM((1, 128), f32),
            pltpu.VMEM((1, 128), f32),
            pltpu.VMEM((512, 128), f32),
            pltpu.VMEM((512, 128), f32),
            pltpu.VMEM((TOPK, 128), jnp.int32),
            pltpu.VMEM((2, 2, 4, 4, 2, 256, 128), low),
            pltpu.VMEM((4, 2048, 128), low),
            pltpu.VMEM((4, 128, 2048), low),
            pltpu.VMEM((2, 2, 128, 128), low),
            pltpu.VMEM((4, 512, 128), low),
            pltpu.VMEM((2, 1024, 128), low),
            pltpu.VMEM((2, 1024, 128), low),
            pltpu.VMEM((2, 1024, 128), f32),
            pltpu.VMEM((2, 1024, 256), f32),
            dma((9,)), dma, dma((4,)), dma((4,)), dma((3,)), dma((3,)), dma((8,)), dma((8,)),
            dma((4,)), dma((4,)), dma((4,)), dma((4,)), dma((4,)), dma((4,)), dma((4,)), dma((4,)),
            dma, dma((4,)), dma((4,)), dma((2,)), dma((2,)), dma((2,)), dma((2,)), dma((8,)), dma((8,)), dma, dma,
        ],
        compiler_params=pltpu.CompilerParams(
            collective_id=1, has_side_effects=True, vmem_limit_bytes=60 * 1024 * 1024
        ),
        name="attend",
    )(
        hidden, attn_gain.reshape(1, -1), wq, wk, wv, q_gain.reshape(1, -1), k_gain.reshape(1, -1),
        cosine, sine, ids, w_out,
    )


def moe_kernel(
    cap,
    slot_tok,
    heads_in, hidden_in, ffn_gain_in, slot_in, gates_in, w_out, w_gate, w_up, w_down,
    out_ref,
    send_buf, in_buf, ans_buf, ret_buf, vo, vg, vu, vd, stage, xrows, x_tiles, resid, acc,
    heads, hidden, ffn_gain, slot_at, gates,
    wsem, insem, dsend, drecv, asend, arecv,
):
    tok = hidden.shape[0]
    loads = [
        pltpu.make_async_copy(src, dst, insem.at[i])
        for i, (src, dst) in enumerate(
            [(heads_in, heads), (w_out, vo), (hidden_in, hidden), (ffn_gain_in, ffn_gain),
             (slot_in, slot_at), (gates_in, gates)]
        )
    ]
    for load in loads:
        load.start()
    copies = [
        pltpu.make_async_copy(w_gate, vg, wsem.at[0]),
        pltpu.make_async_copy(w_up, vu, wsem.at[1]),
        pltpu.make_async_copy(w_down, vd, wsem.at[2]),
    ]
    for copy in copies:
        copy.start()
    barrier = pltpu.get_barrier_semaphore()

    def greet(o, carry):
        pl.semaphore_signal(barrier, inc=1, device_id=peer_to(o), device_id_type=MESH)
        return carry

    lax.fori_loop(1, GROUPS * PEERS, greet, 0)
    x_tiles[tok:] = jnp.zeros((8, 16, 128), jnp.bfloat16)
    for load in loads:
        load.wait()
    projected = jnp.dot(heads[...], vo[...], preferred_element_type=jnp.float32)
    summed = (hidden[...].astype(jnp.float32) + projected).astype(jnp.bfloat16)
    resid[...] = summed
    normed = rms_scale(summed.astype(jnp.float32), ffn_gain[...])
    for s in range(16):
        stage[pl.ds(s, tok, stride=16), :] = normed[:, s * 128 : (s + 1) * 128]
    x_tiles[:tok] = stage[: tok * 16].astype(jnp.bfloat16).reshape(tok, 16, 128)

    for r in range(cap):
        in_buf[0, r] = x_tiles[slot_tok[r, 0]]
    pl.semaphore_wait(barrier, GROUPS * PEERS - 1)

    def fill(o, carry):
        for r in range(cap):
            send_buf[o, r] = x_tiles[slot_tok[r, o]]
        return carry


    def dispatch(o, sem):
        return pltpu.make_async_remote_copy(
            src_ref=send_buf.at[o], dst_ref=in_buf.at[o],
            send_sem=dsend.at[sem], recv_sem=drecv.at[sem],
            device_id=peer_to(o), device_id_type=MESH,
        )

    def give_back(o, sem):
        return pltpu.make_async_remote_copy(
            src_ref=ans_buf.at[o], dst_ref=ret_buf.at[o],
            send_sem=asend.at[sem], recv_sem=arecv.at[sem],
            device_id=peer_from(o), device_id_type=MESH,
        )

    def send(o, carry):
        fill(o, 0)
        dispatch(o, o // PEERS).start()
        return carry

    lax.fori_loop(1, GROUPS * PEERS, send, 0)
    for copy in copies[:3]:
        copy.wait()
    rows = PEERS * cap

    def rows_of(buf, g):
        block = buf[pl.ds(g * PEERS, PEERS)]
        stage[...] = block.astype(jnp.float32).reshape(rows * 16, 128)
        for s in range(16):
            xrows[:, s * 128 : (s + 1) * 128] = stage[pl.ds(s, rows, stride=16), :].astype(jnp.bfloat16)
        return xrows[...]

    def compute(g):
        rows_in = rows_of(in_buf, g)
        gate = jnp.dot(rows_in, vg[...], preferred_element_type=jnp.float32)
        up = jnp.dot(rows_in, vu[...], preferred_element_type=jnp.float32)
        inner = (gate / (1.0 + jnp.exp(-gate)) * up).astype(jnp.bfloat16)
        for q in range(4):
            part = jnp.dot(inner, vd[:, q * 512 : (q + 1) * 512], preferred_element_type=jnp.float32)
            for s in range(4):
                stage[pl.ds(q * 4 + s, rows, stride=16), :] = part[:, s * 128 : (s + 1) * 128]
        return stage[...].astype(jnp.bfloat16).reshape(PEERS, cap, 16, 128)

    def wait_bytes(buf, start, count, sem):
        pltpu.make_async_copy(buf.at[pl.ds(start, count)], buf.at[pl.ds(start, count)], sem).wait()

    def start_back(o, sem):
        give_back(o, sem).start()
        return sem

    for g in range(GROUPS):
        first = 1 if g == 0 else 0
        wait_bytes(in_buf, g * PEERS + first, PEERS - first, drecv.at[g])
        answers = compute(g)
        if g == 0:
            ret_buf[0] = answers[0]
        ans_buf[pl.ds(g * PEERS, PEERS)] = answers
        lax.fori_loop(g * PEERS + first, (g + 1) * PEERS, lambda o, c, g=g: start_back(o, g), g)
    acc[...] = resid[...].astype(jnp.float32)
    weights = gates[...]
    shares = weights / jnp.sum(weights, axis=1, keepdims=True)
    at = slot_at[...]
    for g in range(GROUPS):
        slot = lax.broadcasted_iota(jnp.int32, (tok, rows), 1) + g * rows
        mix = jnp.zeros((tok, rows), jnp.float32)
        for k in range(TOPK):
            mix = mix + jnp.where(at[:, k : k + 1] == slot, shares[:, k : k + 1], 0.0)
        high = mix.astype(jnp.bfloat16)
        low = (mix - high.astype(jnp.float32)).astype(jnp.bfloat16)
        first = 1 if g == 0 else 0
        wait_bytes(ret_buf, g * PEERS + first, PEERS - first, arecv.at[g])
        back = rows_of(ret_buf, g)
        acc[...] += jnp.dot(high, back, preferred_element_type=jnp.float32) + jnp.dot(
            low, back, preferred_element_type=jnp.float32
        )
    out_ref[...] = acc[...].astype(jnp.bfloat16)
    for g in range(GROUPS):
        first = 1 if g == 0 else 0
        wait_bytes(send_buf, g * PEERS + first, PEERS - first, dsend.at[g])
        wait_bytes(ans_buf, g * PEERS + first, PEERS - first, asend.at[g])


def tail(heads, hidden, ffn_gain, w_out, slot_tok, slot_at, gates, w_gate, w_up, w_down):
    tok, width = hidden.shape
    ff = w_gate.shape[1]
    n = GROUPS * PEERS
    anywhere = pl.BlockSpec(memory_space=pl.ANY)
    dma = pltpu.SemaphoreType.DMA
    low, f32 = jnp.bfloat16, jnp.float32
    return pl.pallas_call(
        functools.partial(moe_kernel, CAP),
        out_shape=jax.ShapeDtypeStruct((tok, width), low),
        in_specs=[pl.BlockSpec(memory_space=pltpu.SMEM)] + [anywhere] * 9,
        out_specs=pl.BlockSpec(memory_space=pltpu.VMEM),
        scratch_shapes=[pltpu.VMEM((n, CAP, 16, 128), low)] * 4
        + [
            pltpu.VMEM((width, width), low),
            pltpu.VMEM((width, ff), low),
            pltpu.VMEM((width, ff), low),
            pltpu.VMEM((ff, width), low),
            pltpu.VMEM((PEERS * CAP * 16, 128), f32),
            pltpu.VMEM((PEERS * CAP, width), low),
            pltpu.VMEM((tok + 8, 16, 128), low),
            pltpu.VMEM((tok, width), low),
            pltpu.VMEM((tok, width), f32),
            pltpu.VMEM((tok, width), low),
            pltpu.VMEM((tok, width), low),
            pltpu.VMEM((1, width), f32),
            pltpu.VMEM((tok, TOPK), jnp.int32),
            pltpu.VMEM((tok, TOPK), f32),
            dma((3,)), dma((6,)), dma((GROUPS,)), dma((GROUPS,)), dma((GROUPS,)), dma((GROUPS,)),
        ],
        compiler_params=pltpu.CompilerParams(
            collective_id=3, has_side_effects=True, vmem_limit_bytes=62 * 1024 * 1024
        ),
        name="tail",
    )(slot_tok, heads, hidden, ffn_gain.reshape(1, -1), slot_at, gates, w_out, w_gate, w_up, w_down)


def on_device(
    hidden_in, attn_gain, w_query, w_key, w_value, q_gain, k_gain, w_out, ffn_gain,
    w_gate, w_up, w_down, expert_ids, gate_weights,
):
    ctx, exp = lax.axis_index("ctx"), lax.axis_index("exp")
    places = ctx * 2048 + (exp // 4) * 512 + jnp.arange(512, dtype=jnp.int32)
    frequency = jnp.exp(jnp.arange(64, dtype=jnp.float32) * (-2.0 * math.log(rope_base) / 128))
    angles = places.astype(jnp.float32)[:, None] * frequency[None, :]
    cosine, sine = jnp.cos(angles), jnp.sin(angles)
    heads, w_out_all, slot_tok, slot_at = attend(
        hidden_in, attn_gain, w_query, w_key, w_value, q_gain, k_gain,
        jnp.concatenate([cosine, cosine], axis=1), jnp.concatenate([-sine, sine], axis=1), expert_ids.T, w_out,
    )
    return tail(
        heads, hidden_in, ffn_gain, w_out_all.reshape(2048, 2048), slot_tok, slot_at, gate_weights,
        w_gate[0], w_up[0], w_down[0],
    )


def solution(mesh):
    placed = (
        P(("ctx", "exp"), None),
        P(),
        P(None, "exp"),
        P(),
        P(),
        P(),
        P(),
        P("exp", None),
        P(),
        P(("ctx", "exp"), None, None),
        P(("ctx", "exp"), None, None),
        P(("ctx", "exp"), None, None),
        P(("ctx", "exp"), None),
        P(("ctx", "exp"), None),
    )
    return jax.shard_map(
        on_device, mesh=mesh, in_specs=placed, out_specs=P(("ctx", "exp"), None), check_vma=False
    )
```

```python
import functools
import math

import jax
import jax.numpy as jnp
from jax import lax
from jax.experimental import pallas as pl
from jax.experimental.pallas import tpu as pltpu
from jax.sharding import PartitionSpec as P

MESH = pl.DeviceIdType.MESH
TOPK = 8
CAP = 10
GROUPS = 4
PEERS = 32


def my_coords():
    ctx = lax.axis_index("ctx")
    exp = lax.axis_index("exp")
    x = (ctx // 4) * 2 + (exp // 2) % 2
    return x, ctx % 4, exp // 4, exp % 2


def device_at(x, y, z, core):
    return ((x // 2) * 4 + y, z * 4 + (x % 2) * 2 + core)


def offset_parts(o):
    dc, k, dy, dx = o // 64, (o // 16) % 4, (o // 4) % 4, o % 4
    return dx, dy, (k + 8 - dx - dy) % 4, dc


def peer_to(o):
    x, y, z, c = my_coords()
    dx, dy, dz, dc = offset_parts(o)
    return device_at((x + dx) % 4, (y + dy) % 4, (z + dz) % 4, (c + dc) % 2)


def peer_from(o):
    x, y, z, c = my_coords()
    dx, dy, dz, dc = offset_parts(o)
    return device_at((x + 4 - dx) % 4, (y + 4 - dy) % 4, (z + 4 - dz) % 4, (c + 2 - dc) % 2)


def offset_of_expert(e):
    x, y, z, c = my_coords()
    dx = (((e >> 6) & 1) * 2 + ((e >> 1) & 1) + 4 - x) & 3
    dy = ((e >> 4) + 4 - y) & 3
    dz = ((e >> 2) + 4 - z) & 3
    dc = (e + 2 - c) & 1
    return dc * 64 + ((dx + dy + dz) & 3) * 16 + dy * 4 + dx
epsilon = 1e-06
rope_base = 1000000.0


def rms_scale(values, gains):
    return values * lax.rsqrt(jnp.mean(values * values, axis=-1, keepdims=True) + epsilon) * gains


def rope(values, cosine, sine):
    return values * cosine + pltpu.roll(values, 64, 1) * sine


def push(src, dst, ssem, rsem, device):
    pltpu.make_async_remote_copy(
        src_ref=src, dst_ref=dst, send_sem=ssem, recv_sem=rsem,
        device_id=device, device_id_type=MESH,
    ).start()


def wait_for(ref, sem):
    pltpu.make_async_copy(ref, ref, sem).wait()


class Ring:
    def __init__(self, blocks, halves, plus, minus, ssem, rsem, source=None, base=0):
        self.own, self.left, self.right = blocks
        self.left_half, self.right_half, self.far_first, self.far_second = halves
        self.plus, self.minus = plus, minus
        self.ssem = [ssem.at[base + i] for i in range(4)]
        self.rsem = [rsem.at[base + i] for i in range(4)]
        self.source = self.own if source is None else source

    def start(self):
        push(self.source, self.own, self.ssem[0], self.rsem[0], self.plus)
        push(self.source, self.own, self.ssem[1], self.rsem[1], self.minus)

    def forward_left(self):
        wait_for(self.left, self.rsem[0])
        push(self.left_half, self.left_half, self.ssem[2], self.rsem[2], self.plus)

    def forward_right(self):
        wait_for(self.right, self.rsem[1])
        push(self.right_half, self.right_half, self.ssem[3], self.rsem[3], self.minus)

    def finish(self):
        wait_for(self.far_first, self.rsem[2])
        wait_for(self.far_second, self.rsem[3])

    def drain(self):
        wait_for(self.source, self.ssem[0])
        wait_for(self.source, self.ssem[1])
        wait_for(self.left_half, self.ssem[2])
        wait_for(self.right_half, self.ssem[3])


def assign_slots(expert_ids, slot_tok, slot_at):
    sub = lax.broadcasted_iota(jnp.int32, (128, 128), 0)
    lane = lax.broadcasted_iota(jnp.int32, (128, 128), 1)
    before = (sub < lane).astype(jnp.bfloat16)
    ones = jnp.ones((128, 128), jnp.bfloat16)
    offsets = offset_of_expert(expert_ids[...])
    base = jnp.zeros((128, 128), jnp.float32)
    named, ranks = [], []
    for k in range(TOPK):
        match = (sub == offsets[k : k + 1, :]).astype(jnp.float32)
        match_low = match.astype(jnp.bfloat16)
        place = base + jnp.dot(match_low, before, preferred_element_type=jnp.float32)
        rank = jnp.sum(match * place, axis=0, keepdims=True)
        base = base + jnp.dot(match_low, ones, preferred_element_type=jnp.float32)
        named.append(match)
        ranks.append(rank)
    slots = offsets * CAP + jnp.concatenate(ranks, axis=0).astype(jnp.int32)
    slot_at[...] = slots.T
    token = (128 - lane[:8]).astype(jnp.float32).astype(jnp.bfloat16)
    slot_tok[...] = jnp.full(slot_tok.shape, 128, jnp.int32)
    for r in range(CAP):
        chosen = jnp.zeros((128, 128), jnp.float32)
        for k in range(TOPK):
            chosen = chosen + jnp.where(ranks[k] == r, named[k], 0.0)
        found = lax.dot_general(
            token, chosen.astype(jnp.bfloat16), (((1,), (1,)), ((), ())), preferred_element_type=jnp.float32
        )
        slot_tok[r : r + 1, :] = 128 - found[0:1].astype(jnp.int32)


QB = 128
DB = 256
TK = 1024


def attend_kernel(
    hidden_in, attn_gain_in, wq, wk_in, wv_in, q_gain_in, k_gain_in, cosine_in, sine_in, ids_in, w_out,
    heads, w_all, slot_tok, slot_at,
    hidden, attn_gain, wk, wv, q_gain, k_gain, cosine, sine, expert_ids,
    kv, wq_all, normed, kv_stage, q_stage, q_ref, o_ref, m_scr, acc_scr,
    in_sem, own_sem, wq_s, wq_r, n_s, n_r, z_s, z_r, short_s, short_r, long_s, long_r, d_s, d_r, q_s, q_r,
    w_own, a_s, a_r, b_s, b_r, x_s, x_r, w_s, w_r, h_s, h_r,
):
    x, y, z, core = my_coords()
    ctx, exp = lax.axis_index("ctx"), lax.axis_index("exp")
    x_lo = x % 2
    sibling = device_at(x, y, z, 1 - core)
    x_other = (x // 2) * 2 + 1 - x_lo
    x_near = device_at(x_other, y, z, core)

    loads = [
        pltpu.make_async_copy(src, dst, in_sem.at[i])
        for i, (src, dst) in enumerate(
            [
                (hidden_in, hidden), (attn_gain_in, attn_gain), (wk_in, wk), (wv_in, wv),
                (q_gain_in, q_gain), (k_gain_in, k_gain), (cosine_in, cosine), (sine_in, sine),
                (ids_in, expert_ids),
            ]
        )
    ]
    for load in loads:
        load.start()
    own_wq = pltpu.make_async_copy(wq, wq_all.at[z], own_sem)
    own_wq.start()
    barrier = pltpu.get_barrier_semaphore()

    def greet(device):
        pl.semaphore_signal(barrier, inc=1, device_id=device, device_id_type=MESH)

    def greet_block(e, carry):
        greet((7 - ctx, e))
        pl.when(e != exp)(lambda: greet((ctx, e)))
        return carry

    lax.fori_loop(0, 16, greet_block, 0)
    for d in (1, 3):
        greet(device_at((x + d) % 4, y, z, core))
        greet(device_at(x, (y + d) % 4, z, core))
    mine = x_lo * 2 + core
    loads[0].wait()
    loads[1].wait()
    normed[mine] = rms_scale(hidden[...].astype(jnp.float32), attn_gain[...]).astype(jnp.bfloat16)
    pl.semaphore_wait(barrier, 35)

    def wq_half(zz, half):
        return wq_all.at[zz, pl.ds(half * 1024, 1024)]

    z_left, z_right, z_far = (z + 3) % 4, (z + 1) % 4, (z + 2) % 4
    z_plus, z_minus = device_at(x, y, z_right, core), device_at(x, y, z_left, core)
    wq_ring = Ring(
        (wq_all.at[z], wq_all.at[z_left], wq_all.at[z_right]),
        (wq_half(z_left, 0), wq_half(z_right, 1), wq_half(z_far, 0), wq_half(z_far, 1)),
        z_plus, z_minus, wq_s, wq_r, wq,
    )
    other = (1 - x_lo) * 2 + core
    push(normed.at[mine], normed.at[mine], n_s.at[1], n_r.at[1], x_near)
    push(normed.at[mine], normed.at[mine], n_s.at[0], n_r.at[0], sibling)

    for load in loads[2:]:
        load.wait()
    here = pl.ds(pl.multiple_of(mine * 128, 128), 128)
    own_normed = normed[mine]
    key_raw = jnp.dot(own_normed, wk[...], preferred_element_type=jnp.float32)
    value_raw = jnp.dot(own_normed, wv[...], preferred_element_type=jnp.float32)
    for g in range(2):
        cols = slice(g * 128, (g + 1) * 128)
        key = rope(rms_scale(key_raw[:, cols], k_gain[...]), cosine[here, :], sine[here, :])
        kv_stage[0, g] = key.astype(jnp.bfloat16)
        kv_stage[1, g] = value_raw[:, cols].astype(jnp.bfloat16)

    def piece(which, zz, cc):
        return kv.at[which, x // 2, y, zz, x_lo, pl.ds(cc * 128, 128)]

    for which in range(2):
        for zz in range(4):
            is_self = (zz == z) & (which == core)
            src = kv_stage.at[which, zz // 2]
            dst = piece(which, z, core)

            @pl.when(is_self)
            def _(src=src, dst=dst):
                pltpu.make_async_copy(src, dst, z_r.at[z * 2 + core]).start()

            @pl.when(jnp.logical_not(is_self))
            def _(src=src, dst=dst, which=which, zz=zz):
                push(src, dst, z_s.at[which * 4 + zz], z_r.at[z * 2 + core], device_at(x, y, zz, which))

    wq_ring.start()
    for zz in range(4):
        for cc in range(2):
            wait_for(piece(core, zz, cc), z_r.at[zz * 2 + cc])

    def column(n, zs=None):
        xx = (x + n) % 4
        if zs is None:
            return kv.at[core, xx // 2, y, :, xx % 2]
        return kv.at[core, xx // 2, y, pl.ds(zs * 2, 2), xx % 2]

    short = Ring(
        (column(0), column(3), column(1)),
        (column(3, 0), column(1, 1), column(2, 0), column(2, 1)),
        device_at((x + 1) % 4, y, z, core), device_at((x + 3) % 4, y, z, core), short_s, short_r,
    )
    def column_ring(n):
        xx = (x + n) % 4

        def at(dy, half=None):
            yy = (y + dy) % 4
            if half is None:
                return kv.at[core, xx // 2, yy, :, xx % 2]
            return kv.at[core, xx // 2, yy, pl.ds(half * 2, 2), xx % 2]

        return Ring(
            (at(0), at(3), at(1)), (at(3, 0), at(1, 1), at(2, 0), at(2, 1)),
            device_at(x, (y + 1) % 4, z, core), device_at(x, (y + 3) % 4, z, core), long_s, long_r, None, 4 * n,
        )

    columns = [column_ring(n) for n in range(4)]
    short.start()
    columns[0].start()
    short.forward_left()
    columns[3].start()
    short.forward_right()
    columns[1].start()
    wq_ring.forward_left()
    wq_ring.forward_right()
    short.finish()
    columns[2].start()
    columns[0].forward_left()
    columns[0].forward_right()

    def blocks_of(n, which, half=None):
        yy = (y + n) % 4
        return kv.at[which, :, yy] if half is None else kv.at[which, half, yy]

    def mine_of(n, half=None):
        return blocks_of(n, core, half)

    def share_kv(k, n):
        push(mine_of(n), mine_of(n), d_s.at[k], d_r.at[k], sibling)

    def theirs_kv(k, n):
        wait_for(blocks_of(n, 1 - core), d_r.at[k])

    share_kv(0, 0)
    wait_for(normed.at[other], n_r.at[1])
    push(normed.at[other], normed.at[other], n_s.at[2], n_r.at[2], sibling)
    wait_for(normed.at[x_lo * 2 + 1 - core], n_r.at[0])
    own_wq.wait()
    wq_ring.finish()

    def q_rows(xt, zz):
        return q_ref.at[xt, pl.ds(zz * 256, 256)]

    def query_part(xt):
        tokens = normed[pl.ds(xt * 2, 2)].reshape(256, 2048)
        at = pl.ds(pl.multiple_of(xt * 256, 256), 256)
        cos, sin = cosine[at, :], sine[at, :]
        block = jnp.where(xt == 0, ctx, 7 - ctx)
        for pair in range(2):
            weights = jnp.concatenate([wq_all[2 * pair], wq_all[2 * pair + 1]], axis=1)
            raw = jnp.dot(tokens, weights, preferred_element_type=jnp.float32)
            for k in range(2):
                zz = 2 * pair + k
                query = rope(rms_scale(raw[:, k * 128 : (k + 1) * 128], q_gain[...]), cos, sin)
                q_stage[xt, zz] = query.astype(jnp.bfloat16)
                is_self = (zz == z) & (xt == 0)

                @pl.when(is_self)
                def _(zz=zz):
                    pltpu.make_async_copy(q_stage.at[xt, zz], q_rows(xt, z), q_r.at[xt * 4 + z]).start()

                @pl.when(jnp.logical_not(is_self))
                def _(zz=zz):
                    push(
                        q_stage.at[xt, zz], q_rows(xt, z), q_s.at[xt * 4 + zz], q_r.at[xt * 4 + z],
                        (block, zz * 4 + x_lo * 2 + core),
                    )

    query_part(x_lo)
    wait_for(normed.at[(1 - x_lo) * 2 + 1 - core], n_r.at[2])
    query_part(1 - x_lo)

    def shard(dz, xl, cc):
        return w_all.at[(z + dz) % 4, xl, cc]

    def part(dz, xl, half):
        return w_all.at[(z + dz) % 4, xl, core, pl.ds(half * 64, 64)]

    ring = Ring(
        (shard(0, x_lo, core), shard(3, x_lo, core), shard(1, x_lo, core)),
        (part(3, x_lo, 0), part(1, x_lo, 1), part(2, x_lo, 0), part(2, x_lo, 1)),
        z_plus, z_minus, a_s, a_r, w_out,
    )
    order = [(0, 0), (3, 0), (1, 0), (2, 0), (0, 1), (3, 1), (1, 1), (2, 1)]

    def share(n, src=None):
        dz, flip = order[n]
        xl = 1 - x_lo if flip else x_lo
        push(shard(dz, xl, core) if src is None else src, shard(dz, xl, core), w_s.at[n], w_r.at[n], sibling)

    own = pltpu.make_async_copy(w_out, shard(0, x_lo, core), w_own)
    own.start()
    ring.start()
    push(w_out, shard(0, x_lo, core), x_s.at[0], x_r.at[0], x_near)
    share(0, w_out)

    def kv_forward():
        for n in (3, 1):
            columns[n].forward_left()
            columns[n].forward_right()

    def kv_forward_last():
        columns[2].forward_left()
        share_kv(1, 3)
        columns[2].forward_right()
        share_kv(2, 1)

    def kv_left():
        theirs_kv(1, 3)

    def kv_right():
        theirs_kv(2, 1)

    def kv_far():
        for n in (0, 3, 1, 2):
            columns[n].finish()
        share_kv(3, 2)
        theirs_kv(3, 2)

    def w_forward():
        ring.forward_left()
        ring.forward_right()
        share(1)
        share(2)
        theirs = shard(0, 1 - x_lo, core)
        wait_for(theirs, x_r.at[0])
        push(theirs, theirs, b_s.at[0], b_r.at[0], z_plus)
        push(theirs, theirs, b_s.at[1], b_r.at[1], z_minus)
        share(4)

    def w_far():
        ring.finish()
        push(shard(2, x_lo, core), shard(2, x_lo, core), x_s.at[1], x_r.at[1], x_near)
        share(3)

    def stage_4():
        wait_for(shard(3, 1 - x_lo, core), b_r.at[0])
        share(5)
        wait_for(shard(1, 1 - x_lo, core), b_r.at[1])
        share(6)
        wait_for(shard(2, 1 - x_lo, core), x_r.at[1])
        share(7)

    scale = math.log2(math.e) / math.sqrt(128)

    def step(q, k, v, m_prev, acc, masked):
        s = lax.dot_general(q, k, (((1,), (1,)), ((), ())), preferred_element_type=jnp.float32)
        if masked:
            row = lax.broadcasted_iota(jnp.int32, (DB, DB), 0)
            col = lax.broadcasted_iota(jnp.int32, (DB, DB), 1)
            edge = jnp.where(col <= row, s[:, -DB:], -1e30)
            s = edge if s.shape[1] == DB else jnp.concatenate([s[:, :-DB], edge], axis=1)
        m_new = jnp.maximum(m_prev, jnp.max(s, axis=1, keepdims=True))
        alpha = jnp.exp2((m_prev - m_new) * scale)
        shift = (m_new * scale)[:, :1]
        p = jnp.exp2(s * scale - shift).astype(jnp.bfloat16)
        joined = jnp.concatenate([v, jnp.ones_like(v)], axis=1)
        pv = jnp.dot(p, joined, preferred_element_type=jnp.float32)
        return m_new, acc * jnp.concatenate([alpha, alpha], axis=1) + pv

    m_scr[...] = jnp.full_like(m_scr, -1e30)
    acc_scr[...] = jnp.zeros_like(acc_scr)
    last = (2 * ctx, 14 - 2 * ctx)

    def tile_of(t):
        at = (t // 8, (t // 2) % 4, pl.ds((t % 2) * 2, 2))
        return kv[(0, *at)].reshape(TK, 128), kv[(1, *at)].reshape(TK, 128)

    def full(half, t):
        k, v = tile_of(t)
        for b in range(1024 // QB):
            rows = pl.ds(b * QB, QB)
            m, a = step(q_ref[half, rows, :], k, v, m_scr[half, rows, :], acc_scr[half, rows, :], False)
            m_scr[half, rows, :] = m
            acc_scr[half, rows, :] = a

    assign_slots(expert_ids, slot_tok, slot_at)
    theirs_kv(0, 0)
    for xt in range(2):
        for zz in range(4):
            wait_for(q_rows(xt, zz), q_r.at[xt * 4 + zz])

    def visit(i, carry):
        for at, act in (
            (1, kv_forward), (3, kv_forward_last), (4, kv_left), (6, w_forward), (8, kv_right), (11, w_far), (12, kv_far)
        ):
            pl.when(i == at)(act)
        s = i // 4
        n = jnp.where(s == 1, 3, jnp.where(s == 2, 1, jnp.where(s == 3, 2, 0)))
        t = (((i // 2) % 2) * 4 + (y + n) % 4) * 2 + i % 2

        def one(half, carry):
            pl.when(t < jnp.where(half == 0, last[0], last[1]))(functools.partial(full, half, t))
            return carry

        return lax.fori_loop(0, 2, one, carry)

    lax.fori_loop(0, 16, visit, 0)
    stage_4()
    my_columns = pl.ds(pl.multiple_of(exp * 128, 128), 128)
    for half in range(2):
        block = ctx if half == 0 else 7 - ctx
        k = kv[0, block // 4, block % 4].reshape(2048, 128)
        v = kv[1, block // 4, block % 4].reshape(2048, 128)
        for zz in range(4):
            rows = pl.ds(zz * DB, DB)
            seen = zz * 512 + half * 256 + DB
            m, a = step(
                q_ref[half, rows, :], k[:seen], v[:seen], m_scr[half, rows, :], acc_scr[half, rows, :], True
            )
            o_ref[half, rows, :] = (a[:, :128] / a[:, 128:]).astype(jnp.bfloat16)
            for i in range(2):
                e = zz * 4 + half * 2 + i
                src = o_ref.at[half, pl.ds(zz * DB + i * 128, 128)]
                dst = heads.at[:, my_columns]
                if half:
                    push(src, dst, h_s, h_r, (7 - ctx, e))
                else:
                    pl.when(e == exp)(lambda src=src: pltpu.make_async_copy(src, dst, h_r).start())
                    pl.when(e != exp)(lambda src=src, e=e: push(src, dst, h_s, h_r, (ctx, e)))

    for n, (dz, flip) in enumerate(order):
        wait_for(shard(dz, 1 - x_lo if flip else x_lo, 1 - core), w_r.at[n])
        wait_for(shard(dz, 1 - x_lo if flip else x_lo, core), w_s.at[n])
    own.wait()
    ring.drain()
    for sem in (x_s.at[0], x_s.at[1], b_s.at[0], b_s.at[1]):
        wait_for(w_out, sem)
    for n in range(4):
        columns[n].drain()
    for k, n in enumerate((0, 3, 1, 2)):
        wait_for(mine_of(n), d_s.at[k])
    wq_ring.drain()
    short.drain()
    wait_for(normed.at[mine], n_s.at[0])
    wait_for(normed.at[mine], n_s.at[1])
    wait_for(normed.at[other], n_s.at[2])
    for zz in range(4):

        wait_for(q_stage.at[1, zz], q_s.at[4 + zz])

        @pl.when(zz != z)
        def _(zz=zz):
            wait_for(q_stage.at[0, zz], q_s.at[zz])

        for which in range(2):

            @pl.when(jnp.logical_not((zz == z) & (which == core)))
            def _(zz=zz, which=which):
                wait_for(kv_stage.at[which, zz // 2], z_s.at[which * 4 + zz])

    wait_for(heads, h_r)

    @pl.when(x_lo == 0)
    def _():
        wait_for(heads.at[:, pl.ds(0, 15 * 128)], h_s)

    @pl.when(x_lo == 1)
    def _():
        wait_for(heads, h_s)


def attend(hidden, attn_gain, wq, wk, wv, q_gain, k_gain, cosine, sine, ids, w_out):
    vmem = pl.BlockSpec(memory_space=pltpu.VMEM)
    anywhere = pl.BlockSpec(memory_space=pl.ANY)
    dma = pltpu.SemaphoreType.DMA
    low, f32 = jnp.bfloat16, jnp.float32
    return pl.pallas_call(
        attend_kernel,
        out_shape=(
            jax.ShapeDtypeStruct((128, 2048), low),
            jax.ShapeDtypeStruct((4, 2, 2, 128, 2048), low),
            jax.ShapeDtypeStruct((16, 128), jnp.int32),
            jax.ShapeDtypeStruct((128, TOPK), jnp.int32),
        ),
        in_specs=[anywhere] * 11,
        out_specs=(anywhere, anywhere, vmem, vmem),
        scratch_shapes=[
            pltpu.VMEM((128, 2048), low),
            pltpu.VMEM((1, 2048), f32),
            pltpu.VMEM((2048, 256), low),
            pltpu.VMEM((2048, 256), low),
            pltpu.VMEM((1, 128), f32),
            pltpu.VMEM((1, 128), f32),
            pltpu.VMEM((512, 128), f32),
            pltpu.VMEM((512, 128), f32),
            pltpu.VMEM((TOPK, 128), jnp.int32),
            pltpu.VMEM((2, 2, 4, 4, 2, 256, 128), low),
            pltpu.VMEM((4, 2048, 128), low),
            pltpu.VMEM((4, 128, 2048), low),
            pltpu.VMEM((2, 2, 128, 128), low),
            pltpu.VMEM((2, 4, 256, 128), low),
            pltpu.VMEM((2, 1024, 128), low),
            pltpu.VMEM((2, 1024, 128), low),
            pltpu.VMEM((2, 1024, 128), f32),
            pltpu.VMEM((2, 1024, 256), f32),
            dma((9,)), dma, dma((4,)), dma((4,)), dma((3,)), dma((3,)), dma((8,)), dma((8,)),
            dma((4,)), dma((4,)), dma((16,)), dma((16,)), dma((4,)), dma((4,)), dma((8,)), dma((8,)),
            dma, dma((4,)), dma((4,)), dma((2,)), dma((2,)), dma((2,)), dma((2,)), dma((8,)), dma((8,)), dma, dma,
        ],
        compiler_params=pltpu.CompilerParams(
            collective_id=1, has_side_effects=True, vmem_limit_bytes=60 * 1024 * 1024
        ),
        name="attend",
    )(
        hidden, attn_gain.reshape(1, -1), wq, wk, wv, q_gain.reshape(1, -1), k_gain.reshape(1, -1),
        cosine, sine, ids, w_out,
    )


def moe_kernel(
    cap,
    slot_tok,
    heads_in, hidden_in, ffn_gain_in, slot_in, gates_in, w_out, w_gate, w_up, w_down,
    out_ref,
    send_buf, in_buf, ans_buf, ret_buf, vo, vg, vu, vd, stage, xrows, x_tiles, resid, acc,
    heads, hidden, ffn_gain, slot_at, gates,
    wsem, insem, dsend, drecv, asend, arecv,
):
    tok = hidden.shape[0]
    loads = [
        pltpu.make_async_copy(src, dst, insem.at[i])
        for i, (src, dst) in enumerate(
            [(heads_in, heads), (w_out, vo), (hidden_in, hidden), (ffn_gain_in, ffn_gain),
             (slot_in, slot_at), (gates_in, gates)]
        )
    ]
    for load in loads:
        load.start()
    copies = [
        pltpu.make_async_copy(w_gate, vg, wsem.at[0]),
        pltpu.make_async_copy(w_up, vu, wsem.at[1]),
        pltpu.make_async_copy(w_down, vd, wsem.at[2]),
    ]
    for copy in copies:
        copy.start()
    barrier = pltpu.get_barrier_semaphore()

    def greet(o, carry):
        pl.semaphore_signal(barrier, inc=1, device_id=peer_to(o), device_id_type=MESH)
        return carry

    lax.fori_loop(1, GROUPS * PEERS, greet, 0)
    x_tiles[tok:] = jnp.zeros((8, 16, 128), jnp.bfloat16)
    for load in loads:
        load.wait()
    projected = jnp.dot(heads[...], vo[...], preferred_element_type=jnp.float32)
    summed = (hidden[...].astype(jnp.float32) + projected).astype(jnp.bfloat16)
    resid[...] = summed
    normed = rms_scale(summed.astype(jnp.float32), ffn_gain[...])
    for s in range(16):
        stage[pl.ds(s, tok, stride=16), :] = normed[:, s * 128 : (s + 1) * 128]
    x_tiles[:tok] = stage[: tok * 16].astype(jnp.bfloat16).reshape(tok, 16, 128)

    for r in range(cap):
        in_buf[0, r] = x_tiles[slot_tok[r, 0]]
    pl.semaphore_wait(barrier, GROUPS * PEERS - 1)

    def fill(o, carry):
        for r in range(cap):
            send_buf[o, r] = x_tiles[slot_tok[r, o]]
        return carry


    def dispatch(o, sem):
        return pltpu.make_async_remote_copy(
            src_ref=send_buf.at[o], dst_ref=in_buf.at[o],
            send_sem=dsend.at[sem], recv_sem=drecv.at[sem],
            device_id=peer_to(o), device_id_type=MESH,
        )

    def give_back(o, sem):
        return pltpu.make_async_remote_copy(
            src_ref=ans_buf.at[o], dst_ref=ret_buf.at[o],
            send_sem=asend.at[sem], recv_sem=arecv.at[sem],
            device_id=peer_from(o), device_id_type=MESH,
        )

    def send(o, carry):
        fill(o, 0)
        dispatch(o, o // PEERS).start()
        return carry

    lax.fori_loop(1, GROUPS * PEERS, send, 0)
    for copy in copies[:3]:
        copy.wait()
    rows = PEERS * cap

    def rows_of(buf, g):
        block = buf[pl.ds(g * PEERS, PEERS)]
        stage[...] = block.astype(jnp.float32).reshape(rows * 16, 128)
        for s in range(16):
            xrows[:, s * 128 : (s + 1) * 128] = stage[pl.ds(s, rows, stride=16), :].astype(jnp.bfloat16)
        return xrows[...]

    def compute(g):
        rows_in = rows_of(in_buf, g)
        gate = jnp.dot(rows_in, vg[...], preferred_element_type=jnp.float32)
        up = jnp.dot(rows_in, vu[...], preferred_element_type=jnp.float32)
        inner = (gate / (1.0 + jnp.exp(-gate)) * up).astype(jnp.bfloat16)
        for q in range(4):
            part = jnp.dot(inner, vd[:, q * 512 : (q + 1) * 512], preferred_element_type=jnp.float32)
            for s in range(4):
                stage[pl.ds(q * 4 + s, rows, stride=16), :] = part[:, s * 128 : (s + 1) * 128]
        return stage[...].astype(jnp.bfloat16).reshape(PEERS, cap, 16, 128)

    def wait_bytes(buf, start, count, sem):
        pltpu.make_async_copy(buf.at[pl.ds(start, count)], buf.at[pl.ds(start, count)], sem).wait()

    def start_back(o, sem):
        give_back(o, sem).start()
        return sem

    for g in range(GROUPS):
        first = 1 if g == 0 else 0
        wait_bytes(in_buf, g * PEERS + first, PEERS - first, drecv.at[g])
        answers = compute(g)
        if g == 0:
            ret_buf[0] = answers[0]
        ans_buf[pl.ds(g * PEERS, PEERS)] = answers
        lax.fori_loop(g * PEERS + first, (g + 1) * PEERS, lambda o, c, g=g: start_back(o, g), g)
    acc[...] = resid[...].astype(jnp.float32)
    weights = gates[...]
    shares = weights / jnp.sum(weights, axis=1, keepdims=True)
    at = slot_at[...]
    for g in range(GROUPS):
        slot = lax.broadcasted_iota(jnp.int32, (tok, rows), 1) + g * rows
        mix = jnp.zeros((tok, rows), jnp.float32)
        for k in range(TOPK):
            mix = mix + jnp.where(at[:, k : k + 1] == slot, shares[:, k : k + 1], 0.0)
        high = mix.astype(jnp.bfloat16)
        low = (mix - high.astype(jnp.float32)).astype(jnp.bfloat16)
        first = 1 if g == 0 else 0
        wait_bytes(ret_buf, g * PEERS + first, PEERS - first, arecv.at[g])
        back = rows_of(ret_buf, g)
        acc[...] += jnp.dot(high, back, preferred_element_type=jnp.float32) + jnp.dot(
            low, back, preferred_element_type=jnp.float32
        )
    out_ref[...] = acc[...].astype(jnp.bfloat16)
    for g in range(GROUPS):
        first = 1 if g == 0 else 0
        wait_bytes(send_buf, g * PEERS + first, PEERS - first, dsend.at[g])
        wait_bytes(ans_buf, g * PEERS + first, PEERS - first, asend.at[g])


def tail(heads, hidden, ffn_gain, w_out, slot_tok, slot_at, gates, w_gate, w_up, w_down):
    tok, width = hidden.shape
    ff = w_gate.shape[1]
    n = GROUPS * PEERS
    anywhere = pl.BlockSpec(memory_space=pl.ANY)
    dma = pltpu.SemaphoreType.DMA
    low, f32 = jnp.bfloat16, jnp.float32
    return pl.pallas_call(
        functools.partial(moe_kernel, CAP),
        out_shape=jax.ShapeDtypeStruct((tok, width), low),
        in_specs=[pl.BlockSpec(memory_space=pltpu.SMEM)] + [anywhere] * 9,
        out_specs=pl.BlockSpec(memory_space=pltpu.VMEM),
        scratch_shapes=[pltpu.VMEM((n, CAP, 16, 128), low)] * 4
        + [
            pltpu.VMEM((width, width), low),
            pltpu.VMEM((width, ff), low),
            pltpu.VMEM((width, ff), low),
            pltpu.VMEM((ff, width), low),
            pltpu.VMEM((PEERS * CAP * 16, 128), f32),
            pltpu.VMEM((PEERS * CAP, width), low),
            pltpu.VMEM((tok + 8, 16, 128), low),
            pltpu.VMEM((tok, width), low),
            pltpu.VMEM((tok, width), f32),
            pltpu.VMEM((tok, width), low),
            pltpu.VMEM((tok, width), low),
            pltpu.VMEM((1, width), f32),
            pltpu.VMEM((tok, TOPK), jnp.int32),
            pltpu.VMEM((tok, TOPK), f32),
            dma((3,)), dma((6,)), dma((GROUPS,)), dma((GROUPS,)), dma((GROUPS,)), dma((GROUPS,)),
        ],
        compiler_params=pltpu.CompilerParams(
            collective_id=3, has_side_effects=True, vmem_limit_bytes=62 * 1024 * 1024
        ),
        name="tail",
    )(slot_tok, heads, hidden, ffn_gain.reshape(1, -1), slot_at, gates, w_out, w_gate, w_up, w_down)


def on_device(
    hidden_in, attn_gain, w_query, w_key, w_value, q_gain, k_gain, w_out, ffn_gain,
    w_gate, w_up, w_down, expert_ids, gate_weights,
):
    ctx, exp = lax.axis_index("ctx"), lax.axis_index("exp")
    places = ctx * 2048 + (exp // 4) * 512 + jnp.arange(512, dtype=jnp.int32)
    frequency = jnp.exp(jnp.arange(64, dtype=jnp.float32) * (-2.0 * math.log(rope_base) / 128))
    angles = places.astype(jnp.float32)[:, None] * frequency[None, :]
    cosine, sine = jnp.cos(angles), jnp.sin(angles)
    heads, w_out_all, slot_tok, slot_at = attend(
        hidden_in, attn_gain, w_query, w_key, w_value, q_gain, k_gain,
        jnp.concatenate([cosine, cosine], axis=1), jnp.concatenate([-sine, sine], axis=1), expert_ids.T, w_out,
    )
    return tail(
        heads, hidden_in, ffn_gain, w_out_all.reshape(2048, 2048), slot_tok, slot_at, gate_weights,
        w_gate[0], w_up[0], w_down[0],
    )


def solution(mesh):
    placed = (
        P(("ctx", "exp"), None),
        P(),
        P(None, "exp"),
        P(),
        P(),
        P(),
        P(),
        P("exp", None),
        P(),
        P(("ctx", "exp"), None, None),
        P(("ctx", "exp"), None, None),
        P(("ctx", "exp"), None, None),
        P(("ctx", "exp"), None),
        P(("ctx", "exp"), None),
    )
    return jax.shard_map(
        on_device, mesh=mesh, in_specs=placed, out_specs=P(("ctx", "exp"), None), check_vma=False
    )
```

```python
import functools
import math

import jax
import jax.numpy as jnp
from jax import lax
from jax.experimental import pallas as pl
from jax.experimental.pallas import tpu as pltpu
from jax.sharding import PartitionSpec as P

MESH = pl.DeviceIdType.MESH
TOPK = 8
CAP = 10
GROUPS = 4
PEERS = 32


def my_coords():
    ctx = lax.axis_index("ctx")
    exp = lax.axis_index("exp")
    x = (ctx // 4) * 2 + (exp // 2) % 2
    return x, ctx % 4, exp // 4, exp % 2


def device_at(x, y, z, core):
    return ((x // 2) * 4 + y, z * 4 + (x % 2) * 2 + core)


def offset_parts(o):
    dc, k, dy, dx = o // 64, (o // 16) % 4, (o // 4) % 4, o % 4
    return dx, (dy + dx) % 4, (k + 12 - 2 * dx - dy) % 4, dc


def peer_to(o):
    x, y, z, c = my_coords()
    dx, dy, dz, dc = offset_parts(o)
    return device_at((x + dx) % 4, (y + dy) % 4, (z + dz) % 4, (c + dc) % 2)


def peer_from(o):
    x, y, z, c = my_coords()
    dx, dy, dz, dc = offset_parts(o)
    return device_at((x + 4 - dx) % 4, (y + 4 - dy) % 4, (z + 4 - dz) % 4, (c + 2 - dc) % 2)


def offset_of_expert(e):
    x, y, z, c = my_coords()
    dx = (((e >> 6) & 1) * 2 + ((e >> 1) & 1) + 4 - x) & 3
    dy = ((e >> 4) + 4 - y) & 3
    dz = ((e >> 2) + 4 - z) & 3
    dc = (e + 2 - c) & 1
    return dc * 64 + ((dx + dy + dz) & 3) * 16 + ((dy - dx) & 3) * 4 + dx
epsilon = 1e-06
rope_base = 1000000.0


def rms_scale(values, gains):
    return values * lax.rsqrt(jnp.mean(values * values, axis=-1, keepdims=True) + epsilon) * gains


def rope(values, cosine, sine):
    return values * cosine + pltpu.roll(values, 64, 1) * sine


def push(src, dst, ssem, rsem, device):
    pltpu.make_async_remote_copy(
        src_ref=src, dst_ref=dst, send_sem=ssem, recv_sem=rsem,
        device_id=device, device_id_type=MESH,
    ).start()


def wait_for(ref, sem):
    pltpu.make_async_copy(ref, ref, sem).wait()


class Ring:
    def __init__(self, blocks, halves, plus, minus, ssem, rsem, source=None, base=0):
        self.own, self.left, self.right = blocks
        self.left_half, self.right_half, self.far_first, self.far_second = halves
        self.plus, self.minus = plus, minus
        self.ssem = [ssem.at[base + i] for i in range(4)]
        self.rsem = [rsem.at[base + i] for i in range(4)]
        self.source = self.own if source is None else source

    def start(self):
        push(self.source, self.own, self.ssem[0], self.rsem[0], self.plus)
        push(self.source, self.own, self.ssem[1], self.rsem[1], self.minus)

    def forward_left(self):
        wait_for(self.left, self.rsem[0])
        push(self.left_half, self.left_half, self.ssem[2], self.rsem[2], self.plus)

    def forward_right(self):
        wait_for(self.right, self.rsem[1])
        push(self.right_half, self.right_half, self.ssem[3], self.rsem[3], self.minus)

    def finish(self):
        wait_for(self.far_first, self.rsem[2])
        wait_for(self.far_second, self.rsem[3])

    def drain(self):
        wait_for(self.source, self.ssem[0])
        wait_for(self.source, self.ssem[1])
        wait_for(self.left_half, self.ssem[2])
        wait_for(self.right_half, self.ssem[3])


def assign_slots(expert_ids, slot_tok, slot_at):
    sub = lax.broadcasted_iota(jnp.int32, (128, 128), 0)
    lane = lax.broadcasted_iota(jnp.int32, (128, 128), 1)
    before = (sub < lane).astype(jnp.bfloat16)
    ones = jnp.ones((128, 128), jnp.bfloat16)
    offsets = offset_of_expert(expert_ids[...])
    base = jnp.zeros((128, 128), jnp.float32)
    named, ranks = [], []
    for k in range(TOPK):
        match = (sub == offsets[k : k + 1, :]).astype(jnp.float32)
        match_low = match.astype(jnp.bfloat16)
        place = base + jnp.dot(match_low, before, preferred_element_type=jnp.float32)
        rank = jnp.sum(match * place, axis=0, keepdims=True)
        base = base + jnp.dot(match_low, ones, preferred_element_type=jnp.float32)
        named.append(match)
        ranks.append(rank)
    slots = offsets * CAP + jnp.concatenate(ranks, axis=0).astype(jnp.int32)
    slot_at[...] = slots.T
    token = (128 - lane[:8]).astype(jnp.float32).astype(jnp.bfloat16)
    slot_tok[...] = jnp.full(slot_tok.shape, 128, jnp.int32)
    for r in range(CAP):
        chosen = jnp.zeros((128, 128), jnp.float32)
        for k in range(TOPK):
            chosen = chosen + jnp.where(ranks[k] == r, named[k], 0.0)
        found = lax.dot_general(
            token, chosen.astype(jnp.bfloat16), (((1,), (1,)), ((), ())), preferred_element_type=jnp.float32
        )
        slot_tok[r : r + 1, :] = 128 - found[0:1].astype(jnp.int32)


QB = 128
DB = 256
TK = 1024


def attend_kernel(
    hidden_in, attn_gain_in, wq, wk_in, wv_in, q_gain_in, k_gain_in, cosine_in, sine_in, ids_in, w_out,
    heads, w_all, slot_tok, slot_at,
    hidden, attn_gain, wk, wv, q_gain, k_gain, cosine, sine, expert_ids,
    kv, wq_all, normed, kv_stage, q_stage, q_ref, o_ref, m_scr, acc_scr,
    in_sem, own_sem, wq_s, wq_r, n_s, n_r, z_s, z_r, short_s, short_r, long_s, long_r, d_s, d_r, q_s, q_r,
    w_own, a_s, a_r, b_s, b_r, x_s, x_r, w_s, w_r, h_s, h_r,
):
    x, y, z, core = my_coords()
    ctx, exp = lax.axis_index("ctx"), lax.axis_index("exp")
    x_lo = x % 2
    sibling = device_at(x, y, z, 1 - core)
    x_other = (x // 2) * 2 + 1 - x_lo
    x_near = device_at(x_other, y, z, core)

    loads = [
        pltpu.make_async_copy(src, dst, in_sem.at[i])
        for i, (src, dst) in enumerate(
            [
                (hidden_in, hidden), (attn_gain_in, attn_gain), (wk_in, wk), (wv_in, wv),
                (q_gain_in, q_gain), (k_gain_in, k_gain), (cosine_in, cosine), (sine_in, sine),
                (ids_in, expert_ids),
            ]
        )
    ]
    for load in loads:
        load.start()
    own_wq = pltpu.make_async_copy(wq, wq_all.at[z], own_sem)
    own_wq.start()
    barrier = pltpu.get_barrier_semaphore()

    def greet(device):
        pl.semaphore_signal(barrier, inc=1, device_id=device, device_id_type=MESH)

    def greet_block(e, carry):
        greet((7 - ctx, e))
        pl.when(e != exp)(lambda: greet((ctx, e)))
        return carry

    lax.fori_loop(0, 16, greet_block, 0)
    for d in (1, 3):
        greet(device_at((x + d) % 4, y, z, core))
        greet(device_at(x, (y + d) % 4, z, core))
    mine = x_lo * 2 + core
    loads[0].wait()
    loads[1].wait()
    normed[mine] = rms_scale(hidden[...].astype(jnp.float32), attn_gain[...]).astype(jnp.bfloat16)
    pl.semaphore_wait(barrier, 35)

    def wq_half(zz, half):
        return wq_all.at[zz, pl.ds(half * 1024, 1024)]

    z_left, z_right, z_far = (z + 3) % 4, (z + 1) % 4, (z + 2) % 4
    z_plus, z_minus = device_at(x, y, z_right, core), device_at(x, y, z_left, core)
    wq_ring = Ring(
        (wq_all.at[z], wq_all.at[z_left], wq_all.at[z_right]),
        (wq_half(z_left, 0), wq_half(z_right, 1), wq_half(z_far, 0), wq_half(z_far, 1)),
        z_plus, z_minus, wq_s, wq_r, wq,
    )
    other = (1 - x_lo) * 2 + core
    push(normed.at[mine], normed.at[mine], n_s.at[1], n_r.at[1], x_near)
    push(normed.at[mine], normed.at[mine], n_s.at[0], n_r.at[0], sibling)

    for load in loads[2:]:
        load.wait()
    here = pl.ds(pl.multiple_of(mine * 128, 128), 128)
    own_normed = normed[mine]
    key_raw = jnp.dot(own_normed, wk[...], preferred_element_type=jnp.float32)
    value_raw = jnp.dot(own_normed, wv[...], preferred_element_type=jnp.float32)
    for g in range(2):
        cols = slice(g * 128, (g + 1) * 128)
        key = rope(rms_scale(key_raw[:, cols], k_gain[...]), cosine[here, :], sine[here, :])
        kv_stage[0, g] = key.astype(jnp.bfloat16)
        kv_stage[1, g] = value_raw[:, cols].astype(jnp.bfloat16)

    def piece(which, zz, cc):
        return kv.at[which, x // 2, y, zz, x_lo, pl.ds(cc * 128, 128)]

    for which in range(2):
        for zz in range(4):
            is_self = (zz == z) & (which == core)
            src = kv_stage.at[which, zz // 2]
            dst = piece(which, z, core)

            @pl.when(is_self)
            def _(src=src, dst=dst):
                pltpu.make_async_copy(src, dst, z_r.at[z * 2 + core]).start()

            @pl.when(jnp.logical_not(is_self))
            def _(src=src, dst=dst, which=which, zz=zz):
                push(src, dst, z_s.at[which * 4 + zz], z_r.at[z * 2 + core], device_at(x, y, zz, which))

    wq_ring.start()
    for zz in range(4):
        for cc in range(2):
            wait_for(piece(core, zz, cc), z_r.at[zz * 2 + cc])

    def column(n, zs=None):
        xx = (x + n) % 4
        if zs is None:
            return kv.at[core, xx // 2, y, :, xx % 2]
        return kv.at[core, xx // 2, y, pl.ds(zs * 2, 2), xx % 2]

    short = Ring(
        (column(0), column(3), column(1)),
        (column(3, 0), column(1, 1), column(2, 0), column(2, 1)),
        device_at((x + 1) % 4, y, z, core), device_at((x + 3) % 4, y, z, core), short_s, short_r,
    )
    def column_ring(n):
        xx = (x + n) % 4

        def at(dy, half=None):
            yy = (y + dy) % 4
            if half is None:
                return kv.at[core, xx // 2, yy, :, xx % 2]
            return kv.at[core, xx // 2, yy, pl.ds(half * 2, 2), xx % 2]

        return Ring(
            (at(0), at(3), at(1)), (at(3, 0), at(1, 1), at(2, 0), at(2, 1)),
            device_at(x, (y + 1) % 4, z, core), device_at(x, (y + 3) % 4, z, core), long_s, long_r, None, 4 * n,
        )

    columns = [column_ring(n) for n in range(4)]
    short.start()
    columns[0].start()
    short.forward_left()
    columns[3].start()
    short.forward_right()
    columns[1].start()
    wq_ring.forward_left()
    wq_ring.forward_right()
    short.finish()
    columns[2].start()
    columns[0].forward_left()
    columns[0].forward_right()

    def blocks_of(n, which, half=None):
        yy = (y + n) % 4
        return kv.at[which, :, yy] if half is None else kv.at[which, half, yy]

    def mine_of(n, half=None):
        return blocks_of(n, core, half)

    def share_kv(k, n):
        push(mine_of(n), mine_of(n), d_s.at[k], d_r.at[k], sibling)

    def theirs_kv(k, n):
        wait_for(blocks_of(n, 1 - core), d_r.at[k])

    share_kv(0, 0)
    wait_for(normed.at[other], n_r.at[1])
    push(normed.at[other], normed.at[other], n_s.at[2], n_r.at[2], sibling)
    wait_for(normed.at[x_lo * 2 + 1 - core], n_r.at[0])
    own_wq.wait()
    wq_ring.finish()

    def q_rows(xt, zz):
        return q_ref.at[xt, pl.ds(zz * 256, 256)]

    def query_part(xt):
        tokens = normed[pl.ds(xt * 2, 2)].reshape(256, 2048)
        at = pl.ds(pl.multiple_of(xt * 256, 256), 256)
        cos, sin = cosine[at, :], sine[at, :]
        block = jnp.where(xt == 0, ctx, 7 - ctx)
        for pair in range(2):
            weights = jnp.concatenate([wq_all[2 * pair], wq_all[2 * pair + 1]], axis=1)
            raw = jnp.dot(tokens, weights, preferred_element_type=jnp.float32)
            for k in range(2):
                zz = 2 * pair + k
                query = rope(rms_scale(raw[:, k * 128 : (k + 1) * 128], q_gain[...]), cos, sin)
                q_stage[xt, zz] = query.astype(jnp.bfloat16)
                is_self = (zz == z) & (xt == 0)

                @pl.when(is_self)
                def _(zz=zz):
                    pltpu.make_async_copy(q_stage.at[xt, zz], q_rows(xt, z), q_r.at[xt * 4 + z]).start()

                @pl.when(jnp.logical_not(is_self))
                def _(zz=zz):
                    push(
                        q_stage.at[xt, zz], q_rows(xt, z), q_s.at[xt * 4 + zz], q_r.at[xt * 4 + z],
                        (block, zz * 4 + x_lo * 2 + core),
                    )

    query_part(x_lo)
    wait_for(normed.at[(1 - x_lo) * 2 + 1 - core], n_r.at[2])
    query_part(1 - x_lo)

    def shard(dz, xl, cc):
        return w_all.at[(z + dz) % 4, xl, cc]

    def part(dz, xl, half):
        return w_all.at[(z + dz) % 4, xl, core, pl.ds(half * 64, 64)]

    ring = Ring(
        (shard(0, x_lo, core), shard(3, x_lo, core), shard(1, x_lo, core)),
        (part(3, x_lo, 0), part(1, x_lo, 1), part(2, x_lo, 0), part(2, x_lo, 1)),
        z_plus, z_minus, a_s, a_r, w_out,
    )
    order = [(0, 0), (3, 0), (1, 0), (2, 0), (0, 1), (3, 1), (1, 1), (2, 1)]

    def share(n, src=None):
        dz, flip = order[n]
        xl = 1 - x_lo if flip else x_lo
        push(shard(dz, xl, core) if src is None else src, shard(dz, xl, core), w_s.at[n], w_r.at[n], sibling)

    own = pltpu.make_async_copy(w_out, shard(0, x_lo, core), w_own)
    own.start()
    ring.start()
    push(w_out, shard(0, x_lo, core), x_s.at[0], x_r.at[0], x_near)
    share(0, w_out)

    def kv_forward():
        for n in (3, 1):
            columns[n].forward_left()
            columns[n].forward_right()

    def kv_forward_last():
        columns[2].forward_left()
        share_kv(1, 3)
        columns[2].forward_right()
        share_kv(2, 1)

    def kv_left():
        theirs_kv(1, 3)

    def kv_right():
        theirs_kv(2, 1)

    def kv_far():
        for n in (0, 3, 1, 2):
            columns[n].finish()
        share_kv(3, 2)
        theirs_kv(3, 2)

    def w_forward():
        ring.forward_left()
        ring.forward_right()
        share(1)
        share(2)
        theirs = shard(0, 1 - x_lo, core)
        wait_for(theirs, x_r.at[0])
        push(theirs, theirs, b_s.at[0], b_r.at[0], z_plus)
        push(theirs, theirs, b_s.at[1], b_r.at[1], z_minus)
        share(4)

    def w_far():
        ring.finish()
        push(shard(2, x_lo, core), shard(2, x_lo, core), x_s.at[1], x_r.at[1], x_near)
        share(3)

    def stage_4():
        wait_for(shard(3, 1 - x_lo, core), b_r.at[0])
        share(5)
        wait_for(shard(1, 1 - x_lo, core), b_r.at[1])
        share(6)
        wait_for(shard(2, 1 - x_lo, core), x_r.at[1])
        share(7)

    scale = math.log2(math.e) / math.sqrt(128)

    def step(q, k, v, m_prev, acc, masked):
        s = lax.dot_general(q, k, (((1,), (1,)), ((), ())), preferred_element_type=jnp.float32)
        if masked:
            row = lax.broadcasted_iota(jnp.int32, (DB, DB), 0)
            col = lax.broadcasted_iota(jnp.int32, (DB, DB), 1)
            edge = jnp.where(col <= row, s[:, -DB:], -1e30)
            s = edge if s.shape[1] == DB else jnp.concatenate([s[:, :-DB], edge], axis=1)
        m_new = jnp.maximum(m_prev, jnp.max(s, axis=1, keepdims=True))
        alpha = jnp.exp2((m_prev - m_new) * scale)
        shift = (m_new * scale)[:, :1]
        p = jnp.exp2(s * scale - shift).astype(jnp.bfloat16)
        joined = jnp.concatenate([v, jnp.ones_like(v)], axis=1)
        pv = jnp.dot(p, joined, preferred_element_type=jnp.float32)
        return m_new, acc * jnp.concatenate([alpha, alpha], axis=1) + pv

    m_scr[...] = jnp.full_like(m_scr, -1e30)
    acc_scr[...] = jnp.zeros_like(acc_scr)
    last = (2 * ctx, 14 - 2 * ctx)

    def tile_of(t):
        at = (t // 8, (t // 2) % 4, pl.ds((t % 2) * 2, 2))
        return kv[(0, *at)].reshape(TK, 128), kv[(1, *at)].reshape(TK, 128)

    def full(half, t):
        k, v = tile_of(t)
        for b in range(1024 // QB):
            rows = pl.ds(b * QB, QB)
            m, a = step(q_ref[half, rows, :], k, v, m_scr[half, rows, :], acc_scr[half, rows, :], False)
            m_scr[half, rows, :] = m
            acc_scr[half, rows, :] = a

    assign_slots(expert_ids, slot_tok, slot_at)
    theirs_kv(0, 0)
    for xt in range(2):
        for zz in range(4):
            wait_for(q_rows(xt, zz), q_r.at[xt * 4 + zz])

    def visit(i, carry):
        for at, act in (
            (1, kv_forward), (3, kv_forward_last), (4, kv_left), (4, w_forward), (8, kv_right), (8, w_far), (12, kv_far)
        ):
            pl.when(i == at)(act)
        s = i // 4
        n = jnp.where(s == 1, 3, jnp.where(s == 2, 1, jnp.where(s == 3, 2, 0)))
        t = (((i // 2) % 2) * 4 + (y + n) % 4) * 2 + i % 2

        def one(half, carry):
            pl.when(t < jnp.where(half == 0, last[0], last[1]))(functools.partial(full, half, t))
            return carry

        return lax.fori_loop(0, 2, one, carry)

    lax.fori_loop(0, 16, visit, 0)
    stage_4()
    my_columns = pl.ds(pl.multiple_of(exp * 128, 128), 128)
    for half in range(2):
        block = ctx if half == 0 else 7 - ctx
        k = kv[0, block // 4, block % 4].reshape(2048, 128)
        v = kv[1, block // 4, block % 4].reshape(2048, 128)
        for zz in range(4):
            rows = pl.ds(zz * DB, DB)
            seen = zz * 512 + half * 256 + DB
            m, a = step(
                q_ref[half, rows, :], k[:seen], v[:seen], m_scr[half, rows, :], acc_scr[half, rows, :], True
            )
            o_ref[half, rows, :] = (a[:, :128] / a[:, 128:]).astype(jnp.bfloat16)
            for i in range(2):
                e = zz * 4 + half * 2 + i
                src = o_ref.at[half, pl.ds(zz * DB + i * 128, 128)]
                dst = heads.at[:, my_columns]
                if half:
                    push(src, dst, h_s, h_r, (7 - ctx, e))
                else:
                    pl.when(e == exp)(lambda src=src: pltpu.make_async_copy(src, dst, h_r).start())
                    pl.when(e != exp)(lambda src=src, e=e: push(src, dst, h_s, h_r, (ctx, e)))

    for n, (dz, flip) in enumerate(order):
        wait_for(shard(dz, 1 - x_lo if flip else x_lo, 1 - core), w_r.at[n])
        wait_for(shard(dz, 1 - x_lo if flip else x_lo, core), w_s.at[n])
    own.wait()
    ring.drain()
    for sem in (x_s.at[0], x_s.at[1], b_s.at[0], b_s.at[1]):
        wait_for(w_out, sem)
    for n in range(4):
        columns[n].drain()
    for k, n in enumerate((0, 3, 1, 2)):
        wait_for(mine_of(n), d_s.at[k])
    wq_ring.drain()
    short.drain()
    wait_for(normed.at[mine], n_s.at[0])
    wait_for(normed.at[mine], n_s.at[1])
    wait_for(normed.at[other], n_s.at[2])
    for zz in range(4):

        wait_for(q_stage.at[1, zz], q_s.at[4 + zz])

        @pl.when(zz != z)
        def _(zz=zz):
            wait_for(q_stage.at[0, zz], q_s.at[zz])

        for which in range(2):

            @pl.when(jnp.logical_not((zz == z) & (which == core)))
            def _(zz=zz, which=which):
                wait_for(kv_stage.at[which, zz // 2], z_s.at[which * 4 + zz])

    wait_for(heads, h_r)

    @pl.when(x_lo == 0)
    def _():
        wait_for(heads.at[:, pl.ds(0, 15 * 128)], h_s)

    @pl.when(x_lo == 1)
    def _():
        wait_for(heads, h_s)


def attend(hidden, attn_gain, wq, wk, wv, q_gain, k_gain, cosine, sine, ids, w_out):
    vmem = pl.BlockSpec(memory_space=pltpu.VMEM)
    anywhere = pl.BlockSpec(memory_space=pl.ANY)
    dma = pltpu.SemaphoreType.DMA
    low, f32 = jnp.bfloat16, jnp.float32
    return pl.pallas_call(
        attend_kernel,
        out_shape=(
            jax.ShapeDtypeStruct((128, 2048), low),
            jax.ShapeDtypeStruct((4, 2, 2, 128, 2048), low),
            jax.ShapeDtypeStruct((16, 128), jnp.int32),
            jax.ShapeDtypeStruct((128, TOPK), jnp.int32),
        ),
        in_specs=[anywhere] * 11,
        out_specs=(anywhere, anywhere, vmem, vmem),
        scratch_shapes=[
            pltpu.VMEM((128, 2048), low),
            pltpu.VMEM((1, 2048), f32),
            pltpu.VMEM((2048, 256), low),
            pltpu.VMEM((2048, 256), low),
            pltpu.VMEM((1, 128), f32),
            pltpu.VMEM((1, 128), f32),
            pltpu.VMEM((512, 128), f32),
            pltpu.VMEM((512, 128), f32),
            pltpu.VMEM((TOPK, 128), jnp.int32),
            pltpu.VMEM((2, 2, 4, 4, 2, 256, 128), low),
            pltpu.VMEM((4, 2048, 128), low),
            pltpu.VMEM((4, 128, 2048), low),
            pltpu.VMEM((2, 2, 128, 128), low),
            pltpu.VMEM((2, 4, 256, 128), low),
            pltpu.VMEM((2, 1024, 128), low),
            pltpu.VMEM((2, 1024, 128), low),
            pltpu.VMEM((2, 1024, 128), f32),
            pltpu.VMEM((2, 1024, 256), f32),
            dma((9,)), dma, dma((4,)), dma((4,)), dma((3,)), dma((3,)), dma((8,)), dma((8,)),
            dma((4,)), dma((4,)), dma((16,)), dma((16,)), dma((4,)), dma((4,)), dma((8,)), dma((8,)),
            dma, dma((4,)), dma((4,)), dma((2,)), dma((2,)), dma((2,)), dma((2,)), dma((8,)), dma((8,)), dma, dma,
        ],
        compiler_params=pltpu.CompilerParams(
            collective_id=1, has_side_effects=True, vmem_limit_bytes=60 * 1024 * 1024
        ),
        name="attend",
    )(
        hidden, attn_gain.reshape(1, -1), wq, wk, wv, q_gain.reshape(1, -1), k_gain.reshape(1, -1),
        cosine, sine, ids, w_out,
    )


def moe_kernel(
    cap,
    slot_tok,
    heads_in, hidden_in, ffn_gain_in, slot_in, gates_in, w_out, w_gate, w_up, w_down,
    out_ref,
    send_buf, in_buf, ans_buf, ret_buf, vo, vg, vu, vd, stage, xrows, x_tiles, resid, acc,
    heads, hidden, ffn_gain, slot_at, gates,
    wsem, insem, dsend, drecv, asend, arecv,
):
    tok = hidden.shape[0]
    loads = [
        pltpu.make_async_copy(src, dst, insem.at[i])
        for i, (src, dst) in enumerate(
            [(heads_in, heads), (w_out, vo), (hidden_in, hidden), (ffn_gain_in, ffn_gain),
             (slot_in, slot_at), (gates_in, gates)]
        )
    ]
    for load in loads:
        load.start()
    copies = [
        pltpu.make_async_copy(w_gate, vg, wsem.at[0]),
        pltpu.make_async_copy(w_up, vu, wsem.at[1]),
        pltpu.make_async_copy(w_down, vd, wsem.at[2]),
    ]
    for copy in copies:
        copy.start()
    barrier = pltpu.get_barrier_semaphore()

    def greet(o, carry):
        pl.semaphore_signal(barrier, inc=1, device_id=peer_to(o), device_id_type=MESH)
        return carry

    lax.fori_loop(1, GROUPS * PEERS, greet, 0)
    x_tiles[tok:] = jnp.zeros((8, 16, 128), jnp.bfloat16)
    for load in loads:
        load.wait()
    projected = jnp.dot(heads[...], vo[...], preferred_element_type=jnp.float32)
    summed = (hidden[...].astype(jnp.float32) + projected).astype(jnp.bfloat16)
    resid[...] = summed
    normed = rms_scale(summed.astype(jnp.float32), ffn_gain[...])
    for s in range(16):
        stage[pl.ds(s, tok, stride=16), :] = normed[:, s * 128 : (s + 1) * 128]
    x_tiles[:tok] = stage[: tok * 16].astype(jnp.bfloat16).reshape(tok, 16, 128)

    for r in range(cap):
        in_buf[0, r] = x_tiles[slot_tok[r, 0]]
    pl.semaphore_wait(barrier, GROUPS * PEERS - 1)

    def fill(o, carry):
        for r in range(cap):
            send_buf[o, r] = x_tiles[slot_tok[r, o]]
        return carry


    def dispatch(o, sem):
        return pltpu.make_async_remote_copy(
            src_ref=send_buf.at[o], dst_ref=in_buf.at[o],
            send_sem=dsend.at[sem], recv_sem=drecv.at[sem],
            device_id=peer_to(o), device_id_type=MESH,
        )

    def give_back(o, sem):
        return pltpu.make_async_remote_copy(
            src_ref=ans_buf.at[o], dst_ref=ret_buf.at[o],
            send_sem=asend.at[sem], recv_sem=arecv.at[sem],
            device_id=peer_from(o), device_id_type=MESH,
        )

    def send(o, carry):
        fill(o, 0)
        dispatch(o, o // PEERS).start()
        return carry

    lax.fori_loop(1, GROUPS * PEERS, send, 0)
    for copy in copies[:3]:
        copy.wait()
    rows = PEERS * cap

    def rows_of(buf, g):
        block = buf[pl.ds(g * PEERS, PEERS)]
        stage[...] = block.astype(jnp.float32).reshape(rows * 16, 128)
        for s in range(16):
            xrows[:, s * 128 : (s + 1) * 128] = stage[pl.ds(s, rows, stride=16), :].astype(jnp.bfloat16)
        return xrows[...]

    def compute(g):
        rows_in = rows_of(in_buf, g)
        gate = jnp.dot(rows_in, vg[...], preferred_element_type=jnp.float32)
        up = jnp.dot(rows_in, vu[...], preferred_element_type=jnp.float32)
        inner = (gate / (1.0 + jnp.exp(-gate)) * up).astype(jnp.bfloat16)
        for q in range(4):
            part = jnp.dot(inner, vd[:, q * 512 : (q + 1) * 512], preferred_element_type=jnp.float32)
            for s in range(4):
                stage[pl.ds(q * 4 + s, rows, stride=16), :] = part[:, s * 128 : (s + 1) * 128]
        return stage[...].astype(jnp.bfloat16).reshape(PEERS, cap, 16, 128)

    def wait_bytes(buf, start, count, sem):
        pltpu.make_async_copy(buf.at[pl.ds(start, count)], buf.at[pl.ds(start, count)], sem).wait()

    def start_back(o, sem):
        give_back(o, sem).start()
        return sem

    for g in range(GROUPS):
        first = 1 if g == 0 else 0
        wait_bytes(in_buf, g * PEERS + first, PEERS - first, drecv.at[g])
        answers = compute(g)
        if g == 0:
            ret_buf[0] = answers[0]
        ans_buf[pl.ds(g * PEERS, PEERS)] = answers
        lax.fori_loop(g * PEERS + first, (g + 1) * PEERS, lambda o, c, g=g: start_back(o, g), g)
    acc[...] = resid[...].astype(jnp.float32)
    weights = gates[...]
    shares = weights / jnp.sum(weights, axis=1, keepdims=True)
    at = slot_at[...]
    for g in range(GROUPS):
        slot = lax.broadcasted_iota(jnp.int32, (tok, rows), 1) + g * rows
        mix = jnp.zeros((tok, rows), jnp.float32)
        for k in range(TOPK):
            mix = mix + jnp.where(at[:, k : k + 1] == slot, shares[:, k : k + 1], 0.0)
        high = mix.astype(jnp.bfloat16)
        low = (mix - high.astype(jnp.float32)).astype(jnp.bfloat16)
        first = 1 if g == 0 else 0
        wait_bytes(ret_buf, g * PEERS + first, PEERS - first, arecv.at[g])
        back = rows_of(ret_buf, g)
        acc[...] += jnp.dot(high, back, preferred_element_type=jnp.float32) + jnp.dot(
            low, back, preferred_element_type=jnp.float32
        )
    out_ref[...] = acc[...].astype(jnp.bfloat16)
    for g in range(GROUPS):
        first = 1 if g == 0 else 0
        wait_bytes(send_buf, g * PEERS + first, PEERS - first, dsend.at[g])
        wait_bytes(ans_buf, g * PEERS + first, PEERS - first, asend.at[g])


def tail(heads, hidden, ffn_gain, w_out, slot_tok, slot_at, gates, w_gate, w_up, w_down):
    tok, width = hidden.shape
    ff = w_gate.shape[1]
    n = GROUPS * PEERS
    anywhere = pl.BlockSpec(memory_space=pl.ANY)
    dma = pltpu.SemaphoreType.DMA
    low, f32 = jnp.bfloat16, jnp.float32
    return pl.pallas_call(
        functools.partial(moe_kernel, CAP),
        out_shape=jax.ShapeDtypeStruct((tok, width), low),
        in_specs=[pl.BlockSpec(memory_space=pltpu.SMEM)] + [anywhere] * 9,
        out_specs=pl.BlockSpec(memory_space=pltpu.VMEM),
        scratch_shapes=[pltpu.VMEM((n, CAP, 16, 128), low)] * 4
        + [
            pltpu.VMEM((width, width), low),
            pltpu.VMEM((width, ff), low),
            pltpu.VMEM((width, ff), low),
            pltpu.VMEM((ff, width), low),
            pltpu.VMEM((PEERS * CAP * 16, 128), f32),
            pltpu.VMEM((PEERS * CAP, width), low),
            pltpu.VMEM((tok + 8, 16, 128), low),
            pltpu.VMEM((tok, width), low),
            pltpu.VMEM((tok, width), f32),
            pltpu.VMEM((tok, width), low),
            pltpu.VMEM((tok, width), low),
            pltpu.VMEM((1, width), f32),
            pltpu.VMEM((tok, TOPK), jnp.int32),
            pltpu.VMEM((tok, TOPK), f32),
            dma((3,)), dma((6,)), dma((GROUPS,)), dma((GROUPS,)), dma((GROUPS,)), dma((GROUPS,)),
        ],
        compiler_params=pltpu.CompilerParams(
            collective_id=3, has_side_effects=True, vmem_limit_bytes=62 * 1024 * 1024
        ),
        name="tail",
    )(slot_tok, heads, hidden, ffn_gain.reshape(1, -1), slot_at, gates, w_out, w_gate, w_up, w_down)


def on_device(
    hidden_in, attn_gain, w_query, w_key, w_value, q_gain, k_gain, w_out, ffn_gain,
    w_gate, w_up, w_down, expert_ids, gate_weights,
):
    ctx, exp = lax.axis_index("ctx"), lax.axis_index("exp")
    places = ctx * 2048 + (exp // 4) * 512 + jnp.arange(512, dtype=jnp.int32)
    frequency = jnp.exp(jnp.arange(64, dtype=jnp.float32) * (-2.0 * math.log(rope_base) / 128))
    angles = places.astype(jnp.float32)[:, None] * frequency[None, :]
    cosine, sine = jnp.cos(angles), jnp.sin(angles)
    heads, w_out_all, slot_tok, slot_at = attend(
        hidden_in, attn_gain, w_query, w_key, w_value, q_gain, k_gain,
        jnp.concatenate([cosine, cosine], axis=1), jnp.concatenate([-sine, sine], axis=1), expert_ids.T, w_out,
    )
    return tail(
        heads, hidden_in, ffn_gain, w_out_all.reshape(2048, 2048), slot_tok, slot_at, gate_weights,
        w_gate[0], w_up[0], w_down[0],
    )


def solution(mesh):
    placed = (
        P(("ctx", "exp"), None),
        P(),
        P(None, "exp"),
        P(),
        P(),
        P(),
        P(),
        P("exp", None),
        P(),
        P(("ctx", "exp"), None, None),
        P(("ctx", "exp"), None, None),
        P(("ctx", "exp"), None, None),
        P(("ctx", "exp"), None),
        P(("ctx", "exp"), None),
    )
    return jax.shard_map(
        on_device, mesh=mesh, in_specs=placed, out_specs=P(("ctx", "exp"), None), check_vma=False
    )
```

```python
import functools
import math

import jax
import jax.numpy as jnp
from jax import lax
from jax.experimental import pallas as pl
from jax.experimental.pallas import tpu as pltpu
from jax.sharding import PartitionSpec as P

MESH = pl.DeviceIdType.MESH
TOPK = 8
CAP = 10
GROUPS = 4
PEERS = 32


def my_coords():
    ctx = lax.axis_index("ctx")
    exp = lax.axis_index("exp")
    x = (ctx // 4) * 2 + (exp // 2) % 2
    return x, ctx % 4, exp // 4, exp % 2


def device_at(x, y, z, core):
    return ((x // 2) * 4 + y, z * 4 + (x % 2) * 2 + core)


def offset_parts(o):
    dc, k, dy, dx = o // 64, (o // 16) % 4, (o // 4) % 4, o % 4
    return dx, (dy + dx) % 4, (k + 12 - 2 * dx - dy) % 4, dc


def peer_to(o):
    x, y, z, c = my_coords()
    dx, dy, dz, dc = offset_parts(o)
    return device_at((x + dx) % 4, (y + dy) % 4, (z + dz) % 4, (c + dc) % 2)


def peer_from(o):
    x, y, z, c = my_coords()
    dx, dy, dz, dc = offset_parts(o)
    return device_at((x + 4 - dx) % 4, (y + 4 - dy) % 4, (z + 4 - dz) % 4, (c + 2 - dc) % 2)


def offset_of_expert(e):
    x, y, z, c = my_coords()
    dx = (((e >> 6) & 1) * 2 + ((e >> 1) & 1) + 4 - x) & 3
    dy = ((e >> 4) + 4 - y) & 3
    dz = ((e >> 2) + 4 - z) & 3
    dc = (e + 2 - c) & 1
    return dc * 64 + ((dx + dy + dz) & 3) * 16 + ((dy - dx) & 3) * 4 + dx
epsilon = 1e-06
rope_base = 1000000.0


def rms_scale(values, gains):
    return values * lax.rsqrt(jnp.mean(values * values, axis=-1, keepdims=True) + epsilon) * gains


def rope(values, cosine, sine):
    return values * cosine + pltpu.roll(values, 64, 1) * sine


def push(src, dst, ssem, rsem, device):
    pltpu.make_async_remote_copy(
        src_ref=src, dst_ref=dst, send_sem=ssem, recv_sem=rsem,
        device_id=device, device_id_type=MESH,
    ).start()


def wait_for(ref, sem):
    pltpu.make_async_copy(ref, ref, sem).wait()


class Ring:
    def __init__(self, blocks, halves, plus, minus, ssem, rsem, source=None, base=0):
        self.own, self.left, self.right = blocks
        self.left_half, self.right_half, self.far_first, self.far_second = halves
        self.plus, self.minus = plus, minus
        self.ssem = [ssem.at[base + i] for i in range(4)]
        self.rsem = [rsem.at[base + i] for i in range(4)]
        self.source = self.own if source is None else source

    def start(self):
        push(self.source, self.own, self.ssem[0], self.rsem[0], self.plus)
        push(self.source, self.own, self.ssem[1], self.rsem[1], self.minus)

    def forward_left(self):
        wait_for(self.left, self.rsem[0])
        push(self.left_half, self.left_half, self.ssem[2], self.rsem[2], self.plus)

    def forward_right(self):
        wait_for(self.right, self.rsem[1])
        push(self.right_half, self.right_half, self.ssem[3], self.rsem[3], self.minus)

    def finish(self):
        wait_for(self.far_first, self.rsem[2])
        wait_for(self.far_second, self.rsem[3])

    def drain(self):
        wait_for(self.source, self.ssem[0])
        wait_for(self.source, self.ssem[1])
        wait_for(self.left_half, self.ssem[2])
        wait_for(self.right_half, self.ssem[3])


def assign_slots(expert_ids, slot_tok, slot_at):
    sub = lax.broadcasted_iota(jnp.int32, (128, 128), 0)
    lane = lax.broadcasted_iota(jnp.int32, (128, 128), 1)
    before = (sub < lane).astype(jnp.bfloat16)
    ones = jnp.ones((128, 128), jnp.bfloat16)
    offsets = offset_of_expert(expert_ids[...])
    base = jnp.zeros((128, 128), jnp.float32)
    named, ranks = [], []
    for k in range(TOPK):
        match = (sub == offsets[k : k + 1, :]).astype(jnp.float32)
        match_low = match.astype(jnp.bfloat16)
        place = base + jnp.dot(match_low, before, preferred_element_type=jnp.float32)
        rank = jnp.sum(match * place, axis=0, keepdims=True)
        base = base + jnp.dot(match_low, ones, preferred_element_type=jnp.float32)
        named.append(match)
        ranks.append(rank)
    slots = offsets * CAP + jnp.concatenate(ranks, axis=0).astype(jnp.int32)
    slot_at[...] = slots.T
    token = (128 - lane[:8]).astype(jnp.float32).astype(jnp.bfloat16)
    slot_tok[...] = jnp.full(slot_tok.shape, 128, jnp.int32)
    for r in range(CAP):
        chosen = jnp.zeros((128, 128), jnp.float32)
        for k in range(TOPK):
            chosen = chosen + jnp.where(ranks[k] == r, named[k], 0.0)
        found = lax.dot_general(
            token, chosen.astype(jnp.bfloat16), (((1,), (1,)), ((), ())), preferred_element_type=jnp.float32
        )
        slot_tok[r : r + 1, :] = 128 - found[0:1].astype(jnp.int32)


QB = 128
DB = 256
TK = 1024


def attend_kernel(
    hidden_in, attn_gain_in, wq, wk_in, wv_in, q_gain_in, k_gain_in, cosine_in, sine_in, ids_in, w_out,
    heads, w_all, slot_tok, slot_at,
    hidden, attn_gain, wk, wv, q_gain, k_gain, cosine, sine, expert_ids,
    kv, wq_all, normed, kv_stage, q_stage, q_ref, o_ref, m_scr, acc_scr,
    in_sem, own_sem, wq_s, wq_r, n_s, n_r, z_s, z_r, short_s, short_r, long_s, long_r, d_s, d_r, q_s, q_r,
    w_own, a_s, a_r, b_s, b_r, x_s, x_r, w_s, w_r, h_s, h_r,
):
    x, y, z, core = my_coords()
    ctx, exp = lax.axis_index("ctx"), lax.axis_index("exp")
    x_lo = x % 2
    sibling = device_at(x, y, z, 1 - core)
    x_other = (x // 2) * 2 + 1 - x_lo
    x_near = device_at(x_other, y, z, core)

    loads = [
        pltpu.make_async_copy(src, dst, in_sem.at[i])
        for i, (src, dst) in enumerate(
            [
                (hidden_in, hidden), (attn_gain_in, attn_gain), (wk_in, wk), (wv_in, wv),
                (q_gain_in, q_gain), (k_gain_in, k_gain), (cosine_in, cosine), (sine_in, sine),
                (ids_in, expert_ids),
            ]
        )
    ]
    for load in loads:
        load.start()
    own_wq = pltpu.make_async_copy(wq, wq_all.at[z], own_sem)
    own_wq.start()
    barrier = pltpu.get_barrier_semaphore()

    def greet(device):
        pl.semaphore_signal(barrier, inc=1, device_id=device, device_id_type=MESH)

    def greet_block(e, carry):
        greet((7 - ctx, e))
        pl.when(e != exp)(lambda: greet((ctx, e)))
        return carry

    lax.fori_loop(0, 16, greet_block, 0)
    for d in (1, 3):
        greet(device_at((x + d) % 4, y, z, core))
        greet(device_at(x, (y + d) % 4, z, core))
    mine = x_lo * 2 + core
    loads[0].wait()
    loads[1].wait()
    normed[mine] = rms_scale(hidden[...].astype(jnp.float32), attn_gain[...]).astype(jnp.bfloat16)
    pl.semaphore_wait(barrier, 35)

    def wq_half(zz, half):
        return wq_all.at[zz, pl.ds(half * 1024, 1024)]

    z_left, z_right, z_far = (z + 3) % 4, (z + 1) % 4, (z + 2) % 4
    z_plus, z_minus = device_at(x, y, z_right, core), device_at(x, y, z_left, core)
    wq_ring = Ring(
        (wq_all.at[z], wq_all.at[z_left], wq_all.at[z_right]),
        (wq_half(z_left, 0), wq_half(z_right, 1), wq_half(z_far, 0), wq_half(z_far, 1)),
        z_plus, z_minus, wq_s, wq_r, wq,
    )
    other = (1 - x_lo) * 2 + core
    push(normed.at[mine], normed.at[mine], n_s.at[1], n_r.at[1], x_near)
    push(normed.at[mine], normed.at[mine], n_s.at[0], n_r.at[0], sibling)

    for load in loads[2:]:
        load.wait()
    here = pl.ds(pl.multiple_of(mine * 128, 128), 128)
    own_normed = normed[mine]
    key_raw = jnp.dot(own_normed, wk[...], preferred_element_type=jnp.float32)
    value_raw = jnp.dot(own_normed, wv[...], preferred_element_type=jnp.float32)
    for g in range(2):
        cols = slice(g * 128, (g + 1) * 128)
        key = rope(rms_scale(key_raw[:, cols], k_gain[...]), cosine[here, :], sine[here, :])
        kv_stage[0, g] = key.astype(jnp.bfloat16)
        kv_stage[1, g] = value_raw[:, cols].astype(jnp.bfloat16)

    def piece(which, zz, cc):
        return kv.at[which, x // 2, y, zz, x_lo, pl.ds(cc * 128, 128)]

    for which in range(2):
        for zz in range(4):
            is_self = (zz == z) & (which == core)
            src = kv_stage.at[which, zz // 2]
            dst = piece(which, z, core)

            @pl.when(is_self)
            def _(src=src, dst=dst):
                pltpu.make_async_copy(src, dst, z_r.at[z * 2 + core]).start()

            @pl.when(jnp.logical_not(is_self))
            def _(src=src, dst=dst, which=which, zz=zz):
                push(src, dst, z_s.at[which * 4 + zz], z_r.at[z * 2 + core], device_at(x, y, zz, which))

    wq_ring.start()
    for zz in range(4):
        for cc in range(2):
            wait_for(piece(core, zz, cc), z_r.at[zz * 2 + cc])

    def column(n, zs=None):
        xx = (x + n) % 4
        if zs is None:
            return kv.at[core, xx // 2, y, :, xx % 2]
        return kv.at[core, xx // 2, y, pl.ds(zs * 2, 2), xx % 2]

    short = Ring(
        (column(0), column(3), column(1)),
        (column(3, 0), column(1, 1), column(2, 0), column(2, 1)),
        device_at((x + 1) % 4, y, z, core), device_at((x + 3) % 4, y, z, core), short_s, short_r,
    )
    def column_ring(n):
        xx = (x + n) % 4

        def at(dy, half=None):
            yy = (y + dy) % 4
            if half is None:
                return kv.at[core, xx // 2, yy, :, xx % 2]
            return kv.at[core, xx // 2, yy, pl.ds(half * 2, 2), xx % 2]

        return Ring(
            (at(0), at(3), at(1)), (at(3, 0), at(1, 1), at(2, 0), at(2, 1)),
            device_at(x, (y + 1) % 4, z, core), device_at(x, (y + 3) % 4, z, core), long_s, long_r, None, 4 * n,
        )

    columns = [column_ring(n) for n in range(4)]
    short.start()
    columns[0].start()
    short.forward_left()
    columns[3].start()
    short.forward_right()
    columns[1].start()
    wq_ring.forward_left()
    wq_ring.forward_right()
    short.finish()
    columns[2].start()
    columns[0].forward_left()
    columns[0].forward_right()

    def blocks_of(n, which, half=None):
        yy = (y + n) % 4
        return kv.at[which, :, yy] if half is None else kv.at[which, half, yy]

    def mine_of(n, half=None):
        return blocks_of(n, core, half)

    def share_kv(k, n):
        push(mine_of(n), mine_of(n), d_s.at[k], d_r.at[k], sibling)

    def theirs_kv(k, n):
        wait_for(blocks_of(n, 1 - core), d_r.at[k])

    share_kv(0, 0)
    wait_for(normed.at[other], n_r.at[1])
    push(normed.at[other], normed.at[other], n_s.at[2], n_r.at[2], sibling)
    wait_for(normed.at[x_lo * 2 + 1 - core], n_r.at[0])
    own_wq.wait()
    wq_ring.finish()

    def q_rows(xt, zz):
        return q_ref.at[xt, pl.ds(zz * 256, 256)]

    def query_part(xt):
        tokens = normed[pl.ds(xt * 2, 2)].reshape(256, 2048)
        at = pl.ds(pl.multiple_of(xt * 256, 256), 256)
        cos, sin = cosine[at, :], sine[at, :]
        block = jnp.where(xt == 0, ctx, 7 - ctx)
        for pair in range(2):
            weights = jnp.concatenate([wq_all[2 * pair], wq_all[2 * pair + 1]], axis=1)
            raw = jnp.dot(tokens, weights, preferred_element_type=jnp.float32)
            for k in range(2):
                zz = 2 * pair + k
                query = rope(rms_scale(raw[:, k * 128 : (k + 1) * 128], q_gain[...]), cos, sin)
                q_stage[xt, zz] = query.astype(jnp.bfloat16)
                is_self = (zz == z) & (xt == 0)

                @pl.when(is_self)
                def _(zz=zz):
                    pltpu.make_async_copy(q_stage.at[xt, zz], q_rows(xt, z), q_r.at[xt * 4 + z]).start()

                @pl.when(jnp.logical_not(is_self))
                def _(zz=zz):
                    push(
                        q_stage.at[xt, zz], q_rows(xt, z), q_s.at[xt * 4 + zz], q_r.at[xt * 4 + z],
                        (block, zz * 4 + x_lo * 2 + core),
                    )

    query_part(x_lo)
    wait_for(normed.at[(1 - x_lo) * 2 + 1 - core], n_r.at[2])
    query_part(1 - x_lo)

    def shard(dz, xl, cc):
        return w_all.at[(z + dz) % 4, xl, cc]

    def part(dz, xl, half):
        return w_all.at[(z + dz) % 4, xl, core, pl.ds(half * 64, 64)]

    ring = Ring(
        (shard(0, x_lo, core), shard(3, x_lo, core), shard(1, x_lo, core)),
        (part(3, x_lo, 0), part(1, x_lo, 1), part(2, x_lo, 0), part(2, x_lo, 1)),
        z_plus, z_minus, a_s, a_r, w_out,
    )
    order = [(0, 0), (3, 0), (1, 0), (2, 0), (0, 1), (3, 1), (1, 1), (2, 1)]

    def share(n, src=None):
        dz, flip = order[n]
        xl = 1 - x_lo if flip else x_lo
        push(shard(dz, xl, core) if src is None else src, shard(dz, xl, core), w_s.at[n], w_r.at[n], sibling)

    own = pltpu.make_async_copy(w_out, shard(0, x_lo, core), w_own)
    own.start()
    ring.start()
    push(w_out, shard(0, x_lo, core), x_s.at[0], x_r.at[0], x_near)
    share(0, w_out)

    def kv_forward():
        for n in (3, 1):
            columns[n].forward_left()
            columns[n].forward_right()

    def kv_forward_last():
        columns[2].forward_left()
        share_kv(1, 3)
        columns[2].forward_right()
        share_kv(2, 1)

    def kv_left():
        theirs_kv(1, 3)

    def kv_right():
        theirs_kv(2, 1)

    def kv_far():
        for n in (0, 3, 1, 2):
            columns[n].finish()
        share_kv(3, 2)
        theirs_kv(3, 2)

    def w_forward():
        ring.forward_left()
        ring.forward_right()
        share(1)
        share(2)
        theirs = shard(0, 1 - x_lo, core)
        wait_for(theirs, x_r.at[0])
        push(theirs, theirs, b_s.at[0], b_r.at[0], z_plus)
        push(theirs, theirs, b_s.at[1], b_r.at[1], z_minus)
        share(4)

    def w_far():
        ring.finish()
        push(shard(2, x_lo, core), shard(2, x_lo, core), x_s.at[1], x_r.at[1], x_near)
        share(3)

    def stage_4():
        wait_for(shard(3, 1 - x_lo, core), b_r.at[0])
        share(5)
        wait_for(shard(1, 1 - x_lo, core), b_r.at[1])
        share(6)
        wait_for(shard(2, 1 - x_lo, core), x_r.at[1])
        share(7)

    scale = math.log2(math.e) / math.sqrt(128)

    def step(q, k, v, m_prev, acc, masked):
        s = lax.dot_general(q, k, (((1,), (1,)), ((), ())), preferred_element_type=jnp.float32)
        if masked:
            row = lax.broadcasted_iota(jnp.int32, (DB, DB), 0)
            col = lax.broadcasted_iota(jnp.int32, (DB, DB), 1)
            edge = jnp.where(col <= row, s[:, -DB:], -1e30)
            s = edge if s.shape[1] == DB else jnp.concatenate([s[:, :-DB], edge], axis=1)
        m_new = jnp.maximum(m_prev, jnp.max(s, axis=1, keepdims=True))
        alpha = jnp.exp2((m_prev - m_new) * scale)
        shift = (m_new * scale)[:, :1]
        p = jnp.exp2(s * scale - shift).astype(jnp.bfloat16)
        joined = jnp.concatenate([v, jnp.ones_like(v)], axis=1)
        pv = jnp.dot(p, joined, preferred_element_type=jnp.float32)
        return m_new, acc * jnp.concatenate([alpha, alpha], axis=1) + pv

    m_scr[...] = jnp.full_like(m_scr, -1e30)
    acc_scr[...] = jnp.zeros_like(acc_scr)
    last = (2 * ctx, 14 - 2 * ctx)

    def tile_of(t):
        at = (t // 8, (t // 2) % 4, pl.ds((t % 2) * 2, 2))
        return kv[(0, *at)].reshape(TK, 128), kv[(1, *at)].reshape(TK, 128)

    def full(half, t):
        k, v = tile_of(t)
        for b in range(1024 // QB):
            rows = pl.ds(b * QB, QB)
            m, a = step(q_ref[half, rows, :], k, v, m_scr[half, rows, :], acc_scr[half, rows, :], False)
            m_scr[half, rows, :] = m
            acc_scr[half, rows, :] = a

    assign_slots(expert_ids, slot_tok, slot_at)
    theirs_kv(0, 0)
    for xt in range(2):
        for zz in range(4):
            wait_for(q_rows(xt, zz), q_r.at[xt * 4 + zz])

    def visit(i, carry):
        for at, act in (
            (1, kv_forward), (3, kv_forward_last), (4, kv_left), (4, w_forward), (8, kv_right), (8, w_far), (12, kv_far)
        ):
            pl.when(i == at)(act)
        s = i // 4
        n = jnp.where(s == 1, 3, jnp.where(s == 2, 1, jnp.where(s == 3, 2, 0)))
        t = (((i // 2) % 2) * 4 + (y + n) % 4) * 2 + i % 2

        def one(half, carry):
            pl.when(t < jnp.where(half == 0, last[0], last[1]))(functools.partial(full, half, t))
            return carry

        return lax.fori_loop(0, 2, one, carry)

    lax.fori_loop(0, 16, visit, 0)
    stage_4()
    my_columns = pl.ds(pl.multiple_of(exp * 128, 128), 128)
    for half in range(2):
        block = ctx if half == 0 else 7 - ctx
        k = kv[0, block // 4, block % 4].reshape(2048, 128)
        v = kv[1, block // 4, block % 4].reshape(2048, 128)
        for zz in range(4):
            rows = pl.ds(zz * DB, DB)
            seen = zz * 512 + half * 256 + DB
            m, a = step(
                q_ref[half, rows, :], k[:seen], v[:seen], m_scr[half, rows, :], acc_scr[half, rows, :], True
            )
            o_ref[half, rows, :] = (a[:, :128] / a[:, 128:]).astype(jnp.bfloat16)
            for i in range(2):
                e = zz * 4 + half * 2 + i
                src = o_ref.at[half, pl.ds(zz * DB + i * 128, 128)]
                dst = heads.at[:, my_columns]
                if half:
                    push(src, dst, h_s, h_r, (7 - ctx, e))
                else:
                    pl.when(e == exp)(lambda src=src: pltpu.make_async_copy(src, dst, h_r).start())
                    pl.when(e != exp)(lambda src=src, e=e: push(src, dst, h_s, h_r, (ctx, e)))

    for n, (dz, flip) in enumerate(order):
        wait_for(shard(dz, 1 - x_lo if flip else x_lo, 1 - core), w_r.at[n])
        wait_for(shard(dz, 1 - x_lo if flip else x_lo, core), w_s.at[n])
    own.wait()
    ring.drain()
    for sem in (x_s.at[0], x_s.at[1], b_s.at[0], b_s.at[1]):
        wait_for(w_out, sem)
    for n in range(4):
        columns[n].drain()
    for k, n in enumerate((0, 3, 1, 2)):
        wait_for(mine_of(n), d_s.at[k])
    wq_ring.drain()
    short.drain()
    wait_for(normed.at[mine], n_s.at[0])
    wait_for(normed.at[mine], n_s.at[1])
    wait_for(normed.at[other], n_s.at[2])
    for zz in range(4):

        wait_for(q_stage.at[1, zz], q_s.at[4 + zz])

        @pl.when(zz != z)
        def _(zz=zz):
            wait_for(q_stage.at[0, zz], q_s.at[zz])

        for which in range(2):

            @pl.when(jnp.logical_not((zz == z) & (which == core)))
            def _(zz=zz, which=which):
                wait_for(kv_stage.at[which, zz // 2], z_s.at[which * 4 + zz])

    wait_for(heads, h_r)

    @pl.when(x_lo == 0)
    def _():
        wait_for(heads.at[:, pl.ds(0, 15 * 128)], h_s)

    @pl.when(x_lo == 1)
    def _():
        wait_for(heads, h_s)


def attend(hidden, attn_gain, wq, wk, wv, q_gain, k_gain, cosine, sine, ids, w_out):
    vmem = pl.BlockSpec(memory_space=pltpu.VMEM)
    anywhere = pl.BlockSpec(memory_space=pl.ANY)
    dma = pltpu.SemaphoreType.DMA
    low, f32 = jnp.bfloat16, jnp.float32
    return pl.pallas_call(
        attend_kernel,
        out_shape=(
            jax.ShapeDtypeStruct((128, 2048), low),
            jax.ShapeDtypeStruct((4, 2, 2, 128, 2048), low),
            jax.ShapeDtypeStruct((16, 128), jnp.int32),
            jax.ShapeDtypeStruct((128, TOPK), jnp.int32),
        ),
        in_specs=[anywhere] * 11,
        out_specs=(anywhere, anywhere, vmem, vmem),
        scratch_shapes=[
            pltpu.VMEM((128, 2048), low),
            pltpu.VMEM((1, 2048), f32),
            pltpu.VMEM((2048, 256), low),
            pltpu.VMEM((2048, 256), low),
            pltpu.VMEM((1, 128), f32),
            pltpu.VMEM((1, 128), f32),
            pltpu.VMEM((512, 128), f32),
            pltpu.VMEM((512, 128), f32),
            pltpu.VMEM((TOPK, 128), jnp.int32),
            pltpu.VMEM((2, 2, 4, 4, 2, 256, 128), low),
            pltpu.VMEM((4, 2048, 128), low),
            pltpu.VMEM((4, 128, 2048), low),
            pltpu.VMEM((2, 2, 128, 128), low),
            pltpu.VMEM((2, 4, 256, 128), low),
            pltpu.VMEM((2, 1024, 128), low),
            pltpu.VMEM((2, 1024, 128), low),
            pltpu.VMEM((2, 1024, 128), f32),
            pltpu.VMEM((2, 1024, 256), f32),
            dma((9,)), dma, dma((4,)), dma((4,)), dma((3,)), dma((3,)), dma((8,)), dma((8,)),
            dma((4,)), dma((4,)), dma((16,)), dma((16,)), dma((4,)), dma((4,)), dma((8,)), dma((8,)),
            dma, dma((4,)), dma((4,)), dma((2,)), dma((2,)), dma((2,)), dma((2,)), dma((8,)), dma((8,)), dma, dma,
        ],
        compiler_params=pltpu.CompilerParams(
            collective_id=1, has_side_effects=True, vmem_limit_bytes=60 * 1024 * 1024
        ),
        name="attend",
    )(
        hidden, attn_gain.reshape(1, -1), wq, wk, wv, q_gain.reshape(1, -1), k_gain.reshape(1, -1),
        cosine, sine, ids, w_out,
    )


def moe_kernel(
    cap,
    slot_tok,
    heads_in, hidden_in, ffn_gain_in, slot_in, gates_in, w_out, w_gate, w_up, w_down,
    out_ref,
    send_buf, in_buf, ans_buf, ret_buf, vo, vg, vu, vd, stage, xrows, x_tiles, resid, acc,
    heads, hidden, ffn_gain, slot_at, gates,
    wsem, insem, dsend, drecv, asend, arecv,
):
    tok = hidden.shape[0]
    loads = [
        pltpu.make_async_copy(src, dst, insem.at[i])
        for i, (src, dst) in enumerate(
            [(heads_in, heads), (w_out, vo), (hidden_in, hidden), (ffn_gain_in, ffn_gain),
             (slot_in, slot_at), (gates_in, gates)]
        )
    ]
    for load in loads:
        load.start()
    copies = [
        pltpu.make_async_copy(w_gate, vg, wsem.at[0]),
        pltpu.make_async_copy(w_up, vu, wsem.at[1]),
        pltpu.make_async_copy(w_down, vd, wsem.at[2]),
    ]
    for copy in copies:
        copy.start()
    barrier = pltpu.get_barrier_semaphore()

    def greet(o, carry):
        pl.semaphore_signal(barrier, inc=1, device_id=peer_to(o), device_id_type=MESH)
        return carry

    x_tiles[tok:] = jnp.zeros((8, 16, 128), jnp.bfloat16)
    for load in loads:
        load.wait()
    projected = jnp.dot(heads[...], vo[...], preferred_element_type=jnp.float32)
    summed = (hidden[...].astype(jnp.float32) + projected).astype(jnp.bfloat16)
    lax.fori_loop(1, GROUPS * PEERS, greet, 0)
    resid[...] = summed
    normed = rms_scale(summed.astype(jnp.float32), ffn_gain[...])
    for s in range(16):
        stage[pl.ds(s, tok, stride=16), :] = normed[:, s * 128 : (s + 1) * 128]
    x_tiles[:tok] = stage[: tok * 16].astype(jnp.bfloat16).reshape(tok, 16, 128)

    for r in range(cap):
        in_buf[0, r] = x_tiles[slot_tok[r, 0]]
    pl.semaphore_wait(barrier, GROUPS * PEERS - 1)

    def fill(o, carry):
        for r in range(cap):
            send_buf[o, r] = x_tiles[slot_tok[r, o]]
        return carry


    def dispatch(o, sem):
        return pltpu.make_async_remote_copy(
            src_ref=send_buf.at[o], dst_ref=in_buf.at[o],
            send_sem=dsend.at[sem], recv_sem=drecv.at[sem],
            device_id=peer_to(o), device_id_type=MESH,
        )

    def give_back(o, sem):
        return pltpu.make_async_remote_copy(
            src_ref=ans_buf.at[o], dst_ref=ret_buf.at[o],
            send_sem=asend.at[sem], recv_sem=arecv.at[sem],
            device_id=peer_from(o), device_id_type=MESH,
        )

    def send(o, carry):
        fill(o, 0)
        dispatch(o, o // PEERS).start()
        return carry

    lax.fori_loop(1, GROUPS * PEERS, send, 0)
    for copy in copies[:3]:
        copy.wait()
    rows = PEERS * cap

    def rows_of(buf, g):
        block = buf[pl.ds(g * PEERS, PEERS)]
        stage[...] = block.astype(jnp.float32).reshape(rows * 16, 128)
        for s in range(16):
            xrows[:, s * 128 : (s + 1) * 128] = stage[pl.ds(s, rows, stride=16), :].astype(jnp.bfloat16)
        return xrows[...]

    def compute(g):
        rows_in = rows_of(in_buf, g)
        gate = jnp.dot(rows_in, vg[...], preferred_element_type=jnp.float32)
        up = jnp.dot(rows_in, vu[...], preferred_element_type=jnp.float32)
        inner = (gate / (1.0 + jnp.exp(-gate)) * up).astype(jnp.bfloat16)
        for q in range(4):
            part = jnp.dot(inner, vd[:, q * 512 : (q + 1) * 512], preferred_element_type=jnp.float32)
            for s in range(4):
                stage[pl.ds(q * 4 + s, rows, stride=16), :] = part[:, s * 128 : (s + 1) * 128]
        return stage[...].astype(jnp.bfloat16).reshape(PEERS, cap, 16, 128)

    def wait_bytes(buf, start, count, sem):
        pltpu.make_async_copy(buf.at[pl.ds(start, count)], buf.at[pl.ds(start, count)], sem).wait()

    def start_back(o, sem):
        give_back(o, sem).start()
        return sem

    for g in range(GROUPS):
        first = 1 if g == 0 else 0
        wait_bytes(in_buf, g * PEERS + first, PEERS - first, drecv.at[g])
        answers = compute(g)
        if g == 0:
            ret_buf[0] = answers[0]
        ans_buf[pl.ds(g * PEERS, PEERS)] = answers
        lax.fori_loop(g * PEERS + first, (g + 1) * PEERS, lambda o, c, g=g: start_back(o, g), g)
    acc[...] = resid[...].astype(jnp.float32)
    weights = gates[...].T
    shares = weights / jnp.sum(weights, axis=1, keepdims=True)
    at = slot_at[...]
    for g in range(GROUPS):
        slot = lax.broadcasted_iota(jnp.int32, (tok, rows), 1) + g * rows
        mix = jnp.zeros((tok, rows), jnp.float32)
        for k in range(TOPK):
            mix = mix + jnp.where(at[:, k : k + 1] == slot, shares[:, k : k + 1], 0.0)
        high = mix.astype(jnp.bfloat16)
        low = (mix - high.astype(jnp.float32)).astype(jnp.bfloat16)
        first = 1 if g == 0 else 0
        wait_bytes(ret_buf, g * PEERS + first, PEERS - first, arecv.at[g])
        back = rows_of(ret_buf, g)
        acc[...] += jnp.dot(high, back, preferred_element_type=jnp.float32) + jnp.dot(
            low, back, preferred_element_type=jnp.float32
        )
    out_ref[...] = acc[...].astype(jnp.bfloat16)
    for g in range(GROUPS):
        first = 1 if g == 0 else 0
        wait_bytes(send_buf, g * PEERS + first, PEERS - first, dsend.at[g])
        wait_bytes(ans_buf, g * PEERS + first, PEERS - first, asend.at[g])


def tail(heads, hidden, ffn_gain, w_out, slot_tok, slot_at, gates, w_gate, w_up, w_down):
    tok, width = hidden.shape
    ff = w_gate.shape[1]
    n = GROUPS * PEERS
    anywhere = pl.BlockSpec(memory_space=pl.ANY)
    dma = pltpu.SemaphoreType.DMA
    low, f32 = jnp.bfloat16, jnp.float32
    return pl.pallas_call(
        functools.partial(moe_kernel, CAP),
        out_shape=jax.ShapeDtypeStruct((tok, width), low),
        in_specs=[pl.BlockSpec(memory_space=pltpu.SMEM)] + [anywhere] * 9,
        out_specs=pl.BlockSpec(memory_space=pltpu.VMEM),
        scratch_shapes=[pltpu.VMEM((n, CAP, 16, 128), low)] * 4
        + [
            pltpu.VMEM((width, width), low),
            pltpu.VMEM((width, ff), low),
            pltpu.VMEM((width, ff), low),
            pltpu.VMEM((ff, width), low),
            pltpu.VMEM((PEERS * CAP * 16, 128), f32),
            pltpu.VMEM((PEERS * CAP, width), low),
            pltpu.VMEM((tok + 8, 16, 128), low),
            pltpu.VMEM((tok, width), low),
            pltpu.VMEM((tok, width), f32),
            pltpu.VMEM((tok, width), low),
            pltpu.VMEM((tok, width), low),
            pltpu.VMEM((1, width), f32),
            pltpu.VMEM((tok, TOPK), jnp.int32),
            pltpu.VMEM((TOPK, tok), f32),
            dma((3,)), dma((6,)), dma((GROUPS,)), dma((GROUPS,)), dma((GROUPS,)), dma((GROUPS,)),
        ],
        compiler_params=pltpu.CompilerParams(
            collective_id=3, has_side_effects=True, vmem_limit_bytes=62 * 1024 * 1024
        ),
        name="tail",
    )(slot_tok, heads, hidden, ffn_gain.reshape(1, -1), slot_at, gates, w_out, w_gate, w_up, w_down)


def on_device(
    hidden_in, attn_gain, w_query, w_key, w_value, q_gain, k_gain, w_out, ffn_gain,
    w_gate, w_up, w_down, expert_ids, gate_weights,
):
    ctx, exp = lax.axis_index("ctx"), lax.axis_index("exp")
    places = ctx * 2048 + (exp // 4) * 512 + jnp.arange(512, dtype=jnp.int32)
    frequency = jnp.exp(jnp.arange(64, dtype=jnp.float32) * (-2.0 * math.log(rope_base) / 128))
    angles = places.astype(jnp.float32)[:, None] * frequency[None, :]
    cosine, sine = jnp.cos(angles), jnp.sin(angles)
    heads, w_out_all, slot_tok, slot_at = attend(
        hidden_in, attn_gain, w_query, w_key, w_value, q_gain, k_gain,
        jnp.concatenate([cosine, cosine], axis=1), jnp.concatenate([-sine, sine], axis=1), expert_ids.T, w_out,
    )
    return tail(
        heads, hidden_in, ffn_gain, w_out_all.reshape(2048, 2048), slot_tok, slot_at, gate_weights.T,
        w_gate[0], w_up[0], w_down[0],
    )


def solution(mesh):
    placed = (
        P(("ctx", "exp"), None),
        P(),
        P(None, "exp"),
        P(),
        P(),
        P(),
        P(),
        P("exp", None),
        P(),
        P(("ctx", "exp"), None, None),
        P(("ctx", "exp"), None, None),
        P(("ctx", "exp"), None, None),
        P(("ctx", "exp"), None),
        P(("ctx", "exp"), None),
    )
    return jax.shard_map(
        on_device, mesh=mesh, in_specs=placed, out_specs=P(("ctx", "exp"), None), check_vma=False
    )
```

```python
import functools
import math

import jax
import jax.numpy as jnp
from jax import lax
from jax.experimental import pallas as pl
from jax.experimental.pallas import tpu as pltpu
from jax.sharding import PartitionSpec as P

MESH = pl.DeviceIdType.MESH
TOPK = 8
CAP = 10
GROUPS = 4
PEERS = 32


def my_coords():
    ctx = lax.axis_index("ctx")
    exp = lax.axis_index("exp")
    x = (ctx // 4) * 2 + (exp // 2) % 2
    return x, ctx % 4, exp // 4, exp % 2


def device_at(x, y, z, core):
    return ((x // 2) * 4 + y, z * 4 + (x % 2) * 2 + core)


def offset_parts(o):
    dc, k, dy, dx = o // 64, (o // 16) % 4, (o // 4) % 4, o % 4
    return dx, (dy + dx) % 4, (k + 12 - 2 * dx - dy) % 4, dc


def peer_to(o):
    x, y, z, c = my_coords()
    dx, dy, dz, dc = offset_parts(o)
    return device_at((x + dx) % 4, (y + dy) % 4, (z + dz) % 4, (c + dc) % 2)


def peer_from(o):
    x, y, z, c = my_coords()
    dx, dy, dz, dc = offset_parts(o)
    return device_at((x + 4 - dx) % 4, (y + 4 - dy) % 4, (z + 4 - dz) % 4, (c + 2 - dc) % 2)


def offset_of_expert(e):
    x, y, z, c = my_coords()
    dx = (((e >> 6) & 1) * 2 + ((e >> 1) & 1) + 4 - x) & 3
    dy = ((e >> 4) + 4 - y) & 3
    dz = ((e >> 2) + 4 - z) & 3
    dc = (e + 2 - c) & 1
    return dc * 64 + ((dx + dy + dz) & 3) * 16 + ((dy - dx) & 3) * 4 + dx
epsilon = 1e-06
rope_base = 1000000.0


def rms_scale(values, gains):
    return values * lax.rsqrt(jnp.mean(values * values, axis=-1, keepdims=True) + epsilon) * gains


def rope(values, cosine, sine):
    return values * cosine + pltpu.roll(values, 64, 1) * sine


def push(src, dst, ssem, rsem, device):
    pltpu.make_async_remote_copy(
        src_ref=src, dst_ref=dst, send_sem=ssem, recv_sem=rsem,
        device_id=device, device_id_type=MESH,
    ).start()


def wait_for(ref, sem):
    pltpu.make_async_copy(ref, ref, sem).wait()


class Ring:
    def __init__(self, blocks, halves, plus, minus, ssem, rsem, source=None):
        self.own, self.left, self.right = blocks
        self.left_half, self.right_half, self.far_first, self.far_second = halves
        self.plus, self.minus, self.ssem, self.rsem = plus, minus, ssem, rsem
        self.source = self.own if source is None else source

    def start(self):
        push(self.source, self.own, self.ssem.at[0], self.rsem.at[0], self.plus)
        push(self.source, self.own, self.ssem.at[1], self.rsem.at[1], self.minus)

    def forward_left(self):
        wait_for(self.left, self.rsem.at[0])
        push(self.left_half, self.left_half, self.ssem.at[2], self.rsem.at[2], self.plus)

    def forward_right(self):
        wait_for(self.right, self.rsem.at[1])
        push(self.right_half, self.right_half, self.ssem.at[3], self.rsem.at[3], self.minus)

    def finish(self):
        wait_for(self.far_first, self.rsem.at[2])
        wait_for(self.far_second, self.rsem.at[3])

    def drain(self):
        wait_for(self.source, self.ssem.at[0])
        wait_for(self.source, self.ssem.at[1])
        wait_for(self.left_half, self.ssem.at[2])
        wait_for(self.right_half, self.ssem.at[3])


def assign_slots(expert_ids, slot_tok, slot_at):
    sub = lax.broadcasted_iota(jnp.int32, (128, 128), 0)
    lane = lax.broadcasted_iota(jnp.int32, (128, 128), 1)
    before = (sub < lane).astype(jnp.bfloat16)
    ones = jnp.ones((128, 128), jnp.bfloat16)
    offsets = offset_of_expert(expert_ids[...])
    base = jnp.zeros((128, 128), jnp.float32)
    named, ranks = [], []
    for k in range(TOPK):
        match = (sub == offsets[k : k + 1, :]).astype(jnp.float32)
        match_low = match.astype(jnp.bfloat16)
        place = base + jnp.dot(match_low, before, preferred_element_type=jnp.float32)
        rank = jnp.sum(match * place, axis=0, keepdims=True)
        base = base + jnp.dot(match_low, ones, preferred_element_type=jnp.float32)
        named.append(match)
        ranks.append(rank)
    slots = offsets * CAP + jnp.concatenate(ranks, axis=0).astype(jnp.int32)
    slot_at[...] = slots.T
    token = (128 - lane[:8]).astype(jnp.float32).astype(jnp.bfloat16)
    slot_tok[...] = jnp.full(slot_tok.shape, 128, jnp.int32)
    for r in range(CAP):
        chosen = jnp.zeros((128, 128), jnp.float32)
        for k in range(TOPK):
            chosen = chosen + jnp.where(ranks[k] == r, named[k], 0.0)
        found = lax.dot_general(
            token, chosen.astype(jnp.bfloat16), (((1,), (1,)), ((), ())), preferred_element_type=jnp.float32
        )
        slot_tok[r : r + 1, :] = 128 - found[0:1].astype(jnp.int32)


QB = 128
DB = 256
TK = 1024


def attend_kernel(
    hidden_in, attn_gain_in, wq, wk_in, wv_in, q_gain_in, k_gain_in, cosine_in, sine_in, ids_in, w_out,
    heads, w_all, slot_tok, slot_at,
    hidden, attn_gain, wk, wv, q_gain, k_gain, cosine, sine, expert_ids,
    kv, wq_all, normed, kv_stage, q_stage, q_ref, o_ref, m_scr, acc_scr,
    in_sem, own_sem, wq_s, wq_r, n_s, n_r, z_s, z_r, short_s, short_r, long_s, long_r, d_s, d_r, q_s, q_r,
    w_own, a_s, a_r, b_s, b_r, x_s, x_r, w_s, w_r, h_s, h_r,
):
    x, y, z, core = my_coords()
    ctx, exp = lax.axis_index("ctx"), lax.axis_index("exp")
    x_lo = x % 2
    sibling = device_at(x, y, z, 1 - core)
    x_other = (x // 2) * 2 + 1 - x_lo
    x_near = device_at(x_other, y, z, core)
    far_ctx = jnp.where(z < 2, ctx, 7 - ctx)

    loads = [
        pltpu.make_async_copy(src, dst, in_sem.at[i])
        for i, (src, dst) in enumerate(
            [
                (hidden_in, hidden), (attn_gain_in, attn_gain), (wk_in, wk), (wv_in, wv),
                (q_gain_in, q_gain), (k_gain_in, k_gain), (cosine_in, cosine), (sine_in, sine),
                (ids_in, expert_ids),
            ]
        )
    ]
    for load in loads:
        load.start()
    own_wq = pltpu.make_async_copy(wq, wq_all.at[z], own_sem)
    own_wq.start()
    barrier = pltpu.get_barrier_semaphore()

    def greet(device):
        pl.semaphore_signal(barrier, inc=1, device_id=device, device_id_type=MESH)

    def greet_block(e, carry):
        greet((7 - ctx, e))
        pl.when(e != exp)(lambda: greet((ctx, e)))
        return carry

    lax.fori_loop(0, 16, greet_block, 0)
    for d in (1, 3):
        greet(device_at((x + d) % 4, y, z, core))
        greet(device_at(x, (y + d) % 4, z, core))
    mine = x_lo * 2 + core
    loads[0].wait()
    loads[1].wait()
    normed[mine] = rms_scale(hidden[...].astype(jnp.float32), attn_gain[...]).astype(jnp.bfloat16)
    pl.semaphore_wait(barrier, 35)

    def wq_half(zz, half):
        return wq_all.at[zz, pl.ds(half * 1024, 1024)]

    z_left, z_right, z_far = (z + 3) % 4, (z + 1) % 4, (z + 2) % 4
    z_plus, z_minus = device_at(x, y, z_right, core), device_at(x, y, z_left, core)
    wq_ring = Ring(
        (wq_all.at[z], wq_all.at[z_left], wq_all.at[z_right]),
        (wq_half(z_left, 0), wq_half(z_right, 1), wq_half(z_far, 0), wq_half(z_far, 1)),
        z_plus, z_minus, wq_s, wq_r, wq,
    )
    other = (1 - x_lo) * 2 + core
    push(normed.at[mine], normed.at[mine], n_s.at[1], n_r.at[1], x_near)
    push(normed.at[mine], normed.at[mine], n_s.at[0], n_r.at[0], sibling)
    wq_ring.start()

    for load in loads[2:]:
        load.wait()
    here = pl.ds(pl.multiple_of(mine * 128, 128), 128)
    own_normed = normed[mine]
    key_raw = jnp.dot(own_normed, wk[...], preferred_element_type=jnp.float32)
    value_raw = jnp.dot(own_normed, wv[...], preferred_element_type=jnp.float32)
    for g in range(2):
        cols = slice(g * 128, (g + 1) * 128)
        key = rope(rms_scale(key_raw[:, cols], k_gain[...]), cosine[here, :], sine[here, :])
        kv_stage[0, g] = key.astype(jnp.bfloat16)
        kv_stage[1, g] = value_raw[:, cols].astype(jnp.bfloat16)

    def piece(which, zz, cc):
        return kv.at[which, x // 2, y, zz, x_lo, pl.ds(cc * 128, 128)]

    for which in range(2):
        for zz in range(4):
            is_self = (zz == z) & (which == core)
            src = kv_stage.at[which, zz // 2]
            dst = piece(which, z, core)

            @pl.when(is_self)
            def _(src=src, dst=dst):
                pltpu.make_async_copy(src, dst, z_r.at[z * 2 + core]).start()

            @pl.when(jnp.logical_not(is_self))
            def _(src=src, dst=dst, which=which, zz=zz):
                push(src, dst, z_s.at[which * 4 + zz], z_r.at[z * 2 + core], device_at(x, y, zz, which))

    for zz in range(4):
        for cc in range(2):
            wait_for(piece(core, zz, cc), z_r.at[zz * 2 + cc])

    def column(n, zs=None):
        xx = (x + n) % 4
        if zs is None:
            return kv.at[core, xx // 2, y, :, xx % 2]
        return kv.at[core, xx // 2, y, pl.ds(zs * 2, 2), xx % 2]

    short = Ring(
        (column(0), column(3), column(1)),
        (column(3, 0), column(1, 1), column(2, 0), column(2, 1)),
        device_at((x + 1) % 4, y, z, core), device_at((x + 3) % 4, y, z, core), short_s, short_r,
    )
    short.start()
    short.forward_left()
    short.forward_right()
    short.finish()

    def blocks_of(n, which, half=None):
        yy = (y + n) % 4
        return kv.at[which, :, yy] if half is None else kv.at[which, half, yy]

    def mine_of(n, half=None):
        return blocks_of(n, core, half)

    long = Ring(
        (mine_of(0), mine_of(3), mine_of(1)),
        (mine_of(3, 0), mine_of(1, 1), mine_of(2, 0), mine_of(2, 1)),
        device_at(x, (y + 1) % 4, z, core), device_at(x, (y + 3) % 4, z, core), long_s, long_r,
    )

    def share_kv(k, n):
        push(mine_of(n), mine_of(n), d_s.at[k], d_r.at[k], sibling)

    def theirs_kv(k, n):
        wait_for(blocks_of(n, 1 - core), d_r.at[k])

    long.start()
    share_kv(0, 0)
    wq_ring.forward_left()
    wq_ring.forward_right()
    wait_for(normed.at[other], n_r.at[1])
    push(normed.at[other], normed.at[other], n_s.at[2], n_r.at[2], sibling)
    assign_slots(expert_ids, slot_tok, slot_at)
    wait_for(normed.at[x_lo * 2 + 1 - core], n_r.at[0])
    own_wq.wait()
    wq_ring.finish()
    wait_for(normed.at[(1 - x_lo) * 2 + 1 - core], n_r.at[2])

    def q_rows(zz):
        return q_ref.at[zz // 2, pl.ds((zz % 2) * 512, 512)]

    tokens = normed[...].reshape(512, 2048)
    for pair in range(2):
        weights = jnp.concatenate([wq_all[2 * pair], wq_all[2 * pair + 1]], axis=1)
        raw = jnp.dot(tokens, weights, preferred_element_type=jnp.float32)
        for k in range(2):
            zz = 2 * pair + k
            query = rope(rms_scale(raw[:, k * 128 : (k + 1) * 128], q_gain[...]), cosine[...], sine[...])
            q_stage[zz] = query.astype(jnp.bfloat16)
            is_self = (zz == z) & (z < 2)

            @pl.when(is_self)
            def _(zz=zz):
                pltpu.make_async_copy(q_stage.at[zz], q_rows(z), q_r.at[z]).start()

            @pl.when(jnp.logical_not(is_self))
            def _(zz=zz):
                push(q_stage.at[zz], q_rows(z), q_s.at[zz], q_r.at[z], (far_ctx, zz * 4 + x_lo * 2 + core))

    def shard(dz, xl, cc):
        return w_all.at[(z + dz) % 4, xl, cc]

    def part(dz, xl, half):
        return w_all.at[(z + dz) % 4, xl, core, pl.ds(half * 64, 64)]

    ring = Ring(
        (shard(0, x_lo, core), shard(3, x_lo, core), shard(1, x_lo, core)),
        (part(3, x_lo, 0), part(1, x_lo, 1), part(2, x_lo, 0), part(2, x_lo, 1)),
        z_plus, z_minus, a_s, a_r, w_out,
    )
    order = [(0, 0), (3, 0), (1, 0), (2, 0), (0, 1), (3, 1), (1, 1), (2, 1)]

    def share(n, src=None):
        dz, flip = order[n]
        xl = 1 - x_lo if flip else x_lo
        push(shard(dz, xl, core) if src is None else src, shard(dz, xl, core), w_s.at[n], w_r.at[n], sibling)

    own = pltpu.make_async_copy(w_out, shard(0, x_lo, core), w_own)
    own.start()
    ring.start()
    push(w_out, shard(0, x_lo, core), x_s.at[0], x_r.at[0], x_near)
    share(0, w_out)

    def stage_1():
        long.forward_left()
        long.forward_right()
        share_kv(1, 3)
        share_kv(2, 1)
        ring.forward_left()
        ring.forward_right()
        share(1)
        share(2)
        theirs = shard(0, 1 - x_lo, core)
        wait_for(theirs, x_r.at[0])
        push(theirs, theirs, b_s.at[0], b_r.at[0], z_plus)
        push(theirs, theirs, b_s.at[1], b_r.at[1], z_minus)
        share(4)
        theirs_kv(1, 3)

    def stage_2():
        ring.finish()
        push(shard(2, x_lo, core), shard(2, x_lo, core), x_s.at[1], x_r.at[1], x_near)
        share(3)
        theirs_kv(2, 1)

    def stage_3():
        long.finish()
        share_kv(3, 2)
        theirs_kv(3, 2)

    def stage_4():
        wait_for(shard(3, 1 - x_lo, core), b_r.at[0])
        share(5)
        wait_for(shard(1, 1 - x_lo, core), b_r.at[1])
        share(6)
        wait_for(shard(2, 1 - x_lo, core), x_r.at[1])
        share(7)

    scale = math.log2(math.e) / math.sqrt(128)

    def step(q, k, v, m_prev, acc, first_row):
        s = lax.dot_general(q, k, (((1,), (1,)), ((), ())), preferred_element_type=jnp.float32)
        if first_row is not None:
            row = lax.broadcasted_iota(jnp.int32, s.shape, 0) + first_row
            col = lax.broadcasted_iota(jnp.int32, s.shape, 1)
            s = jnp.where(col <= row, s, -1e30)
        m_new = jnp.maximum(m_prev, jnp.max(s, axis=1, keepdims=True))
        alpha = jnp.exp2((m_prev - m_new) * scale)
        shift = (m_new * scale)[:, :1]
        p = jnp.exp2(s * scale - shift).astype(jnp.bfloat16)
        joined = jnp.concatenate([v, jnp.ones_like(v)], axis=1)
        pv = jnp.dot(p, joined, preferred_element_type=jnp.float32)
        return m_new, acc * jnp.concatenate([alpha, alpha], axis=1) + pv

    m_scr[...] = jnp.full_like(m_scr, -1e30)
    acc_scr[...] = jnp.zeros_like(acc_scr)
    last = (2 * ctx, 15 - 2 * ctx)

    def tile_of(t):
        at = (t // 8, (t // 2) % 4, pl.ds((t % 2) * 2, 2))
        return kv[(0, *at)].reshape(TK, 128), kv[(1, *at)].reshape(TK, 128)

    def full(half, t):
        k, v = tile_of(t)
        for b in range(1024 // QB):
            rows = pl.ds(b * QB, QB)
            m, a = step(q_ref[half, rows, :], k, v, m_scr[half, rows, :], acc_scr[half, rows, :], None)
            m_scr[half, rows, :] = m
            acc_scr[half, rows, :] = a

    for zz in range(4):
        wait_for(q_rows(zz), q_r.at[zz])
    theirs_kv(0, 0)

    def visit(s, carry):
        pl.when(s == 1)(stage_1)
        pl.when(s == 2)(stage_2)
        pl.when(s == 3)(stage_3)
        n = jnp.where(s == 1, 3, jnp.where(s == 2, 1, jnp.where(s == 3, 2, 0)))
        yy = (y + n) % 4

        def one(u, carry):
            t = ((u // 4) * 4 + yy) * 2 + (u // 2) % 2
            half = u % 2
            pl.when(t < jnp.where(half == 0, last[0], last[1]))(functools.partial(full, half, t))
            return carry

        return lax.fori_loop(0, 8, one, carry)

    lax.fori_loop(0, 4, visit, 0)
    stage_4()
    my_columns = pl.ds(pl.multiple_of(exp * 128, 128), 128)
    for half in range(2):
        k, v = tile_of(last[half])
        for b in range(1024 // DB):
            rows = pl.ds(b * DB, DB)
            seen = (b + 1) * DB
            m, a = step(
                q_ref[half, rows, :], k[:seen], v[:seen], m_scr[half, rows, :], acc_scr[half, rows, :], b * DB
            )
            o_ref[half, rows, :] = (a[:, :128] / a[:, 128:]).astype(jnp.bfloat16)
            for i in range(2):
                e = half * 8 + b * 2 + i
                src = o_ref.at[half, pl.ds(b * DB + i * 128, 128)]
                dst = heads.at[:, my_columns]
                if half:
                    push(src, dst, h_s, h_r, (7 - ctx, e))
                else:
                    pl.when(e == exp)(lambda src=src: pltpu.make_async_copy(src, dst, h_r).start())
                    pl.when(e != exp)(lambda src=src, e=e: push(src, dst, h_s, h_r, (ctx, e)))

    for n, (dz, flip) in enumerate(order):
        wait_for(shard(dz, 1 - x_lo if flip else x_lo, 1 - core), w_r.at[n])
        wait_for(shard(dz, 1 - x_lo if flip else x_lo, core), w_s.at[n])
    own.wait()
    ring.drain()
    for sem in (x_s.at[0], x_s.at[1], b_s.at[0], b_s.at[1]):
        wait_for(w_out, sem)
    long.drain()
    for k, n in enumerate((0, 3, 1, 2)):
        wait_for(mine_of(n), d_s.at[k])
    wq_ring.drain()
    short.drain()
    wait_for(normed.at[mine], n_s.at[0])
    wait_for(normed.at[mine], n_s.at[1])
    wait_for(normed.at[other], n_s.at[2])
    for zz in range(4):

        @pl.when(jnp.logical_not((zz == z) & (z < 2)))
        def _(zz=zz):
            wait_for(q_stage.at[zz], q_s.at[zz])

        for which in range(2):

            @pl.when(jnp.logical_not((zz == z) & (which == core)))
            def _(zz=zz, which=which):
                wait_for(kv_stage.at[which, zz // 2], z_s.at[which * 4 + zz])

    wait_for(heads, h_r)

    @pl.when(exp < 8)
    def _():
        wait_for(heads.at[:, pl.ds(0, 15 * 128)], h_s)

    @pl.when(exp >= 8)
    def _():
        wait_for(heads, h_s)


def attend(hidden, attn_gain, wq, wk, wv, q_gain, k_gain, cosine, sine, ids, w_out):
    vmem = pl.BlockSpec(memory_space=pltpu.VMEM)
    anywhere = pl.BlockSpec(memory_space=pl.ANY)
    dma = pltpu.SemaphoreType.DMA
    low, f32 = jnp.bfloat16, jnp.float32
    return pl.pallas_call(
        attend_kernel,
        out_shape=(
            jax.ShapeDtypeStruct((128, 2048), low),
            jax.ShapeDtypeStruct((4, 2, 2, 128, 2048), low),
            jax.ShapeDtypeStruct((16, 128), jnp.int32),
            jax.ShapeDtypeStruct((128, TOPK), jnp.int32),
        ),
        in_specs=[anywhere] * 11,
        out_specs=(anywhere, anywhere, vmem, vmem),
        scratch_shapes=[
            pltpu.VMEM((128, 2048), low),
            pltpu.VMEM((1, 2048), f32),
            pltpu.VMEM((2048, 256), low),
            pltpu.VMEM((2048, 256), low),
            pltpu.VMEM((1, 128), f32),
            pltpu.VMEM((1, 128), f32),
            pltpu.VMEM((512, 128), f32),
            pltpu.VMEM((512, 128), f32),
            pltpu.VMEM((TOPK, 128), jnp.int32),
            pltpu.VMEM((2, 2, 4, 4, 2, 256, 128), low),
            pltpu.VMEM((4, 2048, 128), low),
            pltpu.VMEM((4, 128, 2048), low),
            pltpu.VMEM((2, 2, 128, 128), low),
            pltpu.VMEM((4, 512, 128), low),
            pltpu.VMEM((2, 1024, 128), low),
            pltpu.VMEM((2, 1024, 128), low),
            pltpu.VMEM((2, 1024, 128), f32),
            pltpu.VMEM((2, 1024, 256), f32),
            dma((9,)), dma, dma((4,)), dma((4,)), dma((3,)), dma((3,)), dma((8,)), dma((8,)),
            dma((4,)), dma((4,)), dma((4,)), dma((4,)), dma((4,)), dma((4,)), dma((4,)), dma((4,)),
            dma, dma((4,)), dma((4,)), dma((2,)), dma((2,)), dma((2,)), dma((2,)), dma((8,)), dma((8,)), dma, dma,
        ],
        compiler_params=pltpu.CompilerParams(
            collective_id=1, has_side_effects=True, vmem_limit_bytes=60 * 1024 * 1024
        ),
        name="attend",
    )(
        hidden, attn_gain.reshape(1, -1), wq, wk, wv, q_gain.reshape(1, -1), k_gain.reshape(1, -1),
        cosine, sine, ids, w_out,
    )


def moe_kernel(
    cap,
    slot_tok,
    heads_in, hidden_in, ffn_gain_in, slot_in, gates_in, w_out, w_gate, w_up, w_down,
    out_ref,
    send_buf, in_buf, ans_buf, ret_buf, vo, vg, vu, vd, stage, xrows, x_tiles, resid, acc,
    heads, hidden, ffn_gain, slot_at, gates,
    wsem, insem, dsend, drecv, asend, arecv,
):
    tok = hidden.shape[0]
    loads = [
        pltpu.make_async_copy(src, dst, insem.at[i])
        for i, (src, dst) in enumerate(
            [(heads_in, heads), (w_out, vo), (hidden_in, hidden), (ffn_gain_in, ffn_gain),
             (slot_in, slot_at), (gates_in, gates)]
        )
    ]
    for load in loads:
        load.start()
    copies = [
        pltpu.make_async_copy(w_gate, vg, wsem.at[0]),
        pltpu.make_async_copy(w_up, vu, wsem.at[1]),
        pltpu.make_async_copy(w_down, vd, wsem.at[2]),
    ]
    for copy in copies:
        copy.start()
    barrier = pltpu.get_barrier_semaphore()

    def greet(o, carry):
        pl.semaphore_signal(barrier, inc=1, device_id=peer_to(o), device_id_type=MESH)
        return carry

    lax.fori_loop(1, GROUPS * PEERS, greet, 0)
    x_tiles[tok:] = jnp.zeros((8, 16, 128), jnp.bfloat16)
    for load in loads:
        load.wait()
    projected = jnp.dot(heads[...], vo[...], preferred_element_type=jnp.float32)
    summed = (hidden[...].astype(jnp.float32) + projected).astype(jnp.bfloat16)
    resid[...] = summed
    normed = rms_scale(summed.astype(jnp.float32), ffn_gain[...])
    for s in range(16):
        stage[pl.ds(s, tok, stride=16), :] = normed[:, s * 128 : (s + 1) * 128]
    x_tiles[:tok] = stage[: tok * 16].astype(jnp.bfloat16).reshape(tok, 16, 128)

    for r in range(cap):
        in_buf[0, r] = x_tiles[slot_tok[r, 0]]
    pl.semaphore_wait(barrier, GROUPS * PEERS - 1)

    def fill(o, carry):
        for r in range(cap):
            send_buf[o, r] = x_tiles[slot_tok[r, o]]
        return carry


    def dispatch(o, sem):
        return pltpu.make_async_remote_copy(
            src_ref=send_buf.at[o], dst_ref=in_buf.at[o],
            send_sem=dsend.at[sem], recv_sem=drecv.at[sem],
            device_id=peer_to(o), device_id_type=MESH,
        )

    def give_back(o, sem):
        return pltpu.make_async_remote_copy(
            src_ref=ans_buf.at[o], dst_ref=ret_buf.at[o],
            send_sem=asend.at[sem], recv_sem=arecv.at[sem],
            device_id=peer_from(o), device_id_type=MESH,
        )

    def send(o, carry):
        fill(o, 0)
        dispatch(o, o // PEERS).start()
        return carry

    lax.fori_loop(1, GROUPS * PEERS, send, 0)
    for copy in copies[:3]:
        copy.wait()
    rows = PEERS * cap

    def rows_of(buf, g):
        block = buf[pl.ds(g * PEERS, PEERS)]
        stage[...] = block.astype(jnp.float32).reshape(rows * 16, 128)
        for s in range(16):
            xrows[:, s * 128 : (s + 1) * 128] = stage[pl.ds(s, rows, stride=16), :].astype(jnp.bfloat16)
        return xrows[...]

    def compute(g):
        rows_in = rows_of(in_buf, g)
        gate = jnp.dot(rows_in, vg[...], preferred_element_type=jnp.float32)
        up = jnp.dot(rows_in, vu[...], preferred_element_type=jnp.float32)
        inner = (gate / (1.0 + jnp.exp(-gate)) * up).astype(jnp.bfloat16)
        for q in range(4):
            part = jnp.dot(inner, vd[:, q * 512 : (q + 1) * 512], preferred_element_type=jnp.float32)
            for s in range(4):
                stage[pl.ds(q * 4 + s, rows, stride=16), :] = part[:, s * 128 : (s + 1) * 128]
        return stage[...].astype(jnp.bfloat16).reshape(PEERS, cap, 16, 128)

    def wait_bytes(buf, start, count, sem):
        pltpu.make_async_copy(buf.at[pl.ds(start, count)], buf.at[pl.ds(start, count)], sem).wait()

    def start_back(o, sem):
        give_back(o, sem).start()
        return sem

    for g in range(GROUPS):
        first = 1 if g == 0 else 0
        wait_bytes(in_buf, g * PEERS + first, PEERS - first, drecv.at[g])
        answers = compute(g)
        if g == 0:
            ret_buf[0] = answers[0]
        ans_buf[pl.ds(g * PEERS, PEERS)] = answers
        lax.fori_loop(g * PEERS + first, (g + 1) * PEERS, lambda o, c, g=g: start_back(o, g), g)
    acc[...] = resid[...].astype(jnp.float32)
    weights = gates[...].T
    shares = weights / jnp.sum(weights, axis=1, keepdims=True)
    at = slot_at[...]
    for g in range(GROUPS):
        slot = lax.broadcasted_iota(jnp.int32, (tok, rows), 1) + g * rows
        mix = jnp.zeros((tok, rows), jnp.float32)
        for k in range(TOPK):
            mix = mix + jnp.where(at[:, k : k + 1] == slot, shares[:, k : k + 1], 0.0)
        high = mix.astype(jnp.bfloat16)
        low = (mix - high.astype(jnp.float32)).astype(jnp.bfloat16)
        first = 1 if g == 0 else 0
        wait_bytes(ret_buf, g * PEERS + first, PEERS - first, arecv.at[g])
        back = rows_of(ret_buf, g)
        acc[...] += jnp.dot(high, back, preferred_element_type=jnp.float32) + jnp.dot(
            low, back, preferred_element_type=jnp.float32
        )
    out_ref[...] = acc[...].astype(jnp.bfloat16)
    for g in range(GROUPS):
        first = 1 if g == 0 else 0
        wait_bytes(send_buf, g * PEERS + first, PEERS - first, dsend.at[g])
        wait_bytes(ans_buf, g * PEERS + first, PEERS - first, asend.at[g])


def tail(heads, hidden, ffn_gain, w_out, slot_tok, slot_at, gates, w_gate, w_up, w_down):
    tok, width = hidden.shape
    ff = w_gate.shape[1]
    n = GROUPS * PEERS
    anywhere = pl.BlockSpec(memory_space=pl.ANY)
    dma = pltpu.SemaphoreType.DMA
    low, f32 = jnp.bfloat16, jnp.float32
    return pl.pallas_call(
        functools.partial(moe_kernel, CAP),
        out_shape=jax.ShapeDtypeStruct((tok, width), low),
        in_specs=[pl.BlockSpec(memory_space=pltpu.SMEM)] + [anywhere] * 9,
        out_specs=pl.BlockSpec(memory_space=pltpu.VMEM),
        scratch_shapes=[pltpu.VMEM((n, CAP, 16, 128), low)] * 4
        + [
            pltpu.VMEM((width, width), low),
            pltpu.VMEM((width, ff), low),
            pltpu.VMEM((width, ff), low),
            pltpu.VMEM((ff, width), low),
            pltpu.VMEM((PEERS * CAP * 16, 128), f32),
            pltpu.VMEM((PEERS * CAP, width), low),
            pltpu.VMEM((tok + 8, 16, 128), low),
            pltpu.VMEM((tok, width), low),
            pltpu.VMEM((tok, width), f32),
            pltpu.VMEM((tok, width), low),
            pltpu.VMEM((tok, width), low),
            pltpu.VMEM((1, width), f32),
            pltpu.VMEM((tok, TOPK), jnp.int32),
            pltpu.VMEM((TOPK, tok), f32),
            dma((3,)), dma((6,)), dma((GROUPS,)), dma((GROUPS,)), dma((GROUPS,)), dma((GROUPS,)),
        ],
        compiler_params=pltpu.CompilerParams(
            collective_id=3, has_side_effects=True, vmem_limit_bytes=62 * 1024 * 1024
        ),
        name="tail",
    )(slot_tok, heads, hidden, ffn_gain.reshape(1, -1), slot_at, gates, w_out, w_gate, w_up, w_down)


def on_device(
    hidden_in, attn_gain, w_query, w_key, w_value, q_gain, k_gain, w_out, ffn_gain,
    w_gate, w_up, w_down, expert_ids, gate_weights,
):
    ctx, exp = lax.axis_index("ctx"), lax.axis_index("exp")
    places = ctx * 2048 + (exp // 4) * 512 + jnp.arange(512, dtype=jnp.int32)
    frequency = jnp.exp(jnp.arange(64, dtype=jnp.float32) * (-2.0 * math.log(rope_base) / 128))
    angles = places.astype(jnp.float32)[:, None] * frequency[None, :]
    cosine, sine = jnp.cos(angles), jnp.sin(angles)
    heads, w_out_all, slot_tok, slot_at = attend(
        hidden_in, attn_gain, w_query, w_key, w_value, q_gain, k_gain,
        jnp.concatenate([cosine, cosine], axis=1), jnp.concatenate([-sine, sine], axis=1), expert_ids.T, w_out,
    )
    return tail(
        heads, hidden_in, ffn_gain, w_out_all.reshape(2048, 2048), slot_tok, slot_at, gate_weights.T,
        w_gate[0], w_up[0], w_down[0],
    )


def solution(mesh):
    placed = (
        P(("ctx", "exp"), None),
        P(),
        P(None, "exp"),
        P(),
        P(),
        P(),
        P(),
        P("exp", None),
        P(),
        P(("ctx", "exp"), None, None),
        P(("ctx", "exp"), None, None),
        P(("ctx", "exp"), None, None),
        P(("ctx", "exp"), None),
        P(("ctx", "exp"), None),
    )
    return jax.shard_map(
        on_device, mesh=mesh, in_specs=placed, out_specs=P(("ctx", "exp"), None), check_vma=False
    )
```
